256 devices in a mesh: outer: 16 (over y_lo, x, core), inner: 16 (over z, y_hi).
Axes of the slice: x: 4, y: 4 (y_hi: 2, y_lo: 2; y = y_hi * 2 + y_lo), z: 8, core: 2. Of those that a mesh axis runs over, the one named last changes fastest.
Arguments:
- queries: bfloat16 [65536, 1536], P(('outer', 'inner')), may hold values from -6 to 6
- key_rows: bfloat16 [65536, 1536], P(('outer', 'inner')), may hold values from -6 to 6
- values: bfloat16 [65536, 1536], P(('outer', 'inner')), may hold values from -6 to 6
- out_grads: bfloat16 [65536, 1536], P(('outer', 'inner')), may hold values from -96 to 96
- offsets: int32 [8], replicated, may hold values from 0 to 127, as said below
Outputs:
- grad_queries: bfloat16 [65536, 1536], P(('outer', 'inner'))
- grad_keys: bfloat16 [65536, 1536], P(('outer', 'inner'))
- grad_values: bfloat16 [65536, 1536], P(('outer', 'inner'))
The draws below stay inside these ranges and needn't reach their ends.
Inputs may be any that keep to these rules, and one draw needn't show every extreme that they name: offsets[j] is below 4 for j < 5 and below 128 for the others.
All inputs are finite; a program needn't handle non-finite values.
Results may differ from the reference program's by a relative error of at most 0.0057.
The reference program's roundings to bfloat16 on the way count: a program that leaves them out, or rounds other values in their place, can miss the bound.
Values may be sent and summed in bfloat16 or wider, within the bound.
No kernel may reach another device: no remote copies, remote signals or barrier semaphores. Data moves between devices by JAX's collectives and lax.ppermute only.
A program may use at most 64 MiB of HBM per device.

```python
import math
import jax
import jax.numpy as jnp
from jax import lax

HEAD_DIM = 128
H_NEAR = 4
H_MID = 5
H_WIDE = 3
HEADS = 12
R_MID = 4
R_WIDE = 128
TOK_DEV = 256
SEG_MID = 4096
TOKENS = 65536


def draw_queries(key, part):
    key = jax.random.fold_in(key, 7)
    drawn = jnp.clip(jax.random.normal(key, (TOKENS, HEADS * HEAD_DIM)), -6.0, 6.0)
    return drawn.astype(jnp.bfloat16)


def draw_key_rows(key, part):
    key = jax.random.fold_in(key, 8)
    drawn = jnp.clip(jax.random.normal(key, (TOKENS, HEADS * HEAD_DIM)), -6.0, 6.0)
    return drawn.astype(jnp.bfloat16)


def draw_offsets(key, part):
    key = jax.random.fold_in(key, 9)
    heads_all = H_MID + H_WIDE
    limits = jnp.where(jnp.arange(heads_all) < H_MID, R_MID, R_WIDE).astype(jnp.int32)
    drawn = jax.random.randint(key, (heads_all,), 0, limits).astype(jnp.int32)
    low_head = jax.random.randint(jax.random.fold_in(key, 11), (), 0, H_MID).astype(jnp.int32)
    high_head = jax.random.randint(jax.random.fold_in(key, 12), (), H_MID, heads_all).astype(jnp.int32)
    position = jnp.arange(heads_all, dtype=jnp.int32)
    drawn = jnp.where(position == low_head, jnp.zeros((), jnp.int32), drawn)
    drawn = jnp.where(position == high_head, jnp.full((), R_WIDE - 1, jnp.int32), drawn)
    return drawn.astype(jnp.int32)


def block_levels(rng, dims, pieces, low, top_value):
    loudness = 1.0
    for axis_at, shards_of in pieces:
        heights = jax.random.uniform(jax.random.fold_in(jax.random.fold_in(rng, 6), axis_at), (shards_of,), jnp.float32, low / len(pieces), top_value / len(pieces))
        loudness = loudness * jnp.repeat(jnp.exp(heights), dims[axis_at] // shards_of).reshape((-1,) + (1,) * (len(dims) - 1 - axis_at))
    return loudness


def gaussian(stream_key, shape, width, limit, pieces=(), kind=jnp.bfloat16):
    result = width * jax.random.normal(stream_key, shape, jnp.float32)
    if pieces:
        result = result * block_levels(stream_key, shape, pieces, -0.22, 0.18)
    return jnp.clip(result, -limit, limit).astype(kind)


def setup_inputs(seed: int = 0) -> dict:
    arg_keys = jax.random.split(jax.random.key(seed), 6)
    return {
        "queries": draw_queries(jax.random.fold_in(arg_keys[5], 71), 0),
        "key_rows": draw_key_rows(jax.random.fold_in(arg_keys[5], 71), 0),
        "values": gaussian(arg_keys[2], (TOKENS, HEADS * HEAD_DIM), 1.0, 6.0, ((0, 256),)),
        "out_grads": gaussian(arg_keys[3], (TOKENS, HEADS * HEAD_DIM), 16.0, 96.0, ((0, 256),)),
        "offsets": draw_offsets(jax.random.fold_in(arg_keys[5], 71), 0),
    }


def rounded(tensor):
    return lax.optimization_barrier(tensor.astype(jnp.bfloat16)).astype(jnp.float32)

def select_rows(block, head_offsets, stride):
    row_number, columns = block.shape
    head_count = head_offsets.shape[0]
    shaped = block.reshape(row_number // stride, stride, head_count, columns // head_count)
    chosen = jnp.arange(stride, dtype=jnp.int32)[:, None] == head_offsets[None, :].astype(jnp.int32)
    masked = jnp.where(chosen[None, :, :, None], shaped, jnp.zeros((), block.dtype))
    return lax.optimization_barrier(jnp.sum(masked, axis=1)).astype(block.dtype)

def spread_rows(picked, head_offsets, stride):
    picked_rows, head_count, head_depth = picked.shape
    chosen = jnp.arange(stride, dtype=jnp.int32)[:, None] == head_offsets[None, :].astype(jnp.int32)
    placed = jnp.where(chosen[None, :, :, None], picked[:, None], jnp.zeros((), picked.dtype))
    return placed.reshape(picked_rows * stride, head_count * head_depth)

def backward_full(blocks):
    query_row_block, key_tile_block, value_tile_block, gradient_rows = [part.astype(jnp.float32) for part in blocks]
    score_scale = 1.0 / math.sqrt(query_row_block.shape[-1])
    logit_scores = jnp.einsum('agk,igk->gai', query_row_block, key_tile_block) * score_scale
    row_max = lax.optimization_barrier(jnp.max(logit_scores, axis=2, keepdims=True))
    exponent = jnp.exp(logit_scores - row_max)
    weights = exponent / lax.optimization_barrier(jnp.sum(exponent, axis=2, keepdims=True))
    product_gradients = jnp.einsum('agk,igk->gai', gradient_rows, value_tile_block)
    row_dots = lax.optimization_barrier(jnp.sum(weights * product_gradients, axis=2, keepdims=True))
    weights_bfloat = rounded(weights)
    score_gradients = rounded(weights * (product_gradients - row_dots) * score_scale)
    query_gradient = jnp.einsum('ywr,ryu->wyu', score_gradients, key_tile_block)
    key_gradient = jnp.einsum('wfl,fwp->lwp', score_gradients, query_row_block)
    value_gradient = jnp.einsum('wfl,fwp->lwp', weights_bfloat, gradient_rows)
    return (query_gradient, key_gradient, value_gradient)

def reference(queries, key_rows, values, out_grads, offsets):
    near_end = H_NEAR * HEAD_DIM
    mid_end = near_end + H_MID * HEAD_DIM
    arrays = (queries, key_rows, values, out_grads)
    near_parts = tuple((block[:, :near_end].reshape(TOKENS // TOK_DEV, TOK_DEV, H_NEAR, HEAD_DIM) for block in arrays))
    near_result = lax.map(backward_full, near_parts)
    near_result = [part.reshape(TOKENS, near_end) for part in near_result]
    mid_offsets = offsets[:H_MID]
    wide_offsets = offsets[H_MID:]
    segments = TOKENS // SEG_MID
    mid_parts = tuple((select_rows(block[:, near_end:mid_end], mid_offsets, R_MID).reshape(segments, SEG_MID // R_MID, H_MID, HEAD_DIM) for block in arrays))
    mid_result = lax.map(backward_full, mid_parts)
    mid_result = [spread_rows(part.reshape(TOKENS // R_MID, H_MID, HEAD_DIM), mid_offsets, R_MID) for part in mid_result]
    wide_parts = tuple((select_rows(block[:, mid_end:], wide_offsets, R_WIDE) for block in arrays))
    wide_result = backward_full(wide_parts)
    wide_result = [spread_rows(part, wide_offsets, R_WIDE) for part in wide_result]
    joined = [jnp.concatenate([near_result[index], mid_result[index], wide_result[index]], axis=1).astype(jnp.bfloat16) for index in range(3)]
    return (joined[0], joined[1], joined[2])
```

```python
import math

import jax
import jax.numpy as jnp
from jax import lax
from jax.experimental import pallas as pl
from jax.experimental.pallas import tpu as pltpu
from jax.sharding import PartitionSpec as P

HEAD_DIM = 128
H_NEAR = 4
H_MID = 5
H_WIDE = 3
R_MID = 4
R_WIDE = 128
TOK = 256
NEAR_END = H_NEAR * HEAD_DIM
MID_END = NEAR_END + H_MID * HEAD_DIM
HIDDEN = MID_END + H_WIDE * HEAD_DIM
MEMBERS = 16
OUTERS = 16
MID_ROWS = TOK // R_MID
SPLIT = 3
PART = 24
WIDE_SPLIT = 4
SCALE = 1.0 / math.sqrt(HEAD_DIM)
BF16 = jnp.bfloat16
F32 = jnp.float32
VMEM_LIMIT = 48 * 1024 * 1024


def dot(a, b):
    return lax.dot_general(a, b, (((1,), (0,)), ((), ())), preferred_element_type=F32)


def dot_nt(a, b):
    return lax.dot_general(a, b, (((1,), (1,)), ((), ())), preferred_element_type=F32)


def dot_tn(a, b):
    return lax.dot_general(a, b, (((0,), (0,)), ((), ())), preferred_element_type=F32)


def iota2(rows, columns):
    shape = (rows, columns)
    return (
        lax.broadcasted_iota(jnp.int32, shape, 0),
        lax.broadcasted_iota(jnp.int32, shape, 1),
    )


def one_hot(condition):
    return jnp.where(condition, 1.0, 0.0).astype(BF16)


def pair(left_ref, right_ref, start):
    columns = slice(start, start + HEAD_DIM)
    return jnp.concatenate([left_ref[:, columns], right_ref[:, columns]], axis=1)


def attention_transposed(query, key, value, gradient):
    scores = dot_nt(key, query) * SCALE
    exponent = jnp.exp(scores - jnp.max(scores, axis=0, keepdims=True))
    weights = exponent * (1.0 / jnp.sum(exponent, axis=0, keepdims=True))
    products = dot_nt(value, gradient)
    row_dots = jnp.sum(weights * products, axis=0, keepdims=True)
    score_gradients = (weights * (products - row_dots) * SCALE).astype(BF16)
    return weights.astype(BF16), score_gradients


def pack_kernel(off_ref, q_ref, k_ref, v_ref, g_ref, out_ref):
    row8, column8 = iota2(8, TOK)
    wide_rows = []
    for head in range(H_WIDE):
        start = MID_END + head * HEAD_DIM
        offset = off_ref[H_MID + head]
        pick_kv = one_hot((row8 < 2) & (column8 == offset + R_WIDE * row8))
        pick_qg = one_hot((row8 >= 2) & (row8 < 4) & (column8 == offset + R_WIDE * (row8 - 2)))
        wide_rows.append(
            dot(pick_kv, pair(k_ref, v_ref, start)) + dot(pick_qg, pair(q_ref, g_ref, start))
        )
    row_kv, column_kv = iota2(MID_ROWS, TOK)
    row_qg, column_qg = iota2(SPLIT * PART, TOK)
    for head in range(H_MID):
        start = NEAR_END + head * HEAD_DIM
        offset = off_ref[head]
        pick_kv = one_hot(column_kv == offset + R_MID * row_kv)
        pick_qg = one_hot(column_qg == offset + R_MID * row_qg)
        kv = dot(pick_kv, pair(k_ref, v_ref, start)).astype(BF16)
        qg = dot(pick_qg, pair(q_ref, g_ref, start))
        for part in range(SPLIT):
            worker = head * SPLIT + part
            wide_head = min(worker // WIDE_SPLIT, H_WIDE - 1)
            tail = jnp.concatenate([qg[part * PART : (part + 1) * PART], wide_rows[wide_head]], axis=0)
            out_ref[worker, 0:64, :] = kv
            out_ref[worker, 64:96, :] = tail.astype(BF16)
    out_ref[MEMBERS - 1] = jnp.zeros((96, 2 * HEAD_DIM), BF16)


def near_kernel(q_ref, k_ref, v_ref, g_ref, dq_ref, dk_ref, dv_ref):
    for head in range(H_NEAR):
        columns = slice(head * HEAD_DIM, (head + 1) * HEAD_DIM)
        query, key, value, gradient = (
            q_ref[:, columns],
            k_ref[:, columns],
            v_ref[:, columns],
            g_ref[:, columns],
        )
        weights, score_gradients = attention_transposed(query, key, value, gradient)
        dq_ref[:, columns] = dot_tn(score_gradients, key).astype(BF16)
        dk_ref[:, columns] = dot(score_gradients, query).astype(BF16)
        dv_ref[:, columns] = dot(weights, gradient).astype(BF16)


def forward_kernel(got_ref, out_ref):
    fourth = lax.rem(lax.axis_index("inner"), WIDE_SPLIT)
    rows = got_ref[:, 80:96, :].reshape(MEMBERS * 16, 2 * HEAD_DIM)
    row, column = iota2(48, MEMBERS * 16)
    source_kv = 16 * (row // 2) + 8 + row % 2
    query_row = row - 32
    source_qg = 16 * (WIDE_SPLIT * fourth + query_row // 2) + 10 + row % 2
    source = jnp.where(row < 32, source_kv, source_qg)
    picked = dot(one_hot((column == source) & (row < 40)), rows).astype(BF16)
    for target in range(OUTERS):
        out_ref[target] = picked


def worker_kernel(mid_ref, wide_ref, out_ref, dk_ref, dv_ref, dq_ref):
    outer = lax.axis_index("outer")
    fourth = lax.rem(lax.axis_index("inner"), WIDE_SPLIT)
    kv = wide_ref[:, 0:32, :].reshape(OUTERS * 32, 2 * HEAD_DIM)
    qg = wide_ref[:, 32:48, :].astype(F32)[:, 0:8, :].reshape(OUTERS * 8, 2 * HEAD_DIM).astype(BF16)
    key, value = kv[:, :HEAD_DIM], kv[:, HEAD_DIM:]
    query, gradient = qg[:, :HEAD_DIM], qg[:, HEAD_DIM:]
    weights, score_gradients = attention_transposed(query, key, value, gradient)
    dk_ref[...] = dot(score_gradients, query)
    dv_ref[...] = dot(weights, gradient)
    dq_ref[...] = dot_tn(score_gradients, key)
    own_keys = pl.ds(pl.multiple_of(outer * 32, 32), 32)
    own_queries = pl.ds(pl.multiple_of(outer * 8, 8), 8)
    dk, dv = dk_ref[own_keys, :].astype(BF16), dv_ref[own_keys, :].astype(BF16)
    dq = dq_ref[own_queries, :].astype(BF16)
    row, column = iota2(MEMBERS * 8, 32)
    member, place = row // 8, row % 8
    wide_out = dot(one_hot((column == 2 * member + place - 2) & (place >= 2) & (place < 4)), dk)
    wide_out += dot(one_hot((column == 2 * member + place - 4) & (place >= 4) & (place < 6)), dv)
    row, column = iota2(MEMBERS * 8, 8)
    member, place = row // 8, row % 8
    wide_out += dot(
        one_hot((column == 2 * (member - WIDE_SPLIT * fourth) + place) & (place < 2)), dq
    )
    key = mid_ref[:, 0:64, :HEAD_DIM].reshape(MEMBERS * 64, HEAD_DIM)
    value = mid_ref[:, 0:64, HEAD_DIM:].reshape(MEMBERS * 64, HEAD_DIM)
    qg = mid_ref[:, 64:96, :].astype(F32)[:, 0:PART, :].reshape(MEMBERS * PART, 2 * HEAD_DIM)
    qg = qg.astype(BF16)
    query, gradient = qg[:, :HEAD_DIM], qg[:, HEAD_DIM:]
    weights, score_gradients = attention_transposed(query, key, value, gradient)
    out_ref[:, 0:64, :] = dot(score_gradients, query).astype(BF16).reshape(MEMBERS, 64, HEAD_DIM)
    out_ref[:, 64:128, :] = dot(weights, gradient).astype(BF16).reshape(MEMBERS, 64, HEAD_DIM)
    dq = dot_tn(key, score_gradients).T.reshape(MEMBERS, PART, HEAD_DIM)
    tail = jnp.concatenate([dq, wide_out.reshape(MEMBERS, 8, HEAD_DIM)], axis=1)
    out_ref[:, 128:160, :] = tail.astype(BF16)


def assemble_kernel(off_ref, got_ref, nq_ref, nk_ref, nv_ref, dq_ref, dk_ref, dv_ref):
    inner = lax.axis_index("inner")
    for near_ref, out_ref in ((nq_ref, dq_ref), (nk_ref, dk_ref), (nv_ref, dv_ref)):
        out_ref[:, :NEAR_END] = near_ref[...]
    row, column = iota2(TOK, SPLIT * PART)
    row64, column64 = iota2(TOK, MID_ROWS)
    for head in range(H_MID):
        columns = slice(NEAR_END + head * HEAD_DIM, NEAR_END + (head + 1) * HEAD_DIM)
        offset = off_ref[head]
        workers = range(head * SPLIT, (head + 1) * SPLIT)
        dq = jnp.concatenate(
            [got_ref[worker, 128:160, :].astype(F32)[0:PART] for worker in workers], axis=0
        ).astype(BF16)
        dk = sum(got_ref[worker, 0:64, :].astype(F32) for worker in workers).astype(BF16)
        dv = sum(got_ref[worker, 64:128, :].astype(F32) for worker in workers).astype(BF16)
        place = one_hot(row64 == offset + R_MID * column64)
        dq_ref[:, columns] = dot(one_hot(row == offset + R_MID * column), dq).astype(BF16)
        dk_ref[:, columns] = dot(place, dk).astype(BF16)
        dv_ref[:, columns] = dot(place, dv).astype(BF16)
    row, unused = iota2(TOK, HEAD_DIM)
    for head in range(H_WIDE):
        columns = slice(MID_END + head * HEAD_DIM, MID_END + (head + 1) * HEAD_DIM)
        offset = off_ref[H_MID + head]
        workers = range(head * WIDE_SPLIT, (head + 1) * WIDE_SPLIT)
        sums = sum(got_ref[worker, 144:160, :].astype(F32) for worker in workers)
        owner = head * WIDE_SPLIT + lax.div(inner, WIDE_SPLIT)
        queries = got_ref[owner, 144:160, :].astype(F32)
        first, second = row == offset, row == offset + R_WIDE
        for out_ref, rows, at in ((dq_ref, queries, 8), (dk_ref, sums, 10), (dv_ref, sums, 12)):
            spread = jnp.where(first, rows[at : at + 1], 0.0)
            spread = jnp.where(second, rows[at + 1 : at + 2], spread)
            out_ref[:, columns] = spread.astype(BF16)


def call(kernel, out_shapes, in_smem, scratch=()):
    spaces = {True: pltpu.SMEM, False: pltpu.VMEM}
    outs = [jax.ShapeDtypeStruct(shape, BF16) for shape in out_shapes]
    specs = [pl.BlockSpec(memory_space=pltpu.VMEM) for unused in outs]
    return pl.pallas_call(
        kernel,
        out_shape=outs if len(outs) > 1 else outs[0],
        in_specs=[pl.BlockSpec(memory_space=spaces[smem]) for smem in in_smem],
        out_specs=specs if len(outs) > 1 else specs[0],
        scratch_shapes=list(scratch),
        compiler_params=pltpu.CompilerParams(vmem_limit_bytes=VMEM_LIMIT),
    )


def body(queries, key_rows, values, out_grads, offsets):
    arrays = (queries, key_rows, values, out_grads)
    packed = call(pack_kernel, [(MEMBERS, 96, 256)], [True] + [False] * 4)(offsets, *arrays)
    near_block = pl.BlockSpec((TOK, NEAR_END), lambda step: (0, 0))
    near = pl.pallas_call(
        near_kernel,
        grid=(1,),
        out_shape=[jax.ShapeDtypeStruct((TOK, NEAR_END), BF16)] * 3,
        in_specs=[near_block] * 4,
        out_specs=[near_block] * 3,
        compiler_params=pltpu.CompilerParams(vmem_limit_bytes=VMEM_LIMIT),
    )(*arrays)
    mid_got = lax.all_to_all(packed, "inner", 0, 0)
    wide_send = call(forward_kernel, [(OUTERS, 48, 256)], [False])(mid_got)
    wide_got = lax.all_to_all(wide_send, "outer", 0, 0)
    results = call(
        worker_kernel,
        [(MEMBERS, 160, HEAD_DIM)],
        [False] * 2,
        [pltpu.VMEM((512, 128), F32), pltpu.VMEM((512, 128), F32), pltpu.VMEM((128, 128), F32)],
    )(mid_got, wide_got)
    returned = lax.all_to_all(results, "inner", 0, 0)
    return tuple(
        call(assemble_kernel, [(TOK, HIDDEN)] * 3, [True] + [False] * 4)(offsets, returned, *near)
    )


def solution(mesh):
    spec = P(("outer", "inner"), None)
    return jax.shard_map(
        body,
        mesh=mesh,
        in_specs=(spec, spec, spec, spec, P()),
        out_specs=(spec, spec, spec),
        check_vma=False,
    )
```

```python
import math

import jax
import jax.numpy as jnp
from jax import lax
from jax.experimental import pallas as pl
from jax.experimental.pallas import tpu as pltpu
from jax.sharding import PartitionSpec as P

HEAD_DIM = 128
H_NEAR = 4
H_MID = 5
H_WIDE = 3
R_MID = 4
R_WIDE = 128
TOK = 256
NEAR_END = H_NEAR * HEAD_DIM
MID_END = NEAR_END + H_MID * HEAD_DIM
HIDDEN = MID_END + H_WIDE * HEAD_DIM
MEMBERS = 16
OUTERS = 16
MID_ROWS = TOK // R_MID
SPLIT = 3
PART = 24
WIDE_SPLIT = 4
SCALE = 1.0 / math.sqrt(HEAD_DIM)
BF16 = jnp.bfloat16
F32 = jnp.float32


def dot(a, b):
    return lax.dot_general(a, b, (((1,), (0,)), ((), ())), preferred_element_type=F32)


def dot_nt(a, b):
    return lax.dot_general(a, b, (((1,), (1,)), ((), ())), preferred_element_type=F32)


def dot_tn(a, b):
    return lax.dot_general(a, b, (((0,), (0,)), ((), ())), preferred_element_type=F32)


def iota2(rows, columns):
    shape = (rows, columns)
    return (
        lax.broadcasted_iota(jnp.int32, shape, 0),
        lax.broadcasted_iota(jnp.int32, shape, 1),
    )


def one_hot(condition):
    return jnp.where(condition, 1.0, 0.0).astype(BF16)


def attention_transposed(query, key, value, gradient):
    scores = dot_nt(key, query) * SCALE
    exponent = jnp.exp(scores - jnp.max(scores, axis=0, keepdims=True))
    weights = exponent * (1.0 / jnp.sum(exponent, axis=0, keepdims=True))
    products = dot_nt(value, gradient)
    row_dots = jnp.sum(weights * products, axis=0, keepdims=True)
    score_gradients = (weights * (products - row_dots) * SCALE).astype(BF16)
    return weights.astype(BF16), score_gradients


def pack_kernel(off_hbm, q_hbm, k_hbm, v_hbm, g_hbm, out_ref, off_out, off_ref, held, off_sem, sems):
    off_copy = pltpu.make_async_copy(off_hbm, off_ref, off_sem)
    off_copy.start()
    order = list(range(H_MID, H_MID + H_WIDE)) + list(range(H_MID))
    copies = {}
    for head in order:
        for which, source in enumerate((q_hbm, k_hbm, v_hbm, g_hbm)):
            copies[head, which] = pltpu.make_async_copy(
                source.at[:, pl.ds(NEAR_END + head * HEAD_DIM, HEAD_DIM)],
                held.at[which, head],
                sems.at[which, head],
            )
            copies[head, which].start()
    off_copy.wait()
    for head in range(H_MID + H_WIDE):
        off_out[head : head + 1, :] = jnp.full((1, HEAD_DIM), off_ref[head], jnp.int32)
    row8, column8 = iota2(8, TOK)
    wide_rows = []
    for head in range(H_MID, H_MID + H_WIDE):
        offset = off_ref[head]
        pick_kv = one_hot((row8 < 2) & (column8 == offset + R_WIDE * row8))
        pick_qg = one_hot((row8 >= 2) & (row8 < 4) & (column8 == offset + R_WIDE * (row8 - 2)))
        for which in range(4):
            copies[head, which].wait()
        kv = jnp.concatenate([held[1, head], held[2, head]], axis=1)
        qg = jnp.concatenate([held[0, head], held[3, head]], axis=1)
        wide_rows.append(dot(pick_kv, kv) + dot(pick_qg, qg))
    row_kv, column_kv = iota2(MID_ROWS, TOK)
    row_qg, column_qg = iota2(SPLIT * PART, TOK)
    for head in range(H_MID):
        offset = off_ref[head]
        pick_kv = one_hot(column_kv == offset + R_MID * row_kv)
        pick_qg = one_hot(column_qg == offset + R_MID * row_qg)
        for which in range(4):
            copies[head, which].wait()
        kv = dot(pick_kv, jnp.concatenate([held[1, head], held[2, head]], axis=1)).astype(BF16)
        qg = dot(pick_qg, jnp.concatenate([held[0, head], held[3, head]], axis=1))
        for part in range(SPLIT):
            worker = head * SPLIT + part
            wide_head = min(worker // WIDE_SPLIT, H_WIDE - 1)
            tail = jnp.concatenate([qg[part * PART : (part + 1) * PART], wide_rows[wide_head]], axis=0)
            out_ref[worker, 0:64, :] = kv
            out_ref[worker, 64:96, :] = tail.astype(BF16)
    out_ref[MEMBERS - 1] = jnp.zeros((96, 2 * HEAD_DIM), BF16)


def near_kernel(q_ref, k_ref, v_ref, g_ref, dq_ref, dk_ref, dv_ref):
    query, key, value, gradient = q_ref[...], k_ref[...], v_ref[...], g_ref[...]
    weights, score_gradients = attention_transposed(query, key, value, gradient)
    dq_ref[...] = dot_tn(score_gradients, key).astype(BF16)
    dk_ref[...] = dot(score_gradients, query).astype(BF16)
    dv_ref[...] = dot(weights, gradient).astype(BF16)


def forward_kernel(got_ref, out_ref):
    fourth = lax.rem(lax.axis_index("inner"), WIDE_SPLIT)
    rows = got_ref[:, 80:96, :].reshape(MEMBERS * 16, 2 * HEAD_DIM)
    row, column = iota2(48, MEMBERS * 16)
    source_kv = 16 * (row // 2) + 8 + row % 2
    query_row = row - 32
    source_qg = 16 * (WIDE_SPLIT * fourth + query_row // 2) + 10 + row % 2
    source = jnp.where(row < 32, source_kv, source_qg)
    picked = dot(one_hot((column == source) & (row < 40)), rows).astype(BF16)
    for target in range(OUTERS):
        out_ref[target] = picked


def worker_kernel(mid_ref, wide_ref, out_ref, dk_ref, dv_ref, dq_ref):
    outer = lax.axis_index("outer")
    fourth = lax.rem(lax.axis_index("inner"), WIDE_SPLIT)
    kv = wide_ref[:, 0:32, :].reshape(OUTERS * 32, 2 * HEAD_DIM)
    qg = wide_ref[:, 32:48, :].astype(F32)[:, 0:8, :].reshape(OUTERS * 8, 2 * HEAD_DIM).astype(BF16)
    key, value = kv[:, :HEAD_DIM], kv[:, HEAD_DIM:]
    query, gradient = qg[:, :HEAD_DIM], qg[:, HEAD_DIM:]
    weights, score_gradients = attention_transposed(query, key, value, gradient)
    dk_ref[...] = dot(score_gradients, query)
    dv_ref[...] = dot(weights, gradient)
    dq_ref[...] = dot_tn(score_gradients, key)
    own_keys = pl.ds(pl.multiple_of(outer * 32, 32), 32)
    own_queries = pl.ds(pl.multiple_of(outer * 8, 8), 8)
    dk, dv = dk_ref[own_keys, :].astype(BF16), dv_ref[own_keys, :].astype(BF16)
    dq = dq_ref[own_queries, :].astype(BF16)
    row, column = iota2(MEMBERS * 8, 32)
    member, place = row // 8, row % 8
    wide_out = dot(one_hot((column == 2 * member + place - 2) & (place >= 2) & (place < 4)), dk)
    wide_out += dot(one_hot((column == 2 * member + place - 4) & (place >= 4) & (place < 6)), dv)
    row, column = iota2(MEMBERS * 8, 8)
    member, place = row // 8, row % 8
    wide_out += dot(
        one_hot((column == 2 * (member - WIDE_SPLIT * fourth) + place) & (place < 2)), dq
    )
    key = mid_ref[:, 0:64, :HEAD_DIM].reshape(MEMBERS * 64, HEAD_DIM)
    value = mid_ref[:, 0:64, HEAD_DIM:].reshape(MEMBERS * 64, HEAD_DIM)
    qg = mid_ref[:, 64:96, :].astype(F32)[:, 0:PART, :].reshape(MEMBERS * PART, 2 * HEAD_DIM)
    qg = qg.astype(BF16)
    query, gradient = qg[:, :HEAD_DIM], qg[:, HEAD_DIM:]
    weights, score_gradients = attention_transposed(query, key, value, gradient)
    out_ref[:, 0:64, :] = dot(score_gradients, query).astype(BF16).reshape(MEMBERS, 64, HEAD_DIM)
    out_ref[:, 64:128, :] = dot(weights, gradient).astype(BF16).reshape(MEMBERS, 64, HEAD_DIM)
    dq = dot_tn(key, score_gradients).T.reshape(MEMBERS, PART, HEAD_DIM)
    tail = jnp.concatenate([dq, wide_out.reshape(MEMBERS, 8, HEAD_DIM)], axis=1)
    out_ref[:, 128:160, :] = tail.astype(BF16)


def assemble_kernel(off_ref, got_ref, nq, nk, nv, dq_hbm, dk_hbm, dv_hbm, held, sems):
    inner = lax.axis_index("inner")
    copies = []

    def send(which, head, block):
        held[which, head] = block.astype(BF16)
        target = (dq_hbm, dk_hbm, dv_hbm)[which]
        copy = pltpu.make_async_copy(
            held.at[which, head],
            target.at[:, pl.ds(NEAR_END + head * HEAD_DIM, HEAD_DIM)],
            sems.at[which, head],
        )
        copy.start()
        copies.append(copy)

    row, unused = iota2(TOK, HEAD_DIM)
    for wide_head in range(H_WIDE):
        head = H_MID + wide_head
        offset = off_ref[head : head + 1, :]
        workers = range(wide_head * WIDE_SPLIT, (wide_head + 1) * WIDE_SPLIT)
        sums = sum(got_ref[worker, 144:160, :].astype(F32) for worker in workers)
        owner = wide_head * WIDE_SPLIT + lax.div(inner, WIDE_SPLIT)
        queries = got_ref[owner, 144:160, :].astype(F32)
        first, second = row == offset, row == offset + R_WIDE
        for which, rows, at in ((0, queries, 8), (1, sums, 10), (2, sums, 12)):
            spread = jnp.where(first, rows[at : at + 1], 0.0)
            send(which, head, jnp.where(second, rows[at + 1 : at + 2], spread))
    row, column = iota2(TOK, SPLIT * PART)
    row64, column64 = iota2(TOK, MID_ROWS)
    for head in range(H_MID):
        offset = off_ref[head : head + 1, :1]
        workers = range(head * SPLIT, (head + 1) * SPLIT)
        dq = jnp.concatenate(
            [got_ref[worker, 128:160, :].astype(F32)[0:PART] for worker in workers], axis=0
        ).astype(BF16)
        dk = sum(got_ref[worker, 0:64, :].astype(F32) for worker in workers).astype(BF16)
        dv = sum(got_ref[worker, 64:128, :].astype(F32) for worker in workers).astype(BF16)
        place = one_hot(row64 - R_MID * column64 == offset)
        send(0, head, dot(one_hot(row - R_MID * column == offset), dq))
        send(1, head, dot(place, dk))
        send(2, head, dot(place, dv))
    for copy in copies:
        copy.wait()


def spec(space):
    return pl.BlockSpec(memory_space=space)


def in_hbm(array):
    return pltpu.with_memory_space_constraint(array, pltpu.HBM)


def params(mebibytes):
    return pltpu.CompilerParams(vmem_limit_bytes=mebibytes * 1024 * 1024)


def shape(*sizes, kind=BF16):
    return jax.ShapeDtypeStruct(sizes, kind)


def body(queries, key_rows, values, out_grads, offsets):
    arrays = [in_hbm(array) for array in (queries, key_rows, values, out_grads)]
    heads = H_MID + H_WIDE
    packed, offset_rows = pl.pallas_call(
        pack_kernel,
        out_shape=[shape(MEMBERS, 96, 256), shape(heads, HEAD_DIM, kind=jnp.int32)],
        in_specs=[spec(pltpu.HBM)] * 5,
        out_specs=[spec(pltpu.VMEM)] * 2,
        scratch_shapes=[
            pltpu.SMEM((heads,), jnp.int32),
            pltpu.VMEM((4, heads, TOK, HEAD_DIM), BF16),
            pltpu.SemaphoreType.DMA,
            pltpu.SemaphoreType.DMA((4, heads)),
        ],
        compiler_params=params(16),
    )(in_hbm(offsets), *arrays)
    near_block = pl.BlockSpec((TOK, HEAD_DIM), lambda head: (0, head))
    near = pl.pallas_call(
        near_kernel,
        grid=(H_NEAR,),
        out_shape=[shape(TOK, HIDDEN)] * 3,
        in_specs=[near_block] * 4,
        out_specs=[near_block] * 3,
        cost_estimate=pl.CostEstimate(
            flops=10 * H_NEAR * TOK * TOK * HEAD_DIM,
            bytes_accessed=14 * TOK * NEAR_END,
            transcendentals=H_NEAR * TOK * TOK,
        ),
        compiler_params=params(16),
    )(*arrays)
    mid_got = lax.all_to_all(packed, "inner", 0, 0)
    wide_send = pl.pallas_call(
        forward_kernel,
        out_shape=shape(OUTERS, 48, 256),
        in_specs=[spec(pltpu.VMEM)],
        out_specs=spec(pltpu.VMEM),
        compiler_params=params(16),
    )(mid_got)
    wide_got = lax.all_to_all(wide_send, "outer", 0, 0)
    results = pl.pallas_call(
        worker_kernel,
        out_shape=shape(MEMBERS, 160, HEAD_DIM),
        in_specs=[spec(pltpu.VMEM)] * 2,
        out_specs=spec(pltpu.VMEM),
        scratch_shapes=[
            pltpu.VMEM((512, HEAD_DIM), F32),
            pltpu.VMEM((512, HEAD_DIM), F32),
            pltpu.VMEM((HEAD_DIM, HEAD_DIM), F32),
        ],
        compiler_params=params(32),
    )(mid_got, wide_got)
    returned = lax.all_to_all(results, "inner", 0, 0)
    return tuple(
        pl.pallas_call(
            assemble_kernel,
            out_shape=[shape(TOK, HIDDEN)] * 3,
            in_specs=[spec(pltpu.VMEM)] * 2 + [spec(pltpu.HBM)] * 3,
            out_specs=[spec(pltpu.HBM)] * 3,
            scratch_shapes=[
                pltpu.VMEM((3, heads, TOK, HEAD_DIM), BF16),
                pltpu.SemaphoreType.DMA((3, heads)),
            ],
            input_output_aliases={2: 0, 3: 1, 4: 2},
            compiler_params=params(16),
        )(offset_rows, returned, *near)
    )


def solution(mesh):
    rows = P(("outer", "inner"), None)
    return jax.shard_map(
        body,
        mesh=mesh,
        in_specs=(rows, rows, rows, rows, P()),
        out_specs=(rows, rows, rows),
        check_vma=False,
    )
```

```python
import math

import jax
import jax.numpy as jnp
from jax import lax
from jax.experimental import pallas as pl
from jax.experimental.pallas import tpu as pltpu
from jax.sharding import PartitionSpec as P

HEAD_DIM = 128
H_NEAR = 4
H_MID = 5
H_WIDE = 3
R_MID = 4
R_WIDE = 128
TOK = 256
NEAR_END = H_NEAR * HEAD_DIM
MID_END = NEAR_END + H_MID * HEAD_DIM
HIDDEN = MID_END + H_WIDE * HEAD_DIM
OUTERS = 16
MID_ROWS = TOK // R_MID
SLOTS = 8
HALVES = 2
HALF_KEYS = SLOTS * MID_ROWS
QUERY_BLOCK = 256
ALONG_Z = [[HALVES * z + half for z in range(SLOTS)] for half in range(HALVES)]
ACROSS_Y = [(member, member ^ 1) for member in range(HALVES * SLOTS)]
SCALE = 1.0 / math.sqrt(HEAD_DIM)
BF16 = jnp.bfloat16
F32 = jnp.float32


def dot(a, b):
    return lax.dot_general(a, b, (((1,), (0,)), ((), ())), preferred_element_type=F32)


def dot_nt(a, b):
    return lax.dot_general(a, b, (((1,), (1,)), ((), ())), preferred_element_type=F32)


def dot_tn(a, b):
    return lax.dot_general(a, b, (((0,), (0,)), ((), ())), preferred_element_type=F32)


def iota2(rows, columns):
    shape = (rows, columns)
    return (
        lax.broadcasted_iota(jnp.int32, shape, 0),
        lax.broadcasted_iota(jnp.int32, shape, 1),
    )


def one_hot(condition):
    return jnp.where(condition, 1.0, 0.0).astype(BF16)


def attention_transposed(query, key, value, gradient):
    scores = dot_nt(key, query) * SCALE
    exponent = jnp.exp(scores - jnp.max(scores, axis=0, keepdims=True))
    weights = exponent * (1.0 / jnp.sum(exponent, axis=0, keepdims=True))
    products = dot_nt(value, gradient)
    row_dots = jnp.sum(weights * products, axis=0, keepdims=True)
    score_gradients = (weights * (products - row_dots) * SCALE).astype(BF16)
    return weights.astype(BF16), score_gradients


def pack_kernel(off_hbm, q_hbm, k_hbm, v_hbm, g_hbm, out_ref, off_out, off_ref, held, off_sem, sems):
    off_copy = pltpu.make_async_copy(off_hbm, off_ref, off_sem)
    off_copy.start()
    order = list(range(H_MID, H_MID + H_WIDE)) + list(range(H_MID))
    copies = {}
    for head in order:
        for which, source in enumerate((q_hbm, k_hbm, v_hbm, g_hbm)):
            copies[head, which] = pltpu.make_async_copy(
                source.at[:, pl.ds(NEAR_END + head * HEAD_DIM, HEAD_DIM)],
                held.at[which, head],
                sems.at[which, head],
            )
            copies[head, which].start()
    off_copy.wait()
    for head in range(H_MID + H_WIDE):
        off_out[head : head + 1, :] = jnp.full((1, HEAD_DIM), off_ref[head], jnp.int32)
    row, column = iota2(16, TOK)
    for head in range(H_MID, H_MID + H_WIDE):
        offset = off_ref[head]
        pick_kv = one_hot((row < 2) & (column == offset + R_WIDE * row))
        pick_qg = one_hot((row >= 2) & (row < 4) & (column == offset + R_WIDE * (row - 2)))
        for which in range(4):
            copies[head, which].wait()
        kv = jnp.concatenate([held[1, head], held[2, head]], axis=1)
        qg = jnp.concatenate([held[0, head], held[3, head]], axis=1)
        out_ref[head, 0:16, :] = (dot(pick_kv, kv) + dot(pick_qg, qg)).astype(BF16)
        out_ref[head, 16:128, :] = jnp.zeros((112, 2 * HEAD_DIM), BF16)
    row, column = iota2(MID_ROWS, TOK)
    for head in range(H_MID):
        pick = one_hot(column == off_ref[head] + R_MID * row)
        for which in range(4):
            copies[head, which].wait()
        kv = jnp.concatenate([held[1, head], held[2, head]], axis=1)
        qg = jnp.concatenate([held[0, head], held[3, head]], axis=1)
        out_ref[head, 0:64, :] = dot(pick, kv).astype(BF16)
        out_ref[head, 64:128, :] = dot(pick, qg).astype(BF16)


def near_kernel(q_ref, k_ref, v_ref, g_ref, dq_ref, dk_ref, dv_ref):
    query, key, value, gradient = q_ref[...], k_ref[...], v_ref[...], g_ref[...]
    weights, score_gradients = attention_transposed(query, key, value, gradient)
    dq_ref[...] = dot_tn(score_gradients, key).astype(BF16)
    dk_ref[...] = dot(score_gradients, query).astype(BF16)
    dv_ref[...] = dot(weights, gradient).astype(BF16)


def slot():
    return lax.div(lax.axis_index("inner"), HALVES)


def mid_kernel(own_ref, other_ref, dq_ref, own_out, other_out, wide_out, dkv_ref):
    @pl.when(slot() >= H_MID)
    def forward_wide():
        rows = jnp.concatenate([own_ref[:, 0:16, :], other_ref[:, 0:16, :]], axis=0)
        rows = rows.reshape(2 * SLOTS * 16, 2 * HEAD_DIM)
        row, column = iota2(64, 2 * SLOTS * 16)
        place = row % 2 + jnp.where(row < 32, 0, 2)
        picked = dot(one_hot(column == 16 * ((row % 32) // 2) + place), rows).astype(BF16)
        for target in range(OUTERS):
            wide_out[target] = picked

    @pl.when(slot() < H_MID)
    def attend():
        kv = [ref[:, 0:64, :].reshape(HALF_KEYS, 2 * HEAD_DIM) for ref in (own_ref, other_ref)]
        kv = jnp.concatenate(kv, axis=0)
        key, value = kv[:, :HEAD_DIM], kv[:, HEAD_DIM:]
        qg = own_ref[:, 64:128, :].reshape(HALF_KEYS, 2 * HEAD_DIM)
        for start in range(0, HALF_KEYS, QUERY_BLOCK):
            query = qg[start : start + QUERY_BLOCK, :HEAD_DIM]
            gradient = qg[start : start + QUERY_BLOCK, HEAD_DIM:]
            weights, score_gradients = attention_transposed(query, key, value, gradient)
            dk, dv = dot(score_gradients, query), dot(weights, gradient)
            if start == 0:
                dkv_ref[:, :HEAD_DIM] = dk
                dkv_ref[:, HEAD_DIM:] = dv
            else:
                dkv_ref[:, :HEAD_DIM] += dk
                dkv_ref[:, HEAD_DIM:] += dv
            dq = dot_tn(key, score_gradients).T.astype(BF16)
            blocks = slice(start // MID_ROWS, (start + QUERY_BLOCK) // MID_ROWS)
            dq_ref[blocks] = dq.reshape(QUERY_BLOCK // MID_ROWS, MID_ROWS, HEAD_DIM)
        own_out[...] = dkv_ref[:HALF_KEYS, :]
        other = dkv_ref[HALF_KEYS:, :].astype(BF16)
        other_out[...] = other.reshape(SLOTS, MID_ROWS, 2 * HEAD_DIM)


def return_kernel(wide_ref, dq_ref, own_ref, back_ref, out_ref):
    @pl.when(slot() < H_MID)
    def add_halves():
        out_ref[:, 0:64, :] = dq_ref[...]
        back = back_ref[...].reshape(HALF_KEYS, 2 * HEAD_DIM).astype(F32)
        dkv = (own_ref[...] + back).astype(BF16)
        out_ref[:, 64:128, :] = dkv[:, :HEAD_DIM].reshape(SLOTS, MID_ROWS, HEAD_DIM)
        out_ref[:, 128:192, :] = dkv[:, HEAD_DIM:].reshape(SLOTS, MID_ROWS, HEAD_DIM)

    @pl.when(slot() >= H_MID)
    def attend_wide():
        kv = wide_ref[:, 0:32, :].reshape(OUTERS * 32, 2 * HEAD_DIM)
        qg = wide_ref[:, 32:64, :].reshape(OUTERS * 32, 2 * HEAD_DIM)
        key, value = kv[:, :HEAD_DIM], kv[:, HEAD_DIM:]
        query, gradient = qg[:, :HEAD_DIM], qg[:, HEAD_DIM:]
        scores = dot_nt(key, query) * SCALE
        top = jnp.max(scores, axis=0, keepdims=True)
        exponent = jnp.exp(scores - top)
        inverse = 1.0 / jnp.sum(exponent, axis=0, keepdims=True)
        products = dot_nt(value, gradient)
        row_dots = jnp.sum(exponent * inverse * products, axis=0, keepdims=True)
        outer = lax.axis_index("outer")
        own_kv, own_qg = wide_ref[outer, 0:16, :], wide_ref[outer, 32:48, :]
        own_key, own_value = own_kv[:, :HEAD_DIM], own_kv[:, HEAD_DIM:]
        own_query, own_gradient = own_qg[:, :HEAD_DIM], own_qg[:, HEAD_DIM:]
        weights = jnp.exp(dot_nt(own_key, query) * SCALE - top) * inverse
        score_gradients = weights * (dot_nt(own_value, gradient) - row_dots) * SCALE
        dk = dot(score_gradients.astype(BF16), query).astype(BF16)
        dv = dot(weights.astype(BF16), gradient).astype(BF16)
        scores = dot_nt(own_query, key) * SCALE
        exponent = jnp.exp(scores - jnp.max(scores, axis=1, keepdims=True))
        weights = exponent * (1.0 / jnp.sum(exponent, axis=1, keepdims=True))
        products = dot_nt(own_gradient, value)
        row_dots = jnp.sum(weights * products, axis=1, keepdims=True)
        score_gradients = weights * (products - row_dots) * SCALE
        dq = dot(score_gradients.astype(BF16), key).astype(BF16)
        row, column = iota2(SLOTS * 16, 16)
        member, place = row // 16, row % 16
        spread = 0.0
        for which, rows in enumerate((dq, dk, dv)):
            mine = (place >= 2 * which) & (place < 2 * which + 2)
            spread += dot(one_hot(mine & (column == 2 * member + place - 2 * which)), rows)
        out_ref[:, 0:16, :] = spread.astype(BF16).reshape(SLOTS, 16, HEAD_DIM)


def assemble_kernel(off_ref, got_ref, nq, nk, nv, dq_hbm, dk_hbm, dv_hbm, held, sems):
    copies = []

    def send(which, head, block):
        held[which, head] = block.astype(BF16)
        target = (dq_hbm, dk_hbm, dv_hbm)[which]
        copy = pltpu.make_async_copy(
            held.at[which, head],
            target.at[:, pl.ds(NEAR_END + head * HEAD_DIM, HEAD_DIM)],
            sems.at[which, head],
        )
        copy.start()
        copies.append(copy)

    row, unused = iota2(TOK, HEAD_DIM)
    for head in range(H_MID, H_MID + H_WIDE):
        offset = off_ref[head : head + 1, :]
        rows = got_ref[head, 0:16, :].astype(F32)
        first, second = row == offset, row == offset + R_WIDE
        for which in range(3):
            spread = jnp.where(first, rows[2 * which : 2 * which + 1], 0.0)
            send(which, head, jnp.where(second, rows[2 * which + 1 : 2 * which + 2], spread))
    row, column = iota2(TOK, MID_ROWS)
    for head in range(H_MID):
        place = one_hot(row - R_MID * column == off_ref[head : head + 1, :1])
        for which in range(3):
            send(which, head, dot(place, got_ref[head, 64 * which : 64 * which + 64, :]))
    for copy in copies:
        copy.wait()


def spec(space):
    return pl.BlockSpec(memory_space=space)


def in_hbm(array):
    return pltpu.with_memory_space_constraint(array, pltpu.HBM)


def params(mebibytes):
    return pltpu.CompilerParams(vmem_limit_bytes=mebibytes * 1024 * 1024)


def shape(*sizes, kind=BF16):
    return jax.ShapeDtypeStruct(sizes, kind)


def body(queries, key_rows, values, out_grads, offsets):
    arrays = [in_hbm(array) for array in (queries, key_rows, values, out_grads)]
    heads = H_MID + H_WIDE
    packed, offset_rows = pl.pallas_call(
        pack_kernel,
        out_shape=[shape(SLOTS, 128, 256), shape(heads, HEAD_DIM, kind=jnp.int32)],
        in_specs=[spec(pltpu.HBM)] * 5,
        out_specs=[spec(pltpu.VMEM)] * 2,
        scratch_shapes=[
            pltpu.SMEM((heads,), jnp.int32),
            pltpu.VMEM((4, heads, TOK, HEAD_DIM), BF16),
            pltpu.SemaphoreType.DMA,
            pltpu.SemaphoreType.DMA((4, heads)),
        ],
        compiler_params=params(16),
    )(in_hbm(offsets), *arrays)
    near_block = pl.BlockSpec((TOK, HEAD_DIM), lambda head: (0, head))
    near = pl.pallas_call(
        near_kernel,
        grid=(H_NEAR,),
        out_shape=[shape(TOK, HIDDEN)] * 3,
        in_specs=[near_block] * 4,
        out_specs=[near_block] * 3,
        cost_estimate=pl.CostEstimate(
            flops=10 * H_NEAR * TOK * TOK * HEAD_DIM,
            bytes_accessed=14 * TOK * NEAR_END,
            transcendentals=H_NEAR * TOK * TOK,
        ),
        compiler_params=params(16),
    )(*arrays)
    own = lax.all_to_all(packed, "inner", 0, 0, axis_index_groups=ALONG_Z)
    other = lax.ppermute(own[:, 0:64, :], "inner", ACROSS_Y)
    dq, own_sums, other_sums, wide_send = pl.pallas_call(
        mid_kernel,
        out_shape=[
            shape(SLOTS, MID_ROWS, HEAD_DIM),
            shape(HALF_KEYS, 256, kind=F32),
            shape(SLOTS, MID_ROWS, 256),
            shape(OUTERS, 64, 256),
        ],
        in_specs=[spec(pltpu.VMEM)] * 2,
        out_specs=[spec(pltpu.VMEM)] * 4,
        scratch_shapes=[pltpu.VMEM((HALVES * HALF_KEYS, 256), F32)],
        compiler_params=params(32),
    )(own, other)
    back = lax.ppermute(other_sums, "inner", ACROSS_Y)
    wide_got = lax.all_to_all(wide_send, "outer", 0, 0)
    results = pl.pallas_call(
        return_kernel,
        out_shape=shape(SLOTS, 192, HEAD_DIM),
        in_specs=[spec(pltpu.VMEM)] * 4,
        out_specs=spec(pltpu.VMEM),
        compiler_params=params(32),
    )(wide_got, dq, own_sums, back)
    returned = lax.all_to_all(results, "inner", 0, 0, axis_index_groups=ALONG_Z)
    return tuple(
        pl.pallas_call(
            assemble_kernel,
            out_shape=[shape(TOK, HIDDEN)] * 3,
            in_specs=[spec(pltpu.VMEM)] * 2 + [spec(pltpu.HBM)] * 3,
            out_specs=[spec(pltpu.HBM)] * 3,
            scratch_shapes=[
                pltpu.VMEM((3, heads, TOK, HEAD_DIM), BF16),
                pltpu.SemaphoreType.DMA((3, heads)),
            ],
            input_output_aliases={2: 0, 3: 1, 4: 2},
            compiler_params=params(16),
        )(offset_rows, returned, *near)
    )


def solution(mesh):
    rows = P(("outer", "inner"), None)
    return jax.shard_map(
        body,
        mesh=mesh,
        in_specs=(rows, rows, rows, rows, P()),
        out_specs=(rows, rows, rows),
        check_vma=False,
    )
```

```python
import math

import jax
import jax.numpy as jnp
from jax import lax
from jax.experimental import pallas as pl
from jax.experimental.pallas import tpu as pltpu
from jax.sharding import PartitionSpec as P

HEAD_DIM = 128
H_NEAR = 4
H_MID = 5
H_WIDE = 3
R_MID = 4
R_WIDE = 128
TOK = 256
NEAR_END = H_NEAR * HEAD_DIM
MID_END = NEAR_END + H_MID * HEAD_DIM
HIDDEN = MID_END + H_WIDE * HEAD_DIM
OUTERS = 16
MID_ROWS = TOK // R_MID
SLOTS = 8
HALVES = 2
HALF_KEYS = SLOTS * MID_ROWS
QUERY_BLOCK = 256
ALONG_Z = [[HALVES * z + half for z in range(SLOTS)] for half in range(HALVES)]
ACROSS_Y = [(member, member ^ 1) for member in range(HALVES * SLOTS)]
SCALE = 1.0 / math.sqrt(HEAD_DIM)
BF16 = jnp.bfloat16
F32 = jnp.float32


def dot(a, b):
    return lax.dot_general(a, b, (((1,), (0,)), ((), ())), preferred_element_type=F32)


def dot_nt(a, b):
    return lax.dot_general(a, b, (((1,), (1,)), ((), ())), preferred_element_type=F32)


def dot_tn(a, b):
    return lax.dot_general(a, b, (((0,), (0,)), ((), ())), preferred_element_type=F32)


def iota2(rows, columns):
    shape = (rows, columns)
    return (
        lax.broadcasted_iota(jnp.int32, shape, 0),
        lax.broadcasted_iota(jnp.int32, shape, 1),
    )


def one_hot(condition):
    return jnp.where(condition, 1.0, 0.0).astype(BF16)


def attention_transposed(query, key, value, gradient):
    scores = dot_nt(key, query) * SCALE
    exponent = jnp.exp(scores - jnp.max(scores, axis=0, keepdims=True))
    weights = exponent * (1.0 / jnp.sum(exponent, axis=0, keepdims=True))
    products = dot_nt(value, gradient)
    row_dots = jnp.sum(weights * products, axis=0, keepdims=True)
    score_gradients = (weights * (products - row_dots) * SCALE).astype(BF16)
    return weights.astype(BF16), score_gradients


def fetch(sources, held, sems, heads):
    copies = {}
    for at, head in enumerate(heads):
        for which, source in enumerate(sources):
            copies[head, which] = pltpu.make_async_copy(
                source.at[:, pl.ds(NEAR_END + head * HEAD_DIM, HEAD_DIM)],
                held.at[which, at],
                sems.at[which, at],
            )
            copies[head, which].start()
    return copies


def pairs(copies, held, head, at):
    for which in range(4):
        copies[head, which].wait()
    kv = jnp.concatenate([held[1, at], held[2, at]], axis=1)
    qg = jnp.concatenate([held[0, at], held[3, at]], axis=1)
    return kv, qg


def wide_kernel(off_hbm, q_hbm, k_hbm, v_hbm, g_hbm, out_ref, off_out, off_ref, held, off_sem, sems):
    off_copy = pltpu.make_async_copy(off_hbm, off_ref, off_sem)
    off_copy.start()
    heads = range(H_MID, H_MID + H_WIDE)
    copies = fetch((q_hbm, k_hbm, v_hbm, g_hbm), held, sems, heads)
    off_copy.wait()
    for head in range(H_MID + H_WIDE):
        off_out[head : head + 1, :] = jnp.full((1, TOK), off_ref[head], jnp.int32)
    row, column = iota2(16, TOK)
    rows = 0.0
    for at, head in enumerate(heads):
        kv, qg = pairs(copies, held, head, at)
        offset = off_ref[head]
        for start, block in ((2 * at, kv), (6 + 2 * at, qg)):
            mine = (row >= start) & (row < start + 2)
            rows += dot(one_hot(mine & (column == offset + R_WIDE * (row - start))), block)
    rows = rows.astype(BF16)
    for target in range(OUTERS):
        out_ref[target] = rows


def mid_pack_kernel(off_ref, q_hbm, k_hbm, v_hbm, g_hbm, out_ref, held, sems):
    copies = fetch((q_hbm, k_hbm, v_hbm, g_hbm), held, sems, range(H_MID))
    row, column = iota2(MID_ROWS, TOK)
    for head in range(H_MID):
        pick = one_hot(column - R_MID * row == off_ref[head : head + 1, :])
        kv, qg = pairs(copies, held, head, head)
        out_ref[head, 0:64, :] = dot(pick, kv).astype(BF16)
        out_ref[head, 64:128, :] = dot(pick, qg).astype(BF16)
    for head in range(H_MID, SLOTS):
        out_ref[head, 64:128, :] = jnp.zeros((64, 2 * HEAD_DIM), BF16)


def wide_pack_kernel(got_ref, packed, out, held, sems):
    rows = got_ref[...].reshape(OUTERS * 16, 2 * HEAD_DIM)
    row, column = iota2(64, OUTERS * 16)
    base = 16 * ((row % 32) // 2) + row % 2 + jnp.where(row < 32, 0, 6)
    copies = []
    for head in range(H_WIDE):
        held[head] = dot(one_hot(column == base + 2 * head), rows).astype(BF16)
        copy = pltpu.make_async_copy(
            held.at[head], out.at[H_MID + head, pl.ds(0, 64)], sems.at[head]
        )
        copy.start()
        copies.append(copy)
    for copy in copies:
        copy.wait()


def near_kernel(after, q_ref, k_ref, v_ref, g_ref, dq_ref, dk_ref, dv_ref):
    query, key, value, gradient = q_ref[...], k_ref[...], v_ref[...], g_ref[...]
    weights, score_gradients = attention_transposed(query, key, value, gradient)
    dq_ref[...] = dot_tn(score_gradients, key).astype(BF16)
    dk_ref[...] = dot(score_gradients, query).astype(BF16)
    dv_ref[...] = dot(weights, gradient).astype(BF16)


def slot():
    return lax.div(lax.axis_index("inner"), HALVES)


def attend_wide(own_ref, other_ref, out_ref):
    wide_rows = SLOTS * 32
    kv = [ref[:, 0:32, :].reshape(wide_rows, 2 * HEAD_DIM) for ref in (own_ref, other_ref)]
    qg = [ref[:, 32:64, :].reshape(wide_rows, 2 * HEAD_DIM) for ref in (own_ref, other_ref)]
    row, column = iota2(16, wide_rows)
    source = 32 * (row // 2) + 2 * lax.axis_index("outer") + row % 2
    pick = one_hot(column == source)
    own_kv, own_qg = dot(pick, kv[0]).astype(BF16), dot(pick, qg[0]).astype(BF16)
    kv, qg = jnp.concatenate(kv, axis=0), jnp.concatenate(qg, axis=0)
    key, value = kv[:, :HEAD_DIM], kv[:, HEAD_DIM:]
    query, gradient = qg[:, :HEAD_DIM], qg[:, HEAD_DIM:]
    scores = dot_nt(key, query) * SCALE
    top = jnp.max(scores, axis=0, keepdims=True)
    exponent = jnp.exp(scores - top)
    inverse = 1.0 / jnp.sum(exponent, axis=0, keepdims=True)
    products = dot_nt(value, gradient)
    row_dots = jnp.sum(exponent * inverse * products, axis=0, keepdims=True)
    own_key, own_value = own_kv[:, :HEAD_DIM], own_kv[:, HEAD_DIM:]
    own_query, own_gradient = own_qg[:, :HEAD_DIM], own_qg[:, HEAD_DIM:]
    weights = jnp.exp(dot_nt(own_key, query) * SCALE - top) * inverse
    score_gradients = weights * (dot_nt(own_value, gradient) - row_dots) * SCALE
    dk = dot(score_gradients.astype(BF16), query).astype(BF16)
    dv = dot(weights.astype(BF16), gradient).astype(BF16)
    scores = dot_nt(own_query, key) * SCALE
    exponent = jnp.exp(scores - jnp.max(scores, axis=1, keepdims=True))
    weights = exponent * (1.0 / jnp.sum(exponent, axis=1, keepdims=True))
    products = dot_nt(own_gradient, value)
    row_dots = jnp.sum(weights * products, axis=1, keepdims=True)
    score_gradients = weights * (products - row_dots) * SCALE
    dq = dot(score_gradients.astype(BF16), key).astype(BF16)
    row, column = iota2(SLOTS * 16, 16)
    member, place = row // 16, row % 16
    spread = 0.0
    for which, rows in enumerate((dq, dk, dv)):
        mine = (place >= 2 * which) & (place < 2 * which + 2)
        spread += dot(one_hot(mine & (column == 2 * member + place - 2 * which)), rows)
    out_ref[...] = spread.astype(BF16).reshape(SLOTS, 16, HEAD_DIM)


def work_kernel(own_ref, other_ref, dq_ref, own_out, wide_out, other_out, dkv_ref):
    @pl.when(slot() >= H_MID)
    def wide():
        attend_wide(own_ref, other_ref, wide_out)

    @pl.when(slot() < H_MID)
    def attend():
        kv = [ref[:, 0:64, :].reshape(HALF_KEYS, 2 * HEAD_DIM) for ref in (own_ref, other_ref)]
        kv = jnp.concatenate(kv, axis=0)
        key, value = kv[:, :HEAD_DIM], kv[:, HEAD_DIM:]
        qg = own_ref[:, 64:128, :].reshape(HALF_KEYS, 2 * HEAD_DIM)
        for start in range(0, HALF_KEYS, QUERY_BLOCK):
            query = qg[start : start + QUERY_BLOCK, :HEAD_DIM]
            gradient = qg[start : start + QUERY_BLOCK, HEAD_DIM:]
            weights, score_gradients = attention_transposed(query, key, value, gradient)
            dk, dv = dot(score_gradients, query), dot(weights, gradient)
            if start == 0:
                dkv_ref[:, :HEAD_DIM] = dk
                dkv_ref[:, HEAD_DIM:] = dv
            else:
                dkv_ref[:, :HEAD_DIM] += dk
                dkv_ref[:, HEAD_DIM:] += dv
            dq = dot_tn(key, score_gradients).T.astype(BF16)
            blocks = slice(start // MID_ROWS, (start + QUERY_BLOCK) // MID_ROWS)
            dq_ref[blocks] = dq.reshape(QUERY_BLOCK // MID_ROWS, MID_ROWS, HEAD_DIM)
        own_out[...] = dkv_ref[:HALF_KEYS, :]
        other = dkv_ref[HALF_KEYS:, :].astype(BF16)
        other_out[...] = other.reshape(SLOTS, MID_ROWS, 2 * HEAD_DIM)


def return_kernel(dq_ref, own_ref, wide_ref, back_ref, out_ref):
    @pl.when(slot() < H_MID)
    def add_halves():
        out_ref[:, 0:64, :] = dq_ref[...]
        back = back_ref[...].reshape(HALF_KEYS, 2 * HEAD_DIM).astype(F32)
        dkv = (own_ref[...] + back).astype(BF16)
        out_ref[:, 64:128, :] = dkv[:, :HEAD_DIM].reshape(SLOTS, MID_ROWS, HEAD_DIM)
        out_ref[:, 128:192, :] = dkv[:, HEAD_DIM:].reshape(SLOTS, MID_ROWS, HEAD_DIM)

    @pl.when(slot() >= H_MID)
    def wide():
        out_ref[:, 0:16, :] = wide_ref[...]


def assemble_kernel(off_ref, got_ref, nq, nk, nv, dq_hbm, dk_hbm, dv_hbm, held, sems):
    copies = []

    def send(which, head, block):
        held[which, head] = block.astype(BF16)
        target = (dq_hbm, dk_hbm, dv_hbm)[which]
        copy = pltpu.make_async_copy(
            held.at[which, head],
            target.at[:, pl.ds(NEAR_END + head * HEAD_DIM, HEAD_DIM)],
            sems.at[which, head],
        )
        copy.start()
        copies.append(copy)

    row, unused = iota2(TOK, HEAD_DIM)
    for head in range(H_MID, H_MID + H_WIDE):
        offset = off_ref[head : head + 1, :HEAD_DIM]
        rows = got_ref[head, 0:16, :].astype(F32)
        first, second = row == offset, row == offset + R_WIDE
        for which in range(3):
            spread = jnp.where(first, rows[2 * which : 2 * which + 1], 0.0)
            send(which, head, jnp.where(second, rows[2 * which + 1 : 2 * which + 2], spread))
    row, column = iota2(TOK, MID_ROWS)
    for head in range(H_MID):
        place = one_hot(row - R_MID * column == off_ref[head : head + 1, :1])
        for which in range(3):
            send(which, head, dot(place, got_ref[head, 64 * which : 64 * which + 64, :]))
    for copy in copies:
        copy.wait()


def spec(space):
    return pl.BlockSpec(memory_space=space)


def in_hbm(array):
    return pltpu.with_memory_space_constraint(array, pltpu.HBM)


def params(mebibytes):
    return pltpu.CompilerParams(vmem_limit_bytes=mebibytes * 1024 * 1024)


def shape(*sizes, kind=BF16):
    return jax.ShapeDtypeStruct(sizes, kind)


def body(queries, key_rows, values, out_grads, offsets):
    arrays = [in_hbm(array) for array in (queries, key_rows, values, out_grads)]
    heads = H_MID + H_WIDE
    wide_send, offset_rows = pl.pallas_call(
        wide_kernel,
        out_shape=[shape(OUTERS, 16, 256), shape(heads, TOK, kind=jnp.int32)],
        in_specs=[spec(pltpu.HBM)] * 5,
        out_specs=[spec(pltpu.VMEM)] * 2,
        scratch_shapes=[
            pltpu.SMEM((heads,), jnp.int32),
            pltpu.VMEM((4, H_WIDE, TOK, HEAD_DIM), BF16),
            pltpu.SemaphoreType.DMA,
            pltpu.SemaphoreType.DMA((4, H_WIDE)),
        ],
        compiler_params=params(8),
    )(in_hbm(offsets), *arrays)
    wide_got = lax.all_to_all(wide_send, "outer", 0, 0)
    packed = pl.pallas_call(
        mid_pack_kernel,
        out_shape=shape(SLOTS, 128, 256),
        in_specs=[spec(pltpu.VMEM)] + [spec(pltpu.HBM)] * 4,
        out_specs=spec(pltpu.VMEM),
        scratch_shapes=[
            pltpu.VMEM((4, H_MID, TOK, HEAD_DIM), BF16),
            pltpu.SemaphoreType.DMA((4, H_MID)),
        ],
        cost_estimate=pl.CostEstimate(
            flops=8 * H_MID * MID_ROWS * TOK * HEAD_DIM,
            bytes_accessed=8 * H_MID * TOK * HEAD_DIM,
            transcendentals=0,
        ),
        compiler_params=params(8),
    )(offset_rows, *arrays)
    packed = pl.pallas_call(
        wide_pack_kernel,
        out_shape=shape(SLOTS, 128, 256),
        in_specs=[spec(pltpu.VMEM), spec(pl.ANY)],
        out_specs=spec(pl.ANY),
        scratch_shapes=[
            pltpu.VMEM((H_WIDE, 64, 256), BF16),
            pltpu.SemaphoreType.DMA((H_WIDE,)),
        ],
        input_output_aliases={1: 0},
        compiler_params=params(8),
    )(wide_got, packed)
    own = lax.all_to_all(packed, "inner", 0, 0, axis_index_groups=ALONG_Z)
    other = lax.ppermute(own[:, 0:64, :], "inner", ACROSS_Y)
    dq, own_sums, wide_rows, other_sums = pl.pallas_call(
        work_kernel,
        out_shape=[
            shape(SLOTS, MID_ROWS, HEAD_DIM),
            shape(HALF_KEYS, 256, kind=F32),
            shape(SLOTS, 16, HEAD_DIM),
            shape(SLOTS, MID_ROWS, 256),
        ],
        in_specs=[spec(pltpu.VMEM)] * 2,
        out_specs=[spec(pltpu.VMEM)] * 4,
        scratch_shapes=[pltpu.VMEM((HALVES * HALF_KEYS, 256), F32)],
        compiler_params=params(32),
    )(own, other)
    back = lax.ppermute(other_sums, "inner", ACROSS_Y)
    near_block = pl.BlockSpec((TOK, HEAD_DIM), lambda head: (0, head))
    near = pl.pallas_call(
        near_kernel,
        grid=(H_NEAR,),
        out_shape=[shape(TOK, HIDDEN)] * 3,
        in_specs=[spec(pl.ANY)] + [near_block] * 4,
        out_specs=[near_block] * 3,
        cost_estimate=pl.CostEstimate(
            flops=10 * H_NEAR * TOK * TOK * HEAD_DIM,
            bytes_accessed=14 * TOK * NEAR_END,
            transcendentals=H_NEAR * TOK * TOK,
        ),
        compiler_params=params(16),
    )(other_sums, *arrays)
    results = pl.pallas_call(
        return_kernel,
        out_shape=shape(SLOTS, 192, HEAD_DIM),
        in_specs=[spec(pltpu.VMEM)] * 4,
        out_specs=spec(pltpu.VMEM),
        compiler_params=params(16),
    )(dq, own_sums, wide_rows, back)
    returned = lax.all_to_all(results, "inner", 0, 0, axis_index_groups=ALONG_Z)
    return tuple(
        pl.pallas_call(
            assemble_kernel,
            out_shape=[shape(TOK, HIDDEN)] * 3,
            in_specs=[spec(pltpu.VMEM)] * 2 + [spec(pltpu.HBM)] * 3,
            out_specs=[spec(pltpu.HBM)] * 3,
            scratch_shapes=[
                pltpu.VMEM((3, heads, TOK, HEAD_DIM), BF16),
                pltpu.SemaphoreType.DMA((3, heads)),
            ],
            input_output_aliases={2: 0, 3: 1, 4: 2},
            compiler_params=params(16),
        )(offset_rows, returned, *near)
    )


def solution(mesh):
    rows = P(("outer", "inner"), None)
    return jax.shard_map(
        body,
        mesh=mesh,
        in_specs=(rows, rows, rows, rows, P()),
        out_specs=(rows, rows, rows),
        check_vma=False,
    )
```

```python
import functools
import math

import jax
import jax.numpy as jnp
from jax import lax
from jax.experimental import pallas as pl
from jax.experimental.pallas import tpu as pltpu
from jax.sharding import PartitionSpec as P

HEAD_DIM = 128
H_NEAR = 4
H_MID = 5
H_WIDE = 3
R_MID = 4
R_WIDE = 128
TOK = 256
NEAR_END = H_NEAR * HEAD_DIM
MID_END = NEAR_END + H_MID * HEAD_DIM
HIDDEN = MID_END + H_WIDE * HEAD_DIM
OUTERS = 16
MID_ROWS = TOK // R_MID
SLOTS = 8
HALVES = 2
HALF_KEYS = SLOTS * MID_ROWS
QUERY_BLOCK = 256
ALONG_Z = [[HALVES * z + half for z in range(SLOTS)] for half in range(HALVES)]
ACROSS_Y = [(member, member ^ 1) for member in range(HALVES * SLOTS)]
SCALE = 1.0 / math.sqrt(HEAD_DIM)
BF16 = jnp.bfloat16
F32 = jnp.float32


def dot(a, b):
    return lax.dot_general(a, b, (((1,), (0,)), ((), ())), preferred_element_type=F32)


def dot_nt(a, b):
    return lax.dot_general(a, b, (((1,), (1,)), ((), ())), preferred_element_type=F32)


def dot_tn(a, b):
    return lax.dot_general(a, b, (((0,), (0,)), ((), ())), preferred_element_type=F32)


def iota2(rows, columns):
    shape = (rows, columns)
    return (
        lax.broadcasted_iota(jnp.int32, shape, 0),
        lax.broadcasted_iota(jnp.int32, shape, 1),
    )


def one_hot(condition):
    return jnp.where(condition, 1.0, 0.0).astype(BF16)


def attention_transposed(query, key, value, gradient):
    scores = dot_nt(key, query) * SCALE
    exponent = jnp.exp(scores - jnp.max(scores, axis=0, keepdims=True))
    weights = exponent * (1.0 / jnp.sum(exponent, axis=0, keepdims=True))
    products = dot_nt(value, gradient)
    row_dots = jnp.sum(weights * products, axis=0, keepdims=True)
    score_gradients = (weights * (products - row_dots) * SCALE).astype(BF16)
    return weights.astype(BF16), score_gradients


def fetch(sources, held, sems, heads, first=NEAR_END):
    copies = {}
    for at, head in enumerate(heads):
        for which, source in enumerate(sources):
            copies[head, which] = pltpu.make_async_copy(
                source.at[:, pl.ds(first + head * HEAD_DIM, HEAD_DIM)],
                held.at[which, at],
                sems.at[which, at],
            )
            copies[head, which].start()
    return copies


def pairs(copies, held, head, at):
    for which in range(4):
        copies[head, which].wait()
    kv = jnp.concatenate([held[1, at], held[2, at]], axis=1)
    qg = jnp.concatenate([held[0, at], held[3, at]], axis=1)
    return kv, qg


def wide_kernel(off_hbm, q_hbm, k_hbm, v_hbm, g_hbm, out_ref, off_out, off_ref, held, off_sem, sems):
    off_copy = pltpu.make_async_copy(off_hbm, off_ref, off_sem)
    off_copy.start()
    heads = range(H_MID, H_MID + H_WIDE)
    copies = fetch((q_hbm, k_hbm, v_hbm, g_hbm), held, sems, heads)
    off_copy.wait()
    for head in range(H_MID + H_WIDE):
        off_out[head : head + 1, :] = jnp.full((1, TOK), off_ref[head], jnp.int32)
    row, column = iota2(16, TOK)
    rows = 0.0
    for at, head in enumerate(heads):
        kv, qg = pairs(copies, held, head, at)
        offset = off_ref[head]
        for start, block in ((2 * at, kv), (6 + 2 * at, qg)):
            mine = (row >= start) & (row < start + 2)
            rows += dot(one_hot(mine & (column == offset + R_WIDE * (row - start))), block)
    rows = rows.astype(BF16)
    for target in range(OUTERS):
        out_ref[target] = rows


def mid_pack_kernel(off_ref, q_hbm, k_hbm, v_hbm, g_hbm, out_ref, held, sems):
    copies = fetch((q_hbm, k_hbm, v_hbm, g_hbm), held, sems, range(H_MID))
    row, column = iota2(MID_ROWS, TOK)
    for head in range(H_MID):
        pick = one_hot(column - R_MID * row == off_ref[head : head + 1, :])
        kv, qg = pairs(copies, held, head, head)
        out_ref[head, 0:64, :] = dot(pick, kv).astype(BF16)
        out_ref[head, 64:128, :] = dot(pick, qg).astype(BF16)
    for head in range(H_MID, SLOTS):
        out_ref[head, 64:128, :] = jnp.zeros((64, 2 * HEAD_DIM), BF16)


def wide_pack_kernel(got_ref, packed, after, out, held, sems):
    rows = got_ref[...].reshape(OUTERS * 16, 2 * HEAD_DIM)
    row, column = iota2(64, OUTERS * 16)
    base = 16 * ((row % 32) // 2) + row % 2 + jnp.where(row < 32, 0, 6)
    copies = []
    for head in range(H_WIDE):
        held[head] = dot(one_hot(column == base + 2 * head), rows).astype(BF16)
        copy = pltpu.make_async_copy(
            held.at[head], out.at[H_MID + head, pl.ds(0, 64)], sems.at[head]
        )
        copy.start()
        copies.append(copy)
    for copy in copies:
        copy.wait()


def near_kernel(core, after, q_hbm, k_hbm, v_hbm, g_hbm, *rest):
    targets, (held, results, sems, out_sems) = rest[-7:-4], rest[-4:]

    @pl.when(lax.rem(lax.axis_index("outer"), 2) == core)
    def attend():
        copies = fetch((q_hbm, k_hbm, v_hbm, g_hbm), held, sems, range(H_NEAR), 0)
        sends = []
        for head in range(H_NEAR):
            for which in range(4):
                copies[head, which].wait()
            query, key, value, gradient = (held[which, head] for which in range(4))
            weights, score_gradients = attention_transposed(query, key, value, gradient)
            results[0, head] = dot_tn(score_gradients, key).astype(BF16)
            results[1, head] = dot(score_gradients, query).astype(BF16)
            results[2, head] = dot(weights, gradient).astype(BF16)
            for which, target in enumerate(targets):
                send = pltpu.make_async_copy(
                    results.at[which, head],
                    target.at[:, pl.ds(head * HEAD_DIM, HEAD_DIM)],
                    out_sems.at[which, head],
                )
                send.start()
                sends.append(send)
        for send in sends:
            send.wait()


def near_heads(core, after, arrays, previous=()):
    return pl.pallas_call(
        functools.partial(near_kernel, core),
        out_shape=[shape(TOK, HIDDEN)] * 3,
        in_specs=[spec(pl.ANY)] + [spec(pltpu.HBM)] * (4 + len(previous)),
        out_specs=[spec(pltpu.HBM)] * 3,
        scratch_shapes=[
            pltpu.VMEM((4, H_NEAR, TOK, HEAD_DIM), BF16),
            pltpu.VMEM((3, H_NEAR, TOK, HEAD_DIM), BF16),
            pltpu.SemaphoreType.DMA((4, H_NEAR)),
            pltpu.SemaphoreType.DMA((3, H_NEAR)),
        ],
        input_output_aliases={5 + which: which for which in range(len(previous))},
        cost_estimate=pl.CostEstimate(
            flops=10 * H_NEAR * TOK * TOK * HEAD_DIM,
            bytes_accessed=14 * TOK * NEAR_END,
            transcendentals=H_NEAR * TOK * TOK,
        ),
        compiler_params=params(16),
    )(after, *arrays, *previous)


def slot():
    return lax.div(lax.axis_index("inner"), HALVES)


def attend_wide(own_ref, other_ref, out_ref):
    wide_rows = SLOTS * 32
    kv = [ref[:, 0:32, :].reshape(wide_rows, 2 * HEAD_DIM) for ref in (own_ref, other_ref)]
    qg = [ref[:, 32:64, :].reshape(wide_rows, 2 * HEAD_DIM) for ref in (own_ref, other_ref)]
    row, column = iota2(16, wide_rows)
    source = 32 * (row // 2) + 2 * lax.axis_index("outer") + row % 2
    pick = one_hot(column == source)
    own_kv, own_qg = dot(pick, kv[0]).astype(BF16), dot(pick, qg[0]).astype(BF16)
    kv, qg = jnp.concatenate(kv, axis=0), jnp.concatenate(qg, axis=0)
    key, value = kv[:, :HEAD_DIM], kv[:, HEAD_DIM:]
    query, gradient = qg[:, :HEAD_DIM], qg[:, HEAD_DIM:]
    scores = dot_nt(key, query) * SCALE
    top = jnp.max(scores, axis=0, keepdims=True)
    exponent = jnp.exp(scores - top)
    inverse = 1.0 / jnp.sum(exponent, axis=0, keepdims=True)
    products = dot_nt(value, gradient)
    row_dots = jnp.sum(exponent * inverse * products, axis=0, keepdims=True)
    own_key, own_value = own_kv[:, :HEAD_DIM], own_kv[:, HEAD_DIM:]
    own_query, own_gradient = own_qg[:, :HEAD_DIM], own_qg[:, HEAD_DIM:]
    weights = jnp.exp(dot_nt(own_key, query) * SCALE - top) * inverse
    score_gradients = weights * (dot_nt(own_value, gradient) - row_dots) * SCALE
    dk = dot(score_gradients.astype(BF16), query).astype(BF16)
    dv = dot(weights.astype(BF16), gradient).astype(BF16)
    scores = dot_nt(own_query, key) * SCALE
    exponent = jnp.exp(scores - jnp.max(scores, axis=1, keepdims=True))
    weights = exponent * (1.0 / jnp.sum(exponent, axis=1, keepdims=True))
    products = dot_nt(own_gradient, value)
    row_dots = jnp.sum(weights * products, axis=1, keepdims=True)
    score_gradients = weights * (products - row_dots) * SCALE
    dq = dot(score_gradients.astype(BF16), key).astype(BF16)
    row, column = iota2(SLOTS * 16, 16)
    member, place = row // 16, row % 16
    spread = 0.0
    for which, rows in enumerate((dq, dk, dv)):
        mine = (place >= 2 * which) & (place < 2 * which + 2)
        spread += dot(one_hot(mine & (column == 2 * member + place - 2 * which)), rows)
    out_ref[...] = spread.astype(BF16).reshape(SLOTS, 16, HEAD_DIM)


def work_kernel(own_ref, other_ref, dq_ref, own_out, wide_out, other_out, dkv_ref):
    @pl.when(slot() >= H_MID)
    def wide():
        attend_wide(own_ref, other_ref, wide_out)

    @pl.when(slot() < H_MID)
    def attend():
        kv = [ref[:, 0:64, :].reshape(HALF_KEYS, 2 * HEAD_DIM) for ref in (own_ref, other_ref)]
        kv = jnp.concatenate(kv, axis=0)
        key, value = kv[:, :HEAD_DIM], kv[:, HEAD_DIM:]
        qg = own_ref[:, 64:128, :].reshape(HALF_KEYS, 2 * HEAD_DIM)
        for start in range(0, HALF_KEYS, QUERY_BLOCK):
            query = qg[start : start + QUERY_BLOCK, :HEAD_DIM]
            gradient = qg[start : start + QUERY_BLOCK, HEAD_DIM:]
            weights, score_gradients = attention_transposed(query, key, value, gradient)
            dk, dv = dot(score_gradients, query), dot(weights, gradient)
            if start == 0:
                dkv_ref[:, :HEAD_DIM] = dk
                dkv_ref[:, HEAD_DIM:] = dv
            else:
                dkv_ref[:, :HEAD_DIM] += dk
                dkv_ref[:, HEAD_DIM:] += dv
            dq = dot_tn(key, score_gradients).T.astype(BF16)
            blocks = slice(start // MID_ROWS, (start + QUERY_BLOCK) // MID_ROWS)
            dq_ref[blocks] = dq.reshape(QUERY_BLOCK // MID_ROWS, MID_ROWS, HEAD_DIM)
        own_out[...] = dkv_ref[:HALF_KEYS, :]
        other = dkv_ref[HALF_KEYS:, :].astype(BF16)
        other_out[...] = other.reshape(SLOTS, MID_ROWS, 2 * HEAD_DIM)


def return_kernel(dq_ref, own_ref, wide_ref, back_ref, after, out_ref):
    @pl.when(slot() < H_MID)
    def add_halves():
        out_ref[:, 0:64, :] = dq_ref[...]
        back = back_ref[...].reshape(HALF_KEYS, 2 * HEAD_DIM).astype(F32)
        dkv = (own_ref[...] + back).astype(BF16)
        out_ref[:, 64:128, :] = dkv[:, :HEAD_DIM].reshape(SLOTS, MID_ROWS, HEAD_DIM)
        out_ref[:, 128:192, :] = dkv[:, HEAD_DIM:].reshape(SLOTS, MID_ROWS, HEAD_DIM)

    @pl.when(slot() >= H_MID)
    def wide():
        out_ref[:, 0:16, :] = wide_ref[...]


def assemble_kernel(off_ref, got_ref, nq, nk, nv, dq_hbm, dk_hbm, dv_hbm, held, sems):
    copies = []

    def send(which, head, block):
        held[which, head] = block.astype(BF16)
        target = (dq_hbm, dk_hbm, dv_hbm)[which]
        copy = pltpu.make_async_copy(
            held.at[which, head],
            target.at[:, pl.ds(NEAR_END + head * HEAD_DIM, HEAD_DIM)],
            sems.at[which, head],
        )
        copy.start()
        copies.append(copy)

    row, unused = iota2(TOK, HEAD_DIM)
    for head in range(H_MID, H_MID + H_WIDE):
        offset = off_ref[head : head + 1, :HEAD_DIM]
        rows = got_ref[head, 0:16, :].astype(F32)
        first, second = row == offset, row == offset + R_WIDE
        for which in range(3):
            spread = jnp.where(first, rows[2 * which : 2 * which + 1], 0.0)
            send(which, head, jnp.where(second, rows[2 * which + 1 : 2 * which + 2], spread))
    row, column = iota2(TOK, MID_ROWS)
    for head in range(H_MID):
        place = one_hot(row - R_MID * column == off_ref[head : head + 1, :1])
        for which in range(3):
            send(which, head, dot(place, got_ref[head, 64 * which : 64 * which + 64, :]))
    for copy in copies:
        copy.wait()


def spec(space):
    return pl.BlockSpec(memory_space=space)


def in_hbm(array):
    return pltpu.with_memory_space_constraint(array, pltpu.HBM)


def params(mebibytes):
    return pltpu.CompilerParams(vmem_limit_bytes=mebibytes * 1024 * 1024)


def shape(*sizes, kind=BF16):
    return jax.ShapeDtypeStruct(sizes, kind)


def body(queries, key_rows, values, out_grads, offsets):
    arrays = [in_hbm(array) for array in (queries, key_rows, values, out_grads)]
    heads = H_MID + H_WIDE
    wide_send, offset_rows = pl.pallas_call(
        wide_kernel,
        out_shape=[shape(OUTERS, 16, 256), shape(heads, TOK, kind=jnp.int32)],
        in_specs=[spec(pltpu.HBM)] * 5,
        out_specs=[spec(pltpu.VMEM)] * 2,
        scratch_shapes=[
            pltpu.SMEM((heads,), jnp.int32),
            pltpu.VMEM((4, H_WIDE, TOK, HEAD_DIM), BF16),
            pltpu.SemaphoreType.DMA,
            pltpu.SemaphoreType.DMA((4, H_WIDE)),
        ],
        compiler_params=params(8),
    )(in_hbm(offsets), *arrays)
    wide_got = lax.all_to_all(wide_send, "outer", 0, 0)
    packed = pl.pallas_call(
        mid_pack_kernel,
        out_shape=shape(SLOTS, 128, 256),
        in_specs=[spec(pltpu.VMEM)] + [spec(pltpu.HBM)] * 4,
        out_specs=spec(pltpu.VMEM),
        scratch_shapes=[
            pltpu.VMEM((4, H_MID, TOK, HEAD_DIM), BF16),
            pltpu.SemaphoreType.DMA((4, H_MID)),
        ],
        cost_estimate=pl.CostEstimate(
            flops=8 * H_MID * MID_ROWS * TOK * HEAD_DIM,
            bytes_accessed=8 * H_MID * TOK * HEAD_DIM,
            transcendentals=0,
        ),
        compiler_params=params(8),
    )(offset_rows, *arrays)
    near = near_heads(0, wide_got, arrays)
    packed = pl.pallas_call(
        wide_pack_kernel,
        out_shape=shape(SLOTS, 128, 256),
        in_specs=[spec(pltpu.VMEM), spec(pl.ANY), spec(pl.ANY)],
        out_specs=spec(pl.ANY),
        scratch_shapes=[
            pltpu.VMEM((H_WIDE, 64, 256), BF16),
            pltpu.SemaphoreType.DMA((H_WIDE,)),
        ],
        input_output_aliases={1: 0},
        compiler_params=params(8),
    )(wide_got, packed, in_hbm(near[0]))
    own = lax.all_to_all(packed, "inner", 0, 0, axis_index_groups=ALONG_Z)
    other = lax.ppermute(own[:, 0:64, :], "inner", ACROSS_Y)
    dq, own_sums, wide_rows, other_sums = pl.pallas_call(
        work_kernel,
        out_shape=[
            shape(SLOTS, MID_ROWS, HEAD_DIM),
            shape(HALF_KEYS, 256, kind=F32),
            shape(SLOTS, 16, HEAD_DIM),
            shape(SLOTS, MID_ROWS, 256),
        ],
        in_specs=[spec(pltpu.VMEM)] * 2,
        out_specs=[spec(pltpu.VMEM)] * 4,
        scratch_shapes=[pltpu.VMEM((HALVES * HALF_KEYS, 256), F32)],
        compiler_params=params(32),
    )(own, other)
    back = lax.ppermute(other_sums, "inner", ACROSS_Y)
    near = near_heads(1, other_sums, arrays, near)
    results = pl.pallas_call(
        return_kernel,
        out_shape=shape(SLOTS, 192, HEAD_DIM),
        in_specs=[spec(pltpu.VMEM)] * 4 + [spec(pl.ANY)],
        out_specs=spec(pltpu.VMEM),
        compiler_params=params(16),
    )(dq, own_sums, wide_rows, back, in_hbm(near[0]))
    returned = lax.all_to_all(results, "inner", 0, 0, axis_index_groups=ALONG_Z)
    return tuple(
        pl.pallas_call(
            assemble_kernel,
            out_shape=[shape(TOK, HIDDEN)] * 3,
            in_specs=[spec(pltpu.VMEM)] * 2 + [spec(pltpu.HBM)] * 3,
            out_specs=[spec(pltpu.HBM)] * 3,
            scratch_shapes=[
                pltpu.VMEM((3, heads, TOK, HEAD_DIM), BF16),
                pltpu.SemaphoreType.DMA((3, heads)),
            ],
            input_output_aliases={2: 0, 3: 1, 4: 2},
            compiler_params=params(16),
        )(offset_rows, returned, *near)
    )


def solution(mesh):
    rows = P(("outer", "inner"), None)
    return jax.shard_map(
        body,
        mesh=mesh,
        in_specs=(rows, rows, rows, rows, P()),
        out_specs=(rows, rows, rows),
        check_vma=False,
    )
```

```python
import functools
import math

import jax
import jax.numpy as jnp
from jax import lax
from jax.experimental import pallas as pl
from jax.experimental.pallas import tpu as pltpu
from jax.sharding import PartitionSpec as P

HEAD_DIM = 128
H_NEAR = 4
H_MID = 5
H_WIDE = 3
R_MID = 4
R_WIDE = 128
TOK = 256
NEAR_END = H_NEAR * HEAD_DIM
MID_END = NEAR_END + H_MID * HEAD_DIM
HIDDEN = MID_END + H_WIDE * HEAD_DIM
OUTERS = 16
MID_ROWS = TOK // R_MID
SLOTS = 8
HALVES = 2
HALF_KEYS = SLOTS * MID_ROWS
QUERY_BLOCK = 256
ALONG_Z = [[HALVES * z + half for z in range(SLOTS)] for half in range(HALVES)]
ACROSS_Y = [(member, member ^ 1) for member in range(HALVES * SLOTS)]
SCALE = 1.0 / math.sqrt(HEAD_DIM)
EXP2_SCALE = SCALE * math.log2(math.e)
BF16 = jnp.bfloat16
F32 = jnp.float32


def dot(a, b):
    return lax.dot_general(a, b, (((1,), (0,)), ((), ())), preferred_element_type=F32)


def dot_nt(a, b):
    return lax.dot_general(a, b, (((1,), (1,)), ((), ())), preferred_element_type=F32)


def dot_tn(a, b):
    return lax.dot_general(a, b, (((0,), (0,)), ((), ())), preferred_element_type=F32)


def iota2(rows, columns):
    shape = (rows, columns)
    return (
        lax.broadcasted_iota(jnp.int32, shape, 0),
        lax.broadcasted_iota(jnp.int32, shape, 1),
    )


def one_hot(condition):
    return jnp.where(condition, 1.0, 0.0).astype(BF16)


def scaled_weights(parts, query, gradient):
    scores = [dot_nt(key, query) for key, unused in parts]
    top = functools.reduce(jnp.maximum, [jnp.max(s, axis=0, keepdims=True) for s in scores])
    exponents = [jnp.exp2((s - top) * EXP2_SCALE) for s in scores]
    inverse = 1.0 / sum(jnp.sum(e, axis=0, keepdims=True) for e in exponents)
    products = [dot_nt(value, gradient) for unused, value in parts]
    row_dots = inverse * sum(
        jnp.sum(e * p, axis=0, keepdims=True) for e, p in zip(exponents, products)
    )
    weights = exponents[0] * inverse
    score_gradients = weights * (products[0] - row_dots) * SCALE
    return weights.astype(BF16), score_gradients.astype(BF16)


def attention_transposed(query, key, value, gradient):
    return scaled_weights([(key, value)], query, gradient)


def fetch(sources, held, sems, heads, first=NEAR_END):
    copies = {}
    for at, head in enumerate(heads):
        for which, source in enumerate(sources):
            copies[head, which] = pltpu.make_async_copy(
                source.at[:, pl.ds(first + head * HEAD_DIM, HEAD_DIM)],
                held.at[which, at],
                sems.at[which, at],
            )
            copies[head, which].start()
    return copies


def pairs(copies, held, head, at):
    for which in range(4):
        copies[head, which].wait()
    kv = jnp.concatenate([held[1, at], held[2, at]], axis=1)
    qg = jnp.concatenate([held[0, at], held[3, at]], axis=1)
    return kv, qg


def wide_kernel(off_hbm, q_hbm, k_hbm, v_hbm, g_hbm, out_ref, off_out, off_ref, held, off_sem, sems):
    off_copy = pltpu.make_async_copy(off_hbm, off_ref, off_sem)
    off_copy.start()
    heads = range(H_MID, H_MID + H_WIDE)
    copies = fetch((q_hbm, k_hbm, v_hbm, g_hbm), held, sems, heads)
    off_copy.wait()
    for head in range(H_MID + H_WIDE):
        off_out[head : head + 1, :] = jnp.full((1, TOK), off_ref[head], jnp.int32)
    row, column = iota2(16, TOK)
    rows = 0.0
    for at, head in enumerate(heads):
        kv, qg = pairs(copies, held, head, at)
        offset = off_ref[head]
        for start, block in ((2 * at, kv), (6 + 2 * at, qg)):
            mine = (row >= start) & (row < start + 2)
            rows += dot(one_hot(mine & (column == offset + R_WIDE * (row - start))), block)
    rows = rows.astype(BF16)
    for target in range(OUTERS):
        out_ref[target] = rows


def mid_pack_kernel(off_ref, q_hbm, k_hbm, v_hbm, g_hbm, out_ref, held, sems):
    copies = fetch((q_hbm, k_hbm, v_hbm, g_hbm), held, sems, range(H_MID))
    row, column = iota2(MID_ROWS, TOK)
    for head in range(H_MID):
        pick = one_hot(column - R_MID * row == off_ref[head : head + 1, :])
        kv, qg = pairs(copies, held, head, head)
        out_ref[head, 0:64, :] = dot(pick, kv).astype(BF16)
        out_ref[head, 64:128, :] = dot(pick, qg).astype(BF16)
    for head in range(H_MID, SLOTS):
        out_ref[head, 64:128, :] = jnp.zeros((64, 2 * HEAD_DIM), BF16)


def wide_pack_kernel(got_ref, packed, after, out, held, sems):
    rows = got_ref[...].reshape(OUTERS * 16, 2 * HEAD_DIM)
    row, column = iota2(64, OUTERS * 16)
    base = 16 * ((row % 32) // 2) + row % 2 + jnp.where(row < 32, 0, 6)
    copies = []
    for head in range(H_WIDE):
        held[head] = dot(one_hot(column == base + 2 * head), rows).astype(BF16)
        copy = pltpu.make_async_copy(
            held.at[head], out.at[H_MID + head, pl.ds(0, 64)], sems.at[head]
        )
        copy.start()
        copies.append(copy)
    for copy in copies:
        copy.wait()


def near_kernel(core, after, q_hbm, k_hbm, v_hbm, g_hbm, *rest):
    targets, (held, results, sems, out_sems) = rest[-7:-4], rest[-4:]

    @pl.when(lax.rem(lax.axis_index("outer"), 2) == core)
    def attend():
        copies = fetch((q_hbm, k_hbm, v_hbm, g_hbm), held, sems, range(H_NEAR), 0)
        sends = []
        for head in range(H_NEAR):
            for which in range(4):
                copies[head, which].wait()
            query, key, value, gradient = (held[which, head] for which in range(4))
            weights, score_gradients = attention_transposed(query, key, value, gradient)
            results[0, head] = dot_tn(score_gradients, key).astype(BF16)
            results[1, head] = dot(score_gradients, query).astype(BF16)
            results[2, head] = dot(weights, gradient).astype(BF16)
            for which, target in enumerate(targets):
                send = pltpu.make_async_copy(
                    results.at[which, head],
                    target.at[:, pl.ds(head * HEAD_DIM, HEAD_DIM)],
                    out_sems.at[which, head],
                )
                send.start()
                sends.append(send)
        for send in sends:
            send.wait()


def near_heads(core, after, arrays, previous=()):
    return pl.pallas_call(
        functools.partial(near_kernel, core),
        out_shape=[shape(TOK, HIDDEN)] * 3,
        in_specs=[spec(pl.ANY)] + [spec(pltpu.HBM)] * (4 + len(previous)),
        out_specs=[spec(pltpu.HBM)] * 3,
        scratch_shapes=[
            pltpu.VMEM((4, H_NEAR, TOK, HEAD_DIM), BF16),
            pltpu.VMEM((3, H_NEAR, TOK, HEAD_DIM), BF16),
            pltpu.SemaphoreType.DMA((4, H_NEAR)),
            pltpu.SemaphoreType.DMA((3, H_NEAR)),
        ],
        input_output_aliases={5 + which: which for which in range(len(previous))},
        cost_estimate=pl.CostEstimate(
            flops=10 * H_NEAR * TOK * TOK * HEAD_DIM,
            bytes_accessed=14 * TOK * NEAR_END,
            transcendentals=H_NEAR * TOK * TOK,
        ),
        compiler_params=params(16),
    )(after, *arrays, *previous)


def slot():
    return lax.div(lax.axis_index("inner"), HALVES)


def attend_wide(own_ref, other_ref, out_ref):
    wide_rows = SLOTS * 32
    kv = [ref[:, 0:32, :].reshape(wide_rows, 2 * HEAD_DIM) for ref in (own_ref, other_ref)]
    qg = [ref[:, 32:64, :].reshape(wide_rows, 2 * HEAD_DIM) for ref in (own_ref, other_ref)]
    row, column = iota2(16, wide_rows)
    source = 32 * (row // 2) + 2 * lax.axis_index("outer") + row % 2
    pick = one_hot(column == source)
    own_kv, own_qg = dot(pick, kv[0]).astype(BF16), dot(pick, qg[0]).astype(BF16)
    kv, qg = jnp.concatenate(kv, axis=0), jnp.concatenate(qg, axis=0)
    key, value = kv[:, :HEAD_DIM], kv[:, HEAD_DIM:]
    query, gradient = qg[:, :HEAD_DIM], qg[:, HEAD_DIM:]
    scores = dot_nt(key, query) * SCALE
    top = jnp.max(scores, axis=0, keepdims=True)
    exponent = jnp.exp(scores - top)
    inverse = 1.0 / jnp.sum(exponent, axis=0, keepdims=True)
    products = dot_nt(value, gradient)
    row_dots = jnp.sum(exponent * inverse * products, axis=0, keepdims=True)
    own_key, own_value = own_kv[:, :HEAD_DIM], own_kv[:, HEAD_DIM:]
    own_query, own_gradient = own_qg[:, :HEAD_DIM], own_qg[:, HEAD_DIM:]
    weights = jnp.exp(dot_nt(own_key, query) * SCALE - top) * inverse
    score_gradients = weights * (dot_nt(own_value, gradient) - row_dots) * SCALE
    dk = dot(score_gradients.astype(BF16), query).astype(BF16)
    dv = dot(weights.astype(BF16), gradient).astype(BF16)
    scores = dot_nt(own_query, key) * SCALE
    exponent = jnp.exp(scores - jnp.max(scores, axis=1, keepdims=True))
    weights = exponent * (1.0 / jnp.sum(exponent, axis=1, keepdims=True))
    products = dot_nt(own_gradient, value)
    row_dots = jnp.sum(weights * products, axis=1, keepdims=True)
    score_gradients = weights * (products - row_dots) * SCALE
    dq = dot(score_gradients.astype(BF16), key).astype(BF16)
    row, column = iota2(SLOTS * 16, 16)
    member, place = row // 16, row % 16
    spread = 0.0
    for which, rows in enumerate((dq, dk, dv)):
        mine = (place >= 2 * which) & (place < 2 * which + 2)
        spread += dot(one_hot(mine & (column == 2 * member + place - 2 * which)), rows)
    out_ref[...] = spread.astype(BF16).reshape(SLOTS, 16, HEAD_DIM)


def halves(ref, rows):
    block = ref[:, rows, :].reshape(HALF_KEYS, 2 * HEAD_DIM)
    return block[:, :HEAD_DIM], block[:, HEAD_DIM:]


def own_work_kernel(own_ref, other_ref, after, dq_ref, dkv_ref, wide_out):
    @pl.when(slot() >= H_MID)
    def wide():
        attend_wide(own_ref, other_ref, wide_out)

    @pl.when(slot() < H_MID)
    def attend():
        own_key, own_value = halves(own_ref, slice(0, 64))
        other_key, other_value = halves(other_ref, slice(0, 64))
        key = jnp.concatenate([own_key, other_key], axis=0)
        value = jnp.concatenate([own_value, other_value], axis=0)
        queries, gradients = halves(own_ref, slice(64, 128))
        for start in range(0, HALF_KEYS, QUERY_BLOCK):
            query = queries[start : start + QUERY_BLOCK]
            gradient = gradients[start : start + QUERY_BLOCK]
            weights, score_gradients = attention_transposed(query, key, value, gradient)
            dk = dot(score_gradients[:HALF_KEYS], query)
            dv = dot(weights[:HALF_KEYS], gradient)
            if start == 0:
                dkv_ref[:, :HEAD_DIM] = dk
                dkv_ref[:, HEAD_DIM:] = dv
            else:
                dkv_ref[:, :HEAD_DIM] += dk
                dkv_ref[:, HEAD_DIM:] += dv
            dq = dot_tn(key, score_gradients).T.astype(BF16)
            blocks = slice(start // MID_ROWS, (start + QUERY_BLOCK) // MID_ROWS)
            dq_ref[blocks] = dq.reshape(QUERY_BLOCK // MID_ROWS, MID_ROWS, HEAD_DIM)


def other_work_kernel(own_ref, other_ref, query_ref, dq_ref, dkv_ref, wide_ref, out_ref, sum_ref):
    @pl.when(slot() < H_MID)
    def attend():
        parts = [halves(own_ref, slice(0, 64)), halves(other_ref, slice(0, 64))]
        queries, gradients = halves(query_ref, slice(0, 64))
        for start in range(0, HALF_KEYS, QUERY_BLOCK):
            query = queries[start : start + QUERY_BLOCK]
            gradient = gradients[start : start + QUERY_BLOCK]
            weights, score_gradients = scaled_weights(parts, query, gradient)
            before = dkv_ref if start == 0 else sum_ref
            sum_ref[:, :HEAD_DIM] = before[:, :HEAD_DIM] + dot(score_gradients, query)
            sum_ref[:, HEAD_DIM:] = before[:, HEAD_DIM:] + dot(weights, gradient)
        out_ref[:, 0:64, :] = dq_ref[...]
        dkv = sum_ref[...].astype(BF16)
        out_ref[:, 64:128, :] = dkv[:, :HEAD_DIM].reshape(SLOTS, MID_ROWS, HEAD_DIM)
        out_ref[:, 128:192, :] = dkv[:, HEAD_DIM:].reshape(SLOTS, MID_ROWS, HEAD_DIM)

    @pl.when(slot() >= H_MID)
    def wide():
        out_ref[:, 0:16, :] = wide_ref[...]


def assemble_kernel(off_ref, got_ref, nq, nk, nv, dq_hbm, dk_hbm, dv_hbm, held, sems):
    copies = []

    def send(which, head, block):
        held[which, head] = block.astype(BF16)
        target = (dq_hbm, dk_hbm, dv_hbm)[which]
        copy = pltpu.make_async_copy(
            held.at[which, head],
            target.at[:, pl.ds(NEAR_END + head * HEAD_DIM, HEAD_DIM)],
            sems.at[which, head],
        )
        copy.start()
        copies.append(copy)

    row, unused = iota2(TOK, HEAD_DIM)
    for head in range(H_MID, H_MID + H_WIDE):
        offset = off_ref[head : head + 1, :HEAD_DIM]
        rows = got_ref[head, 0:16, :].astype(F32)
        first, second = row == offset, row == offset + R_WIDE
        for which in range(3):
            spread = jnp.where(first, rows[2 * which : 2 * which + 1], 0.0)
            send(which, head, jnp.where(second, rows[2 * which + 1 : 2 * which + 2], spread))
    row, column = iota2(TOK, MID_ROWS)
    for head in range(H_MID):
        place = one_hot(row - R_MID * column == off_ref[head : head + 1, :1])
        for which in range(3):
            send(which, head, dot(place, got_ref[head, 64 * which : 64 * which + 64, :]))
    for copy in copies:
        copy.wait()


def spec(space):
    return pl.BlockSpec(memory_space=space)


def in_hbm(array):
    return pltpu.with_memory_space_constraint(array, pltpu.HBM)


def params(mebibytes):
    return pltpu.CompilerParams(vmem_limit_bytes=mebibytes * 1024 * 1024)


def shape(*sizes, kind=BF16):
    return jax.ShapeDtypeStruct(sizes, kind)


def work_cost(products):
    return pl.CostEstimate(
        flops=products * 4 * HALF_KEYS * HALF_KEYS * HEAD_DIM,
        bytes_accessed=0,
        transcendentals=2 * HALF_KEYS * HALF_KEYS,
    )


def body(queries, key_rows, values, out_grads, offsets):
    arrays = [in_hbm(array) for array in (queries, key_rows, values, out_grads)]
    heads = H_MID + H_WIDE
    wide_send, offset_rows = pl.pallas_call(
        wide_kernel,
        out_shape=[shape(OUTERS, 16, 256), shape(heads, TOK, kind=jnp.int32)],
        in_specs=[spec(pltpu.HBM)] * 5,
        out_specs=[spec(pltpu.VMEM)] * 2,
        scratch_shapes=[
            pltpu.SMEM((heads,), jnp.int32),
            pltpu.VMEM((4, H_WIDE, TOK, HEAD_DIM), BF16),
            pltpu.SemaphoreType.DMA,
            pltpu.SemaphoreType.DMA((4, H_WIDE)),
        ],
        compiler_params=params(8),
    )(in_hbm(offsets), *arrays)
    wide_got = lax.all_to_all(wide_send, "outer", 0, 0)
    packed = pl.pallas_call(
        mid_pack_kernel,
        out_shape=shape(SLOTS, 128, 256),
        in_specs=[spec(pltpu.VMEM)] + [spec(pltpu.HBM)] * 4,
        out_specs=spec(pltpu.VMEM),
        scratch_shapes=[
            pltpu.VMEM((4, H_MID, TOK, HEAD_DIM), BF16),
            pltpu.SemaphoreType.DMA((4, H_MID)),
        ],
        cost_estimate=pl.CostEstimate(
            flops=8 * H_MID * MID_ROWS * TOK * HEAD_DIM,
            bytes_accessed=8 * H_MID * TOK * HEAD_DIM,
            transcendentals=0,
        ),
        compiler_params=params(8),
    )(offset_rows, *arrays)
    near = near_heads(0, wide_got, arrays)
    packed = pl.pallas_call(
        wide_pack_kernel,
        out_shape=shape(SLOTS, 128, 256),
        in_specs=[spec(pltpu.VMEM), spec(pl.ANY), spec(pl.ANY)],
        out_specs=spec(pl.ANY),
        scratch_shapes=[
            pltpu.VMEM((H_WIDE, 64, 256), BF16),
            pltpu.SemaphoreType.DMA((H_WIDE,)),
        ],
        input_output_aliases={1: 0},
        compiler_params=params(8),
    )(wide_got, packed, in_hbm(near[0]))
    own = lax.all_to_all(packed, "inner", 0, 0, axis_index_groups=ALONG_Z)
    other = lax.ppermute(own[:, 0:64, :], "inner", ACROSS_Y)
    other_queries = lax.ppermute(own[:, 64:128, :], "inner", ACROSS_Y)
    near = near_heads(1, own, arrays, near)
    dq, own_sums, wide_rows = pl.pallas_call(
        own_work_kernel,
        out_shape=[
            shape(SLOTS, MID_ROWS, HEAD_DIM),
            shape(HALF_KEYS, 256, kind=F32),
            shape(SLOTS, 16, HEAD_DIM),
        ],
        in_specs=[spec(pltpu.VMEM)] * 2 + [spec(pl.ANY)],
        out_specs=[spec(pltpu.VMEM)] * 3,
        cost_estimate=work_cost(5),
        compiler_params=params(24),
    )(own, other, in_hbm(near[0]))
    results = pl.pallas_call(
        other_work_kernel,
        out_shape=shape(SLOTS, 192, HEAD_DIM),
        in_specs=[spec(pltpu.VMEM)] * 6,
        out_specs=spec(pltpu.VMEM),
        scratch_shapes=[pltpu.VMEM((HALF_KEYS, 256), F32)],
        cost_estimate=work_cost(4),
        compiler_params=params(24),
    )(own, other, other_queries, dq, own_sums, wide_rows)
    returned = lax.all_to_all(results, "inner", 0, 0, axis_index_groups=ALONG_Z)
    return tuple(
        pl.pallas_call(
            assemble_kernel,
            out_shape=[shape(TOK, HIDDEN)] * 3,
            in_specs=[spec(pltpu.VMEM)] * 2 + [spec(pltpu.HBM)] * 3,
            out_specs=[spec(pltpu.HBM)] * 3,
            scratch_shapes=[
                pltpu.VMEM((3, heads, TOK, HEAD_DIM), BF16),
                pltpu.SemaphoreType.DMA((3, heads)),
            ],
            input_output_aliases={2: 0, 3: 1, 4: 2},
            compiler_params=params(16),
        )(offset_rows, returned, *near)
    )


def solution(mesh):
    rows = P(("outer", "inner"), None)
    return jax.shard_map(
        body,
        mesh=mesh,
        in_specs=(rows, rows, rows, rows, P()),
        out_specs=(rows, rows, rows),
        check_vma=False,
    )
```

```python
import functools
import math

import jax
import jax.numpy as jnp
from jax import lax
from jax.experimental import pallas as pl
from jax.experimental.pallas import tpu as pltpu
from jax.sharding import PartitionSpec as P

HEAD_DIM = 128
H_NEAR = 4
H_MID = 5
H_WIDE = 3
R_MID = 4
R_WIDE = 128
TOK = 256
NEAR_END = H_NEAR * HEAD_DIM
MID_END = NEAR_END + H_MID * HEAD_DIM
HIDDEN = MID_END + H_WIDE * HEAD_DIM
OUTERS = 16
MID_ROWS = TOK // R_MID
SLOTS = 8
HALVES = 2
HALF_KEYS = SLOTS * MID_ROWS
QUERY_BLOCK = 256
ALONG_Z = [[HALVES * z + half for z in range(SLOTS)] for half in range(HALVES)]
ACROSS_Y = [(member, member ^ 1) for member in range(HALVES * SLOTS)]
SCALE = 1.0 / math.sqrt(HEAD_DIM)
EXP2_SCALE = SCALE * math.log2(math.e)
BF16 = jnp.bfloat16
F32 = jnp.float32


def dot(a, b):
    return lax.dot_general(a, b, (((1,), (0,)), ((), ())), preferred_element_type=F32)


def dot_nt(a, b):
    return lax.dot_general(a, b, (((1,), (1,)), ((), ())), preferred_element_type=F32)


def dot_tn(a, b):
    return lax.dot_general(a, b, (((0,), (0,)), ((), ())), preferred_element_type=F32)


def iota2(rows, columns):
    shape = (rows, columns)
    return (
        lax.broadcasted_iota(jnp.int32, shape, 0),
        lax.broadcasted_iota(jnp.int32, shape, 1),
    )


def one_hot(condition):
    return jnp.where(condition, 1.0, 0.0).astype(BF16)


def scaled_weights(parts, query, gradient):
    scores = [dot_nt(key, query) for key, unused in parts]
    top = functools.reduce(jnp.maximum, [jnp.max(s, axis=0, keepdims=True) for s in scores])
    exponents = [jnp.exp2((s - top) * EXP2_SCALE) for s in scores]
    inverse = 1.0 / sum(jnp.sum(e, axis=0, keepdims=True) for e in exponents)
    products = [dot_nt(value, gradient) for unused, value in parts]
    row_dots = inverse * sum(
        jnp.sum(e * p, axis=0, keepdims=True) for e, p in zip(exponents, products)
    )
    weights = exponents[0] * inverse
    score_gradients = weights * (products[0] - row_dots) * SCALE
    return weights.astype(BF16), score_gradients.astype(BF16)


def attention_transposed(query, key, value, gradient):
    return scaled_weights([(key, value)], query, gradient)


def fetch(sources, held, sems, heads, first=NEAR_END):
    copies = {}
    for at, head in enumerate(heads):
        for which, source in enumerate(sources):
            copies[head, which] = pltpu.make_async_copy(
                source.at[:, pl.ds(first + head * HEAD_DIM, HEAD_DIM)],
                held.at[which, at],
                sems.at[which, at],
            )
            copies[head, which].start()
    return copies


def pairs(copies, held, head, at):
    for which in range(4):
        copies[head, which].wait()
    kv = jnp.concatenate([held[1, at], held[2, at]], axis=1)
    qg = jnp.concatenate([held[0, at], held[3, at]], axis=1)
    return kv, qg


def wide_kernel(off_hbm, q_hbm, k_hbm, v_hbm, g_hbm, out_ref, off_out, off_ref, held, off_sem, sems):
    off_copy = pltpu.make_async_copy(off_hbm, off_ref, off_sem)
    off_copy.start()
    heads = range(H_MID, H_MID + H_WIDE)
    copies = fetch((q_hbm, k_hbm, v_hbm, g_hbm), held, sems, heads)
    off_copy.wait()
    for head in range(H_MID + H_WIDE):
        off_out[head : head + 1, :] = jnp.full((1, TOK), off_ref[head], jnp.int32)
    row, unused = iota2(16, HEAD_DIM)
    row_pair, unused = iota2(16, 2 * HEAD_DIM)
    rows = jnp.zeros((16, 2 * HEAD_DIM), F32)
    for at, head in enumerate(heads):
        offset = off_ref[head]
        base, place = lax.div(offset, 16) * 16, lax.rem(offset, 16)
        for which in range(4):
            copies[head, which].wait()
        for again in range(2):
            tile = pl.ds(pl.multiple_of(base + again * R_WIDE, 16), 16)
            picked = [
                jnp.sum(
                    jnp.where(row == place, held[which, at, tile, :].astype(F32), 0.0),
                    axis=0,
                    keepdims=True,
                )
                for which in range(4)
            ]
            kv = jnp.concatenate([picked[1], picked[2]], axis=1)
            qg = jnp.concatenate([picked[0], picked[3]], axis=1)
            rows = jnp.where(row_pair == 2 * at + again, kv, rows)
            rows = jnp.where(row_pair == 6 + 2 * at + again, qg, rows)
    rows = rows.astype(BF16)
    for target in range(OUTERS):
        out_ref[target] = rows


def mid_pack_kernel(off_ref, q_hbm, k_hbm, v_hbm, g_hbm, out_ref, held, sems):
    copies = fetch((q_hbm, k_hbm, v_hbm, g_hbm), held, sems, range(H_MID))
    row, column = iota2(MID_ROWS, TOK)
    for head in range(H_MID):
        pick = one_hot(column - R_MID * row == off_ref[head : head + 1, :])
        kv, qg = pairs(copies, held, head, head)
        out_ref[head, 0:64, :] = dot(pick, kv).astype(BF16)
        out_ref[head, 64:128, :] = dot(pick, qg).astype(BF16)
    for head in range(H_MID, SLOTS):
        out_ref[head, 64:128, :] = jnp.zeros((64, 2 * HEAD_DIM), BF16)


def wide_pack_kernel(got_ref, packed, after, out_ref):
    rows = got_ref[...].reshape(OUTERS * 16, 2 * HEAD_DIM)
    row, column = iota2(64, OUTERS * 16)
    base = 16 * ((row % 32) // 2) + row % 2 + jnp.where(row < 32, 0, 6)
    for head in range(H_WIDE):
        picked = dot(one_hot(column == base + 2 * head), rows)
        out_ref[H_MID + head, 0:64, :] = picked.astype(BF16)


def near_kernel(core, after, q_hbm, k_hbm, v_hbm, g_hbm, *rest):
    targets, (held, results, sems, out_sems) = rest[-7:-4], rest[-4:]

    @pl.when(lax.rem(lax.axis_index("outer"), 2) == core)
    def attend():
        copies = fetch((q_hbm, k_hbm, v_hbm, g_hbm), held, sems, range(H_NEAR), 0)
        sends = []
        for head in range(H_NEAR):
            for which in range(4):
                copies[head, which].wait()
            query, key, value, gradient = (held[which, head] for which in range(4))
            weights, score_gradients = attention_transposed(query, key, value, gradient)
            results[0, head] = dot_tn(score_gradients, key).astype(BF16)
            results[1, head] = dot(score_gradients, query).astype(BF16)
            results[2, head] = dot(weights, gradient).astype(BF16)
            for which, target in enumerate(targets):
                send = pltpu.make_async_copy(
                    results.at[which, head],
                    target.at[:, pl.ds(head * HEAD_DIM, HEAD_DIM)],
                    out_sems.at[which, head],
                )
                send.start()
                sends.append(send)
        for send in sends:
            send.wait()


def near_heads(core, after, arrays, previous=()):
    return pl.pallas_call(
        functools.partial(near_kernel, core),
        out_shape=[shape(TOK, HIDDEN)] * 3,
        in_specs=[spec(pl.ANY)] + [spec(pltpu.HBM)] * (4 + len(previous)),
        out_specs=[spec(pltpu.HBM)] * 3,
        scratch_shapes=[
            pltpu.VMEM((4, H_NEAR, TOK, HEAD_DIM), BF16),
            pltpu.VMEM((3, H_NEAR, TOK, HEAD_DIM), BF16),
            pltpu.SemaphoreType.DMA((4, H_NEAR)),
            pltpu.SemaphoreType.DMA((3, H_NEAR)),
        ],
        input_output_aliases={5 + which: which for which in range(len(previous))},
        cost_estimate=pl.CostEstimate(
            flops=10 * H_NEAR * TOK * TOK * HEAD_DIM,
            bytes_accessed=14 * TOK * NEAR_END,
            transcendentals=H_NEAR * TOK * TOK,
        ),
        compiler_params=params(16),
    )(after, *arrays, *previous)


def slot():
    return lax.div(lax.axis_index("inner"), HALVES)


def attend_wide(own_ref, other_ref, out_ref):
    wide_rows = SLOTS * 32
    kv = [ref[:, 0:32, :].reshape(wide_rows, 2 * HEAD_DIM) for ref in (own_ref, other_ref)]
    qg = [ref[:, 32:64, :].reshape(wide_rows, 2 * HEAD_DIM) for ref in (own_ref, other_ref)]
    row, column = iota2(16, wide_rows)
    source = 32 * (row // 2) + 2 * lax.axis_index("outer") + row % 2
    pick = one_hot(column == source)
    own_kv, own_qg = dot(pick, kv[0]).astype(BF16), dot(pick, qg[0]).astype(BF16)
    kv, qg = jnp.concatenate(kv, axis=0), jnp.concatenate(qg, axis=0)
    key, value = kv[:, :HEAD_DIM], kv[:, HEAD_DIM:]
    query, gradient = qg[:, :HEAD_DIM], qg[:, HEAD_DIM:]
    scores = dot_nt(key, query) * SCALE
    top = jnp.max(scores, axis=0, keepdims=True)
    exponent = jnp.exp(scores - top)
    inverse = 1.0 / jnp.sum(exponent, axis=0, keepdims=True)
    products = dot_nt(value, gradient)
    row_dots = jnp.sum(exponent * inverse * products, axis=0, keepdims=True)
    own_key, own_value = own_kv[:, :HEAD_DIM], own_kv[:, HEAD_DIM:]
    own_query, own_gradient = own_qg[:, :HEAD_DIM], own_qg[:, HEAD_DIM:]
    weights = jnp.exp(dot_nt(own_key, query) * SCALE - top) * inverse
    score_gradients = weights * (dot_nt(own_value, gradient) - row_dots) * SCALE
    dk = dot(score_gradients.astype(BF16), query).astype(BF16)
    dv = dot(weights.astype(BF16), gradient).astype(BF16)
    scores = dot_nt(own_query, key) * SCALE
    exponent = jnp.exp(scores - jnp.max(scores, axis=1, keepdims=True))
    weights = exponent * (1.0 / jnp.sum(exponent, axis=1, keepdims=True))
    products = dot_nt(own_gradient, value)
    row_dots = jnp.sum(weights * products, axis=1, keepdims=True)
    score_gradients = weights * (products - row_dots) * SCALE
    dq = dot(score_gradients.astype(BF16), key).astype(BF16)
    row, column = iota2(SLOTS * 16, 16)
    member, place = row // 16, row % 16
    spread = 0.0
    for which, rows in enumerate((dq, dk, dv)):
        mine = (place >= 2 * which) & (place < 2 * which + 2)
        spread += dot(one_hot(mine & (column == 2 * member + place - 2 * which)), rows)
    out_ref[...] = spread.astype(BF16).reshape(SLOTS, 16, HEAD_DIM)


def halves(ref, rows):
    block = ref[:, rows, :].reshape(HALF_KEYS, 2 * HEAD_DIM)
    return block[:, :HEAD_DIM], block[:, HEAD_DIM:]


def own_work_kernel(own_ref, other_ref, after, dq_ref, dkv_ref, wide_out):
    @pl.when(slot() >= H_MID)
    def wide():
        attend_wide(own_ref, other_ref, wide_out)

    @pl.when(slot() < H_MID)
    def attend():
        own_key, own_value = halves(own_ref, slice(0, 64))
        other_key, other_value = halves(other_ref, slice(0, 64))
        key = jnp.concatenate([own_key, other_key], axis=0)
        value = jnp.concatenate([own_value, other_value], axis=0)
        queries, gradients = halves(own_ref, slice(64, 128))
        for start in range(0, HALF_KEYS, QUERY_BLOCK):
            query = queries[start : start + QUERY_BLOCK]
            gradient = gradients[start : start + QUERY_BLOCK]
            weights, score_gradients = attention_transposed(query, key, value, gradient)
            dk = dot(score_gradients[:HALF_KEYS], query)
            dv = dot(weights[:HALF_KEYS], gradient)
            if start == 0:
                dkv_ref[:, :HEAD_DIM] = dk
                dkv_ref[:, HEAD_DIM:] = dv
            else:
                dkv_ref[:, :HEAD_DIM] += dk
                dkv_ref[:, HEAD_DIM:] += dv
            dq = dot_tn(key, score_gradients).T.astype(BF16)
            blocks = slice(start // MID_ROWS, (start + QUERY_BLOCK) // MID_ROWS)
            dq_ref[blocks] = dq.reshape(QUERY_BLOCK // MID_ROWS, MID_ROWS, HEAD_DIM)


def other_work_kernel(own_ref, other_ref, query_ref, dq_ref, dkv_ref, wide_ref, out_ref, sum_ref):
    @pl.when(slot() < H_MID)
    def attend():
        parts = [halves(own_ref, slice(0, 64)), halves(other_ref, slice(0, 64))]
        queries, gradients = halves(query_ref, slice(0, 64))
        for start in range(0, HALF_KEYS, QUERY_BLOCK):
            query = queries[start : start + QUERY_BLOCK]
            gradient = gradients[start : start + QUERY_BLOCK]
            weights, score_gradients = scaled_weights(parts, query, gradient)
            before = dkv_ref if start == 0 else sum_ref
            sum_ref[:, :HEAD_DIM] = before[:, :HEAD_DIM] + dot(score_gradients, query)
            sum_ref[:, HEAD_DIM:] = before[:, HEAD_DIM:] + dot(weights, gradient)
        out_ref[:, :, :HEAD_DIM] = dq_ref[...]
        dkv = sum_ref[...].astype(BF16)
        out_ref[:, :, HEAD_DIM:] = dkv.reshape(SLOTS, MID_ROWS, 2 * HEAD_DIM)

    @pl.when(slot() >= H_MID)
    def wide():
        out_ref[:, 0:16, :HEAD_DIM] = wide_ref[...]


def assemble_kernel(off_ref, got_ref, nq, nk, nv, dq_hbm, dk_hbm, dv_hbm, held, sems):
    copies = []

    def send(which, head, block):
        held[which, head] = block.astype(BF16)
        target = (dq_hbm, dk_hbm, dv_hbm)[which]
        copy = pltpu.make_async_copy(
            held.at[which, head],
            target.at[:, pl.ds(NEAR_END + head * HEAD_DIM, HEAD_DIM)],
            sems.at[which, head],
        )
        copy.start()
        copies.append(copy)

    row, unused = iota2(TOK, HEAD_DIM)
    for head in range(H_MID, H_MID + H_WIDE):
        offset = off_ref[head : head + 1, :HEAD_DIM]
        rows = got_ref[head, 0:16, :HEAD_DIM].astype(F32)
        first, second = row == offset, row == offset + R_WIDE
        for which in range(3):
            spread = jnp.where(first, rows[2 * which : 2 * which + 1], 0.0)
            send(which, head, jnp.where(second, rows[2 * which + 1 : 2 * which + 2], spread))
    row, column = iota2(TOK, MID_ROWS)
    for head in range(H_MID):
        place = one_hot(row - R_MID * column == off_ref[head : head + 1, :1])
        spread = dot(place, got_ref[head])
        for which in range(3):
            send(which, head, spread[:, which * HEAD_DIM : (which + 1) * HEAD_DIM])
    for copy in copies:
        copy.wait()


def spec(space):
    return pl.BlockSpec(memory_space=space)


def in_hbm(array):
    return pltpu.with_memory_space_constraint(array, pltpu.HBM)


def params(mebibytes):
    return pltpu.CompilerParams(vmem_limit_bytes=mebibytes * 1024 * 1024)


def shape(*sizes, kind=BF16):
    return jax.ShapeDtypeStruct(sizes, kind)


def work_cost(products):
    return pl.CostEstimate(
        flops=products * 4 * HALF_KEYS * HALF_KEYS * HEAD_DIM,
        bytes_accessed=0,
        transcendentals=2 * HALF_KEYS * HALF_KEYS,
    )


def body(queries, key_rows, values, out_grads, offsets):
    arrays = [in_hbm(array) for array in (queries, key_rows, values, out_grads)]
    heads = H_MID + H_WIDE
    wide_send, offset_rows = pl.pallas_call(
        wide_kernel,
        out_shape=[shape(OUTERS, 16, 256), shape(heads, TOK, kind=jnp.int32)],
        in_specs=[spec(pltpu.HBM)] * 5,
        out_specs=[spec(pltpu.VMEM)] * 2,
        scratch_shapes=[
            pltpu.SMEM((heads,), jnp.int32),
            pltpu.VMEM((4, H_WIDE, TOK, HEAD_DIM), BF16),
            pltpu.SemaphoreType.DMA,
            pltpu.SemaphoreType.DMA((4, H_WIDE)),
        ],
        compiler_params=params(8),
    )(in_hbm(offsets), *arrays)
    wide_got = lax.all_to_all(wide_send, "outer", 0, 0)
    packed = pl.pallas_call(
        mid_pack_kernel,
        out_shape=shape(SLOTS, 128, 256),
        in_specs=[spec(pltpu.VMEM)] + [spec(pltpu.HBM)] * 4,
        out_specs=spec(pltpu.VMEM),
        scratch_shapes=[
            pltpu.VMEM((4, H_MID, TOK, HEAD_DIM), BF16),
            pltpu.SemaphoreType.DMA((4, H_MID)),
        ],
        cost_estimate=pl.CostEstimate(
            flops=8 * H_MID * MID_ROWS * TOK * HEAD_DIM,
            bytes_accessed=8 * H_MID * TOK * HEAD_DIM,
            transcendentals=0,
        ),
        compiler_params=params(8),
    )(offset_rows, *arrays)
    near = near_heads(0, offset_rows, arrays)
    packed = pl.pallas_call(
        wide_pack_kernel,
        out_shape=shape(SLOTS, 128, 256),
        in_specs=[spec(pltpu.VMEM), spec(pltpu.VMEM), spec(pl.ANY)],
        out_specs=spec(pltpu.VMEM),
        input_output_aliases={1: 0},
        compiler_params=params(8),
    )(wide_got, packed, in_hbm(near[0]))
    own = lax.all_to_all(packed, "inner", 0, 0, axis_index_groups=ALONG_Z)
    other = lax.ppermute(own[:, 0:64, :], "inner", ACROSS_Y)
    other_queries = lax.ppermute(own[:, 64:128, :], "inner", ACROSS_Y)
    near = near_heads(1, own, arrays, near)
    dq, own_sums, wide_rows = pl.pallas_call(
        own_work_kernel,
        out_shape=[
            shape(SLOTS, MID_ROWS, HEAD_DIM),
            shape(HALF_KEYS, 256, kind=F32),
            shape(SLOTS, 16, HEAD_DIM),
        ],
        in_specs=[spec(pltpu.VMEM)] * 2 + [spec(pl.ANY)],
        out_specs=[spec(pltpu.VMEM)] * 3,
        cost_estimate=work_cost(5),
        compiler_params=params(24),
    )(own, other, in_hbm(near[0]))
    results = pl.pallas_call(
        other_work_kernel,
        out_shape=shape(SLOTS, MID_ROWS, 3 * HEAD_DIM),
        in_specs=[spec(pltpu.VMEM)] * 6,
        out_specs=spec(pltpu.VMEM),
        scratch_shapes=[pltpu.VMEM((HALF_KEYS, 256), F32)],
        cost_estimate=work_cost(4),
        compiler_params=params(24),
    )(own, other, other_queries, dq, own_sums, wide_rows)
    returned = lax.all_to_all(results, "inner", 0, 0, axis_index_groups=ALONG_Z)
    return tuple(
        pl.pallas_call(
            assemble_kernel,
            out_shape=[shape(TOK, HIDDEN)] * 3,
            in_specs=[spec(pltpu.VMEM)] * 2 + [spec(pltpu.HBM)] * 3,
            out_specs=[spec(pltpu.HBM)] * 3,
            scratch_shapes=[
                pltpu.VMEM((3, heads, TOK, HEAD_DIM), BF16),
                pltpu.SemaphoreType.DMA((3, heads)),
            ],
            input_output_aliases={2: 0, 3: 1, 4: 2},
            compiler_params=params(16),
        )(offset_rows, returned, *near)
    )


def solution(mesh):
    rows = P(("outer", "inner"), None)
    return jax.shard_map(
        body,
        mesh=mesh,
        in_specs=(rows, rows, rows, rows, P()),
        out_specs=(rows, rows, rows),
        check_vma=False,
    )
```

```python
import functools
import math

import jax
import jax.numpy as jnp
from jax import lax
from jax.experimental import pallas as pl
from jax.experimental.pallas import tpu as pltpu
from jax.sharding import PartitionSpec as P

HEAD_DIM = 128
H_NEAR = 4
H_MID = 5
H_WIDE = 3
R_MID = 4
R_WIDE = 128
TOK = 256
NEAR_END = H_NEAR * HEAD_DIM
MID_END = NEAR_END + H_MID * HEAD_DIM
HIDDEN = MID_END + H_WIDE * HEAD_DIM
OUTERS = 16
MID_ROWS = TOK // R_MID
SLOTS = 8
HALVES = 2
HALF_KEYS = SLOTS * MID_ROWS
ALONG_Z = [[HALVES * z + half for z in range(SLOTS)] for half in range(HALVES)]
ACROSS_Y = [(member, member ^ 1) for member in range(HALVES * SLOTS)]
SCALE = 1.0 / math.sqrt(HEAD_DIM)
EARLY_NEAR = (range(3), range(0))
LATE_NEAR = tuple(range(len(early), H_NEAR) for early in EARLY_NEAR)
EXP2_SCALE = SCALE * math.log2(math.e)
BF16 = jnp.bfloat16
F32 = jnp.float32


def dot(a, b):
    return lax.dot_general(a, b, (((1,), (0,)), ((), ())), preferred_element_type=F32)


def dot_nt(a, b):
    return lax.dot_general(a, b, (((1,), (1,)), ((), ())), preferred_element_type=F32)


def dot_tn(a, b):
    return lax.dot_general(a, b, (((0,), (0,)), ((), ())), preferred_element_type=F32)


def iota2(rows, columns):
    shape = (rows, columns)
    return (
        lax.broadcasted_iota(jnp.int32, shape, 0),
        lax.broadcasted_iota(jnp.int32, shape, 1),
    )


def one_hot(condition):
    return jnp.where(condition, 1.0, 0.0).astype(BF16)


def scaled_weights(parts, query, gradient):
    scores = [dot_nt(key, query) for key, unused in parts]
    top = functools.reduce(jnp.maximum, [jnp.max(s, axis=0, keepdims=True) for s in scores])
    exponents = [jnp.exp2((s - top) * EXP2_SCALE) for s in scores]
    inverse = 1.0 / sum(jnp.sum(e, axis=0, keepdims=True) for e in exponents)
    products = [dot_nt(value, gradient) for unused, value in parts]
    row_dots = inverse * sum(
        jnp.sum(e * p, axis=0, keepdims=True) for e, p in zip(exponents, products)
    )
    weights = exponents[0] * inverse
    score_gradients = weights * (products[0] - row_dots) * SCALE
    return weights.astype(BF16), score_gradients.astype(BF16)


def attention_transposed(query, key, value, gradient):
    return scaled_weights([(key, value)], query, gradient)


def fetch(sources, held, sems, heads, first=NEAR_END):
    copies = {}
    for at, head in enumerate(heads):
        for which, source in enumerate(sources):
            copies[head, which] = pltpu.make_async_copy(
                source.at[:, pl.ds(first + head * HEAD_DIM, HEAD_DIM)],
                held.at[which, at],
                sems.at[which, at],
            )
            copies[head, which].start()
    return copies


def pairs(copies, held, head, at):
    for which in range(4):
        copies[head, which].wait()
    kv = jnp.concatenate([held[1, at], held[2, at]], axis=1)
    qg = jnp.concatenate([held[0, at], held[3, at]], axis=1)
    return kv, qg


def wide_kernel(off_hbm, q_hbm, k_hbm, v_hbm, g_hbm, out_ref, off_out, off_ref, held, off_sem, sems):
    off_copy = pltpu.make_async_copy(off_hbm, off_ref, off_sem)
    off_copy.start()
    heads = range(H_MID, H_MID + H_WIDE)
    copies = fetch((q_hbm, k_hbm, v_hbm, g_hbm), held, sems, heads)
    off_copy.wait()
    for head in range(H_MID + H_WIDE):
        off_out[head : head + 1, :] = jnp.full((1, TOK), off_ref[head], jnp.int32)
    row, unused = iota2(16, HEAD_DIM)
    row_pair, unused = iota2(16, 2 * HEAD_DIM)
    rows = jnp.zeros((16, 2 * HEAD_DIM), F32)
    for at, head in enumerate(heads):
        offset = off_ref[head]
        base, place = lax.div(offset, 16) * 16, lax.rem(offset, 16)
        for which in range(4):
            copies[head, which].wait()
        for again in range(2):
            tile = pl.ds(pl.multiple_of(base + again * R_WIDE, 16), 16)
            picked = [
                jnp.sum(
                    jnp.where(row == place, held[which, at, tile, :].astype(F32), 0.0),
                    axis=0,
                    keepdims=True,
                )
                for which in range(4)
            ]
            kv = jnp.concatenate([picked[1], picked[2]], axis=1)
            qg = jnp.concatenate([picked[0], picked[3]], axis=1)
            rows = jnp.where(row_pair == 2 * at + again, kv, rows)
            rows = jnp.where(row_pair == 6 + 2 * at + again, qg, rows)
    rows = rows.astype(BF16)
    for target in range(OUTERS):
        out_ref[target] = rows


def mid_pack_kernel(off_ref, q_hbm, k_hbm, v_hbm, g_hbm, out_ref, held, sems):
    copies = fetch((q_hbm, k_hbm, v_hbm, g_hbm), held, sems, range(H_MID))
    row, column = iota2(MID_ROWS, TOK)
    for head in range(H_MID):
        pick = one_hot(column - R_MID * row == off_ref[head : head + 1, :])
        kv, qg = pairs(copies, held, head, head)
        out_ref[head, 0:64, :] = dot(pick, kv).astype(BF16)
        out_ref[head, 64:128, :] = dot(pick, qg).astype(BF16)
    for head in range(H_MID, SLOTS):
        out_ref[head, 64:128, :] = jnp.zeros((64, 2 * HEAD_DIM), BF16)


def wide_pack_kernel(got_ref, packed, after, out_ref):
    rows = got_ref[...].reshape(OUTERS * 16, 2 * HEAD_DIM)
    row, column = iota2(64, OUTERS * 16)
    base = 16 * ((row % 32) // 2) + row % 2 + jnp.where(row < 32, 0, 6)
    for head in range(H_WIDE):
        picked = dot(one_hot(column == base + 2 * head), rows)
        out_ref[H_MID + head, 0:64, :] = picked.astype(BF16)


def near_some(sources, targets, held, results, sems, out_sems, heads):
    copies = fetch(sources, held, sems, heads, 0)
    sends = []
    for at, head in enumerate(heads):
        for which in range(4):
            copies[head, which].wait()
        query, key, value, gradient = (held[which, at] for which in range(4))
        weights, score_gradients = attention_transposed(query, key, value, gradient)
        results[0, at] = dot_tn(score_gradients, key).astype(BF16)
        results[1, at] = dot(score_gradients, query).astype(BF16)
        results[2, at] = dot(weights, gradient).astype(BF16)
        for which, target in enumerate(targets):
            send = pltpu.make_async_copy(
                results.at[which, at],
                target.at[:, pl.ds(head * HEAD_DIM, HEAD_DIM)],
                out_sems.at[which, at],
            )
            send.start()
            sends.append(send)
    for send in sends:
        send.wait()


def near_kernel(heads_of_core, after, q_hbm, k_hbm, v_hbm, g_hbm, *rest):
    targets, (held, results, sems, out_sems) = rest[-7:-4], rest[-4:]
    for core, heads in enumerate(heads_of_core):
        if heads:

            @pl.when(lax.rem(lax.axis_index("outer"), 2) == core)
            def attend(heads=heads):
                sources = (q_hbm, k_hbm, v_hbm, g_hbm)
                near_some(sources, targets, held, results, sems, out_sems, heads)


def near_heads(heads_of_core, after, arrays, previous=()):
    return pl.pallas_call(
        functools.partial(near_kernel, heads_of_core),
        out_shape=[shape(TOK, HIDDEN)] * 3,
        in_specs=[spec(pl.ANY)] + [spec(pltpu.HBM)] * (4 + len(previous)),
        out_specs=[spec(pltpu.HBM)] * 3,
        scratch_shapes=[
            pltpu.VMEM((4, H_NEAR, TOK, HEAD_DIM), BF16),
            pltpu.VMEM((3, H_NEAR, TOK, HEAD_DIM), BF16),
            pltpu.SemaphoreType.DMA((4, H_NEAR)),
            pltpu.SemaphoreType.DMA((3, H_NEAR)),
        ],
        input_output_aliases={5 + which: which for which in range(len(previous))},
        cost_estimate=pl.CostEstimate(
            flops=10 * H_NEAR * TOK * TOK * HEAD_DIM,
            bytes_accessed=14 * TOK * NEAR_END,
            transcendentals=H_NEAR * TOK * TOK,
        ),
        compiler_params=params(16),
    )(after, *arrays, *previous)


def slot():
    return lax.div(lax.axis_index("inner"), HALVES)


def attend_wide(own_ref, other_ref, out_ref):
    wide_rows = SLOTS * 32
    kv = [ref[:, 0:32, :].reshape(wide_rows, 2 * HEAD_DIM) for ref in (own_ref, other_ref)]
    qg = [ref[:, 32:64, :].reshape(wide_rows, 2 * HEAD_DIM) for ref in (own_ref, other_ref)]
    row, column = iota2(16, wide_rows)
    source = 32 * (row // 2) + 2 * lax.axis_index("outer") + row % 2
    pick = one_hot(column == source)
    own_kv, own_qg = dot(pick, kv[0]).astype(BF16), dot(pick, qg[0]).astype(BF16)
    kv, qg = jnp.concatenate(kv, axis=0), jnp.concatenate(qg, axis=0)
    key, value = kv[:, :HEAD_DIM], kv[:, HEAD_DIM:]
    query, gradient = qg[:, :HEAD_DIM], qg[:, HEAD_DIM:]
    scores = dot_nt(key, query) * SCALE
    top = jnp.max(scores, axis=0, keepdims=True)
    exponent = jnp.exp(scores - top)
    inverse = 1.0 / jnp.sum(exponent, axis=0, keepdims=True)
    products = dot_nt(value, gradient)
    row_dots = jnp.sum(exponent * inverse * products, axis=0, keepdims=True)
    own_key, own_value = own_kv[:, :HEAD_DIM], own_kv[:, HEAD_DIM:]
    own_query, own_gradient = own_qg[:, :HEAD_DIM], own_qg[:, HEAD_DIM:]
    weights = jnp.exp(dot_nt(own_key, query) * SCALE - top) * inverse
    score_gradients = weights * (dot_nt(own_value, gradient) - row_dots) * SCALE
    dk = dot(score_gradients.astype(BF16), query).astype(BF16)
    dv = dot(weights.astype(BF16), gradient).astype(BF16)
    scores = dot_nt(own_query, key) * SCALE
    exponent = jnp.exp(scores - jnp.max(scores, axis=1, keepdims=True))
    weights = exponent * (1.0 / jnp.sum(exponent, axis=1, keepdims=True))
    products = dot_nt(own_gradient, value)
    row_dots = jnp.sum(weights * products, axis=1, keepdims=True)
    score_gradients = weights * (products - row_dots) * SCALE
    dq = dot(score_gradients.astype(BF16), key).astype(BF16)
    row, column = iota2(SLOTS * 16, 16)
    member, place = row // 16, row % 16
    spread = 0.0
    for which, rows in enumerate((dq, dk, dv)):
        mine = (place >= 2 * which) & (place < 2 * which + 2)
        spread += dot(one_hot(mine & (column == 2 * member + place - 2 * which)), rows)
    out_ref[...] = spread.astype(BF16).reshape(SLOTS, 16, HEAD_DIM)


def halves(ref, rows):
    block = ref[:, rows, :].reshape(HALF_KEYS, 2 * HEAD_DIM)
    return block[:, :HEAD_DIM], block[:, HEAD_DIM:]


def own_work_kernel(own_ref, other_ref, after, dq_ref, dkv_ref, wide_out):
    @pl.when(slot() >= H_MID)
    def wide():
        attend_wide(own_ref, other_ref, wide_out)

    @pl.when(slot() < H_MID)
    def attend():
        parts = [halves(own_ref, slice(0, 64)), halves(other_ref, slice(0, 64))]
        key, value = (jnp.concatenate(pieces, axis=0) for pieces in zip(*parts))
        query, gradient = halves(own_ref, slice(64, 128))
        weights, score_gradients = attention_transposed(query, key, value, gradient)
        dkv_ref[:, :HEAD_DIM] = dot(score_gradients[:HALF_KEYS], query)
        dkv_ref[:, HEAD_DIM:] = dot(weights[:HALF_KEYS], gradient)
        dq = dot_tn(key, score_gradients).T.astype(BF16)
        dq_ref[...] = dq.reshape(SLOTS, MID_ROWS, HEAD_DIM)


def other_work_kernel(own_ref, other_ref, query_ref, dq_ref, dkv_ref, wide_ref, out_ref):
    @pl.when(slot() < H_MID)
    def attend():
        parts = [halves(own_ref, slice(0, 64)), halves(other_ref, slice(0, 64))]
        query, gradient = halves(query_ref, slice(0, 64))
        weights, score_gradients = scaled_weights(parts, query, gradient)
        dk = dkv_ref[:, :HEAD_DIM] + dot(score_gradients, query)
        dv = dkv_ref[:, HEAD_DIM:] + dot(weights, gradient)
        out_ref[:, :, :HEAD_DIM] = dq_ref[...]
        for at, sums in ((HEAD_DIM, dk), (2 * HEAD_DIM, dv)):
            sums = sums.astype(BF16).reshape(SLOTS, MID_ROWS, HEAD_DIM)
            out_ref[:, :, at : at + HEAD_DIM] = sums

    @pl.when(slot() >= H_MID)
    def wide():
        out_ref[:, 0:16, :HEAD_DIM] = wide_ref[...]


def assemble_kernel(off_ref, got_ref, nq, nk, nv, dq_hbm, dk_hbm, dv_hbm, held, sems):
    copies = []

    def send(which, head, block):
        held[which, head] = block.astype(BF16)
        target = (dq_hbm, dk_hbm, dv_hbm)[which]
        copy = pltpu.make_async_copy(
            held.at[which, head],
            target.at[:, pl.ds(NEAR_END + head * HEAD_DIM, HEAD_DIM)],
            sems.at[which, head],
        )
        copy.start()
        copies.append(copy)

    row, unused = iota2(TOK, HEAD_DIM)
    for head in range(H_MID, H_MID + H_WIDE):
        offset = off_ref[head : head + 1, :HEAD_DIM]
        rows = got_ref[head, 0:16, :HEAD_DIM].astype(F32)
        first, second = row == offset, row == offset + R_WIDE
        for which in range(3):
            spread = jnp.where(first, rows[2 * which : 2 * which + 1], 0.0)
            send(which, head, jnp.where(second, rows[2 * which + 1 : 2 * which + 2], spread))
    row, column = iota2(TOK, MID_ROWS)
    for head in range(H_MID):
        place = one_hot(row - R_MID * column == off_ref[head : head + 1, :1])
        spread = dot(place, got_ref[head])
        for which in range(3):
            send(which, head, spread[:, which * HEAD_DIM : (which + 1) * HEAD_DIM])
    for copy in copies:
        copy.wait()


def spec(space):
    return pl.BlockSpec(memory_space=space)


def in_hbm(array):
    return pltpu.with_memory_space_constraint(array, pltpu.HBM)


def params(mebibytes):
    return pltpu.CompilerParams(vmem_limit_bytes=mebibytes * 1024 * 1024)


def shape(*sizes, kind=BF16):
    return jax.ShapeDtypeStruct(sizes, kind)


def work_cost(products):
    return pl.CostEstimate(
        flops=products * 4 * HALF_KEYS * HALF_KEYS * HEAD_DIM,
        bytes_accessed=0,
        transcendentals=2 * HALF_KEYS * HALF_KEYS,
    )


def body(queries, key_rows, values, out_grads, offsets):
    arrays = [in_hbm(array) for array in (queries, key_rows, values, out_grads)]
    heads = H_MID + H_WIDE
    wide_send, offset_rows = pl.pallas_call(
        wide_kernel,
        out_shape=[shape(OUTERS, 16, 256), shape(heads, TOK, kind=jnp.int32)],
        in_specs=[spec(pltpu.HBM)] * 5,
        out_specs=[spec(pltpu.VMEM)] * 2,
        scratch_shapes=[
            pltpu.SMEM((heads,), jnp.int32),
            pltpu.VMEM((4, H_WIDE, TOK, HEAD_DIM), BF16),
            pltpu.SemaphoreType.DMA,
            pltpu.SemaphoreType.DMA((4, H_WIDE)),
        ],
        compiler_params=params(8),
    )(in_hbm(offsets), *arrays)
    wide_got = lax.all_to_all(wide_send, "outer", 0, 0)
    packed = pl.pallas_call(
        mid_pack_kernel,
        out_shape=shape(SLOTS, 128, 256),
        in_specs=[spec(pltpu.VMEM)] + [spec(pltpu.HBM)] * 4,
        out_specs=spec(pltpu.VMEM),
        scratch_shapes=[
            pltpu.VMEM((4, H_MID, TOK, HEAD_DIM), BF16),
            pltpu.SemaphoreType.DMA((4, H_MID)),
        ],
        cost_estimate=pl.CostEstimate(
            flops=8 * H_MID * MID_ROWS * TOK * HEAD_DIM,
            bytes_accessed=8 * H_MID * TOK * HEAD_DIM,
            transcendentals=0,
        ),
        compiler_params=params(8),
    )(offset_rows, *arrays)
    near = near_heads(EARLY_NEAR, wide_got, arrays)
    packed = pl.pallas_call(
        wide_pack_kernel,
        out_shape=shape(SLOTS, 128, 256),
        in_specs=[spec(pltpu.VMEM), spec(pltpu.VMEM), spec(pl.ANY)],
        out_specs=spec(pltpu.VMEM),
        input_output_aliases={1: 0},
        compiler_params=params(8),
    )(wide_got, packed, in_hbm(near[0]))
    own = lax.all_to_all(packed, "inner", 0, 0, axis_index_groups=ALONG_Z)
    other = lax.ppermute(own[:, 0:64, :], "inner", ACROSS_Y)
    other_queries = lax.ppermute(own[:, 64:128, :], "inner", ACROSS_Y)
    near = near_heads(LATE_NEAR, own, arrays, near)
    dq, own_sums, wide_rows = pl.pallas_call(
        own_work_kernel,
        out_shape=[
            shape(SLOTS, MID_ROWS, HEAD_DIM),
            shape(HALF_KEYS, 256, kind=F32),
            shape(SLOTS, 16, HEAD_DIM),
        ],
        in_specs=[spec(pltpu.VMEM)] * 2 + [spec(pl.ANY)],
        out_specs=[spec(pltpu.VMEM)] * 3,
        cost_estimate=work_cost(5),
        compiler_params=params(24),
    )(own, other, in_hbm(near[0]))
    results = pl.pallas_call(
        other_work_kernel,
        out_shape=shape(SLOTS, MID_ROWS, 3 * HEAD_DIM),
        in_specs=[spec(pltpu.VMEM)] * 6,
        out_specs=spec(pltpu.VMEM),
        cost_estimate=work_cost(4),
        compiler_params=params(24),
    )(own, other, other_queries, dq, own_sums, wide_rows)
    returned = lax.all_to_all(results, "inner", 0, 0, axis_index_groups=ALONG_Z)
    return tuple(
        pl.pallas_call(
            assemble_kernel,
            out_shape=[shape(TOK, HIDDEN)] * 3,
            in_specs=[spec(pltpu.VMEM)] * 2 + [spec(pltpu.HBM)] * 3,
            out_specs=[spec(pltpu.HBM)] * 3,
            scratch_shapes=[
                pltpu.VMEM((3, heads, TOK, HEAD_DIM), BF16),
                pltpu.SemaphoreType.DMA((3, heads)),
            ],
            input_output_aliases={2: 0, 3: 1, 4: 2},
            compiler_params=params(16),
        )(offset_rows, returned, *near)
    )


def solution(mesh):
    rows = P(("outer", "inner"), None)
    return jax.shard_map(
        body,
        mesh=mesh,
        in_specs=(rows, rows, rows, rows, P()),
        out_specs=(rows, rows, rows),
        check_vma=False,
    )
```

```python
import functools
import math

import jax
import jax.numpy as jnp
from jax import lax
from jax.experimental import pallas as pl
from jax.experimental.pallas import tpu as pltpu
from jax.sharding import PartitionSpec as P

HEAD_DIM = 128
H_NEAR = 4
H_MID = 5
H_WIDE = 3
R_MID = 4
R_WIDE = 128
TOK = 256
NEAR_END = H_NEAR * HEAD_DIM
MID_END = NEAR_END + H_MID * HEAD_DIM
HIDDEN = MID_END + H_WIDE * HEAD_DIM
OUTERS = 16
MID_ROWS = TOK // R_MID
SLOTS = 8
HALVES = 2
HALF_KEYS = SLOTS * MID_ROWS
Z_ORDER = (5, 6, 7, 3, 4, 1, 2, 0)
ALONG_Z = [[HALVES * z + half for z in Z_ORDER] for half in range(HALVES)]
ACROSS_Y = [(member, member ^ 1) for member in range(HALVES * SLOTS)]
SCALE = 1.0 / math.sqrt(HEAD_DIM)
EARLY_NEAR = (range(3), range(0))
LATE_NEAR = tuple(range(len(early), H_NEAR) for early in EARLY_NEAR)
EXP2_SCALE = SCALE * math.log2(math.e)
BF16 = jnp.bfloat16
F32 = jnp.float32


def dot(a, b):
    return lax.dot_general(a, b, (((1,), (0,)), ((), ())), preferred_element_type=F32)


def dot_nt(a, b):
    return lax.dot_general(a, b, (((1,), (1,)), ((), ())), preferred_element_type=F32)


def dot_tn(a, b):
    return lax.dot_general(a, b, (((0,), (0,)), ((), ())), preferred_element_type=F32)


def iota2(rows, columns):
    shape = (rows, columns)
    return (
        lax.broadcasted_iota(jnp.int32, shape, 0),
        lax.broadcasted_iota(jnp.int32, shape, 1),
    )


def one_hot(condition):
    return jnp.where(condition, 1.0, 0.0).astype(BF16)


def scaled_weights(parts, query, gradient):
    scores = [dot_nt(key, query) for key, unused in parts]
    top = functools.reduce(jnp.maximum, [jnp.max(s, axis=0, keepdims=True) for s in scores])
    exponents = [jnp.exp2((s - top) * EXP2_SCALE) for s in scores]
    inverse = 1.0 / sum(jnp.sum(e, axis=0, keepdims=True) for e in exponents)
    products = [dot_nt(value, gradient) for unused, value in parts]
    row_dots = inverse * sum(
        jnp.sum(e * p, axis=0, keepdims=True) for e, p in zip(exponents, products)
    )
    weights = exponents[0] * inverse
    score_gradients = weights * (products[0] - row_dots) * SCALE
    return weights.astype(BF16), score_gradients.astype(BF16)


def attention_transposed(query, key, value, gradient):
    return scaled_weights([(key, value)], query, gradient)


def fetch(sources, held, sems, heads, first=NEAR_END):
    copies = {}
    for at, head in enumerate(heads):
        for which, source in enumerate(sources):
            copies[head, which] = pltpu.make_async_copy(
                source.at[:, pl.ds(first + head * HEAD_DIM, HEAD_DIM)],
                held.at[which, at],
                sems.at[which, at],
            )
            copies[head, which].start()
    return copies


def pairs(copies, held, head, at):
    for which in range(4):
        copies[head, which].wait()
    kv = jnp.concatenate([held[1, at], held[2, at]], axis=1)
    qg = jnp.concatenate([held[0, at], held[3, at]], axis=1)
    return kv, qg


def wide_kernel(off_hbm, q_hbm, k_hbm, v_hbm, g_hbm, out_ref, off_out, off_ref, held, off_sem, sems):
    off_copy = pltpu.make_async_copy(off_hbm, off_ref, off_sem)
    off_copy.start()
    heads = range(H_MID, H_MID + H_WIDE)
    copies = fetch((q_hbm, k_hbm, v_hbm, g_hbm), held, sems, heads)
    off_copy.wait()
    for head in range(H_MID + H_WIDE):
        off_out[head : head + 1, :] = jnp.full((1, TOK), off_ref[head], jnp.int32)
    row, unused = iota2(16, HEAD_DIM)
    row_pair, unused = iota2(16, 2 * HEAD_DIM)
    rows = jnp.zeros((16, 2 * HEAD_DIM), F32)
    for at, head in enumerate(heads):
        offset = off_ref[head]
        base, place = lax.div(offset, 16) * 16, lax.rem(offset, 16)
        for which in range(4):
            copies[head, which].wait()
        for again in range(2):
            tile = pl.ds(pl.multiple_of(base + again * R_WIDE, 16), 16)
            picked = [
                jnp.sum(
                    jnp.where(row == place, held[which, at, tile, :].astype(F32), 0.0),
                    axis=0,
                    keepdims=True,
                )
                for which in range(4)
            ]
            kv = jnp.concatenate([picked[1], picked[2]], axis=1)
            qg = jnp.concatenate([picked[0], picked[3]], axis=1)
            rows = jnp.where(row_pair == 2 * at + again, kv, rows)
            rows = jnp.where(row_pair == 6 + 2 * at + again, qg, rows)
    rows = rows.astype(BF16)
    for target in range(OUTERS):
        out_ref[target] = rows


def mid_pack_kernel(off_ref, q_hbm, k_hbm, v_hbm, g_hbm, out_ref, held, sems):
    copies = fetch((q_hbm, k_hbm, v_hbm, g_hbm), held, sems, range(H_MID))
    row, column = iota2(MID_ROWS, TOK)
    for head in range(H_MID):
        pick = one_hot(column - R_MID * row == off_ref[head : head + 1, :])
        kv, qg = pairs(copies, held, head, head)
        out_ref[head, 0:64, :] = dot(pick, kv).astype(BF16)
        out_ref[head, 64:128, :] = dot(pick, qg).astype(BF16)
    for head in range(H_MID, SLOTS):
        out_ref[head, 64:128, :] = jnp.zeros((64, 2 * HEAD_DIM), BF16)


def wide_pack_kernel(got_ref, packed, after, out_ref):
    rows = got_ref[...].reshape(OUTERS * 16, 2 * HEAD_DIM)
    row, column = iota2(64, OUTERS * 16)
    base = 16 * ((row % 32) // 2) + row % 2 + jnp.where(row < 32, 0, 6)
    for head in range(H_WIDE):
        picked = dot(one_hot(column == base + 2 * head), rows)
        out_ref[H_MID + head, 0:64, :] = picked.astype(BF16)


def near_some(sources, targets, held, results, sems, out_sems, heads):
    copies = fetch(sources, held, sems, heads, 0)
    sends = []
    for at, head in enumerate(heads):
        for which in range(4):
            copies[head, which].wait()
        query, key, value, gradient = (held[which, at] for which in range(4))
        weights, score_gradients = attention_transposed(query, key, value, gradient)
        results[0, at] = dot_tn(score_gradients, key).astype(BF16)
        results[1, at] = dot(score_gradients, query).astype(BF16)
        results[2, at] = dot(weights, gradient).astype(BF16)
        for which, target in enumerate(targets):
            send = pltpu.make_async_copy(
                results.at[which, at],
                target.at[:, pl.ds(head * HEAD_DIM, HEAD_DIM)],
                out_sems.at[which, at],
            )
            send.start()
            sends.append(send)
    for send in sends:
        send.wait()


def near_kernel(heads_of_core, after, q_hbm, k_hbm, v_hbm, g_hbm, *rest):
    targets, (held, results, sems, out_sems) = rest[-7:-4], rest[-4:]
    for core, heads in enumerate(heads_of_core):
        if heads:

            @pl.when(lax.rem(lax.axis_index("outer"), 2) == core)
            def attend(heads=heads):
                sources = (q_hbm, k_hbm, v_hbm, g_hbm)
                near_some(sources, targets, held, results, sems, out_sems, heads)


def near_heads(heads_of_core, after, arrays, previous=()):
    return pl.pallas_call(
        functools.partial(near_kernel, heads_of_core),
        out_shape=[shape(TOK, HIDDEN)] * 3,
        in_specs=[spec(pl.ANY)] + [spec(pltpu.HBM)] * (4 + len(previous)),
        out_specs=[spec(pltpu.HBM)] * 3,
        scratch_shapes=[
            pltpu.VMEM((4, H_NEAR, TOK, HEAD_DIM), BF16),
            pltpu.VMEM((3, H_NEAR, TOK, HEAD_DIM), BF16),
            pltpu.SemaphoreType.DMA((4, H_NEAR)),
            pltpu.SemaphoreType.DMA((3, H_NEAR)),
        ],
        input_output_aliases={5 + which: which for which in range(len(previous))},
        cost_estimate=pl.CostEstimate(
            flops=10 * H_NEAR * TOK * TOK * HEAD_DIM,
            bytes_accessed=14 * TOK * NEAR_END,
            transcendentals=H_NEAR * TOK * TOK,
        ),
        compiler_params=params(16),
    )(after, *arrays, *previous)


def slot():
    z = lax.div(lax.axis_index("inner"), HALVES)
    return sum(jnp.where(z == place, at, 0) for at, place in enumerate(Z_ORDER))


def attend_wide(own_ref, other_ref, out_ref):
    wide_rows = SLOTS * 32
    kv = [ref[:, 0:32, :].reshape(wide_rows, 2 * HEAD_DIM) for ref in (own_ref, other_ref)]
    qg = [ref[:, 32:64, :].reshape(wide_rows, 2 * HEAD_DIM) for ref in (own_ref, other_ref)]
    row, column = iota2(16, wide_rows)
    source = 32 * (row // 2) + 2 * lax.axis_index("outer") + row % 2
    pick = one_hot(column == source)
    own_kv, own_qg = dot(pick, kv[0]).astype(BF16), dot(pick, qg[0]).astype(BF16)
    kv, qg = jnp.concatenate(kv, axis=0), jnp.concatenate(qg, axis=0)
    key, value = kv[:, :HEAD_DIM], kv[:, HEAD_DIM:]
    query, gradient = qg[:, :HEAD_DIM], qg[:, HEAD_DIM:]
    scores = dot_nt(key, query) * SCALE
    top = jnp.max(scores, axis=0, keepdims=True)
    exponent = jnp.exp(scores - top)
    inverse = 1.0 / jnp.sum(exponent, axis=0, keepdims=True)
    products = dot_nt(value, gradient)
    row_dots = jnp.sum(exponent * inverse * products, axis=0, keepdims=True)
    own_key, own_value = own_kv[:, :HEAD_DIM], own_kv[:, HEAD_DIM:]
    own_query, own_gradient = own_qg[:, :HEAD_DIM], own_qg[:, HEAD_DIM:]
    weights = jnp.exp(dot_nt(own_key, query) * SCALE - top) * inverse
    score_gradients = weights * (dot_nt(own_value, gradient) - row_dots) * SCALE
    dk = dot(score_gradients.astype(BF16), query).astype(BF16)
    dv = dot(weights.astype(BF16), gradient).astype(BF16)
    scores = dot_nt(own_query, key) * SCALE
    exponent = jnp.exp(scores - jnp.max(scores, axis=1, keepdims=True))
    weights = exponent * (1.0 / jnp.sum(exponent, axis=1, keepdims=True))
    products = dot_nt(own_gradient, value)
    row_dots = jnp.sum(weights * products, axis=1, keepdims=True)
    score_gradients = weights * (products - row_dots) * SCALE
    dq = dot(score_gradients.astype(BF16), key).astype(BF16)
    row, column = iota2(SLOTS * 16, 16)
    member, place = row // 16, row % 16
    spread = 0.0
    for which, rows in enumerate((dq, dk, dv)):
        mine = (place >= 2 * which) & (place < 2 * which + 2)
        spread += dot(one_hot(mine & (column == 2 * member + place - 2 * which)), rows)
    out_ref[...] = spread.astype(BF16).reshape(SLOTS, 16, HEAD_DIM)


def halves(ref, rows):
    block = ref[:, rows, :].reshape(HALF_KEYS, 2 * HEAD_DIM)
    return block[:, :HEAD_DIM], block[:, HEAD_DIM:]


def own_work_kernel(own_ref, other_ref, after, dq_ref, dkv_ref, wide_out):
    @pl.when(slot() >= H_MID)
    def wide():
        attend_wide(own_ref, other_ref, wide_out)

    @pl.when(slot() < H_MID)
    def attend():
        parts = [halves(own_ref, slice(0, 64)), halves(other_ref, slice(0, 64))]
        key, value = (jnp.concatenate(pieces, axis=0) for pieces in zip(*parts))
        query, gradient = halves(own_ref, slice(64, 128))
        weights, score_gradients = attention_transposed(query, key, value, gradient)
        dkv_ref[:, :HEAD_DIM] = dot(score_gradients[:HALF_KEYS], query)
        dkv_ref[:, HEAD_DIM:] = dot(weights[:HALF_KEYS], gradient)
        dq = dot_tn(key, score_gradients).T.astype(BF16)
        dq_ref[...] = dq.reshape(SLOTS, MID_ROWS, HEAD_DIM)


def other_work_kernel(own_ref, other_ref, query_ref, dq_ref, dkv_ref, wide_ref, out_ref):
    @pl.when(slot() < H_MID)
    def attend():
        parts = [halves(own_ref, slice(0, 64)), halves(other_ref, slice(0, 64))]
        query, gradient = halves(query_ref, slice(0, 64))
        weights, score_gradients = scaled_weights(parts, query, gradient)
        dk = dkv_ref[:, :HEAD_DIM] + dot(score_gradients, query)
        dv = dkv_ref[:, HEAD_DIM:] + dot(weights, gradient)
        out_ref[:, :, :HEAD_DIM] = dq_ref[...]
        for at, sums in ((HEAD_DIM, dk), (2 * HEAD_DIM, dv)):
            sums = sums.astype(BF16).reshape(SLOTS, MID_ROWS, HEAD_DIM)
            out_ref[:, :, at : at + HEAD_DIM] = sums

    @pl.when(slot() >= H_MID)
    def wide():
        out_ref[:, 0:16, :HEAD_DIM] = wide_ref[...]


def assemble_kernel(off_ref, got_ref, nq, nk, nv, dq_hbm, dk_hbm, dv_hbm, held, sems):
    copies = []

    def send(which, head, block):
        held[which, head] = block.astype(BF16)
        target = (dq_hbm, dk_hbm, dv_hbm)[which]
        copy = pltpu.make_async_copy(
            held.at[which, head],
            target.at[:, pl.ds(NEAR_END + head * HEAD_DIM, HEAD_DIM)],
            sems.at[which, head],
        )
        copy.start()
        copies.append(copy)

    row, unused = iota2(TOK, HEAD_DIM)
    for head in range(H_MID, H_MID + H_WIDE):
        offset = off_ref[head : head + 1, :HEAD_DIM]
        rows = got_ref[head, 0:16, :HEAD_DIM].astype(F32)
        first, second = row == offset, row == offset + R_WIDE
        for which in range(3):
            spread = jnp.where(first, rows[2 * which : 2 * which + 1], 0.0)
            send(which, head, jnp.where(second, rows[2 * which + 1 : 2 * which + 2], spread))
    row, column = iota2(TOK, MID_ROWS)
    for head in range(H_MID):
        place = one_hot(row - R_MID * column == off_ref[head : head + 1, :1])
        spread = dot(place, got_ref[head])
        for which in range(3):
            send(which, head, spread[:, which * HEAD_DIM : (which + 1) * HEAD_DIM])
    for copy in copies:
        copy.wait()


def spec(space):
    return pl.BlockSpec(memory_space=space)


def in_hbm(array):
    return pltpu.with_memory_space_constraint(array, pltpu.HBM)


def params(mebibytes):
    return pltpu.CompilerParams(vmem_limit_bytes=mebibytes * 1024 * 1024)


def shape(*sizes, kind=BF16):
    return jax.ShapeDtypeStruct(sizes, kind)


def work_cost(products):
    return pl.CostEstimate(
        flops=products * 4 * HALF_KEYS * HALF_KEYS * HEAD_DIM,
        bytes_accessed=0,
        transcendentals=2 * HALF_KEYS * HALF_KEYS,
    )


def body(queries, key_rows, values, out_grads, offsets):
    arrays = [in_hbm(array) for array in (queries, key_rows, values, out_grads)]
    heads = H_MID + H_WIDE
    wide_send, offset_rows = pl.pallas_call(
        wide_kernel,
        out_shape=[shape(OUTERS, 16, 256), shape(heads, TOK, kind=jnp.int32)],
        in_specs=[spec(pltpu.HBM)] * 5,
        out_specs=[spec(pltpu.VMEM)] * 2,
        scratch_shapes=[
            pltpu.SMEM((heads,), jnp.int32),
            pltpu.VMEM((4, H_WIDE, TOK, HEAD_DIM), BF16),
            pltpu.SemaphoreType.DMA,
            pltpu.SemaphoreType.DMA((4, H_WIDE)),
        ],
        compiler_params=params(8),
    )(in_hbm(offsets), *arrays)
    wide_got = lax.all_to_all(wide_send, "outer", 0, 0)
    packed = pl.pallas_call(
        mid_pack_kernel,
        out_shape=shape(SLOTS, 128, 256),
        in_specs=[spec(pltpu.VMEM)] + [spec(pltpu.HBM)] * 4,
        out_specs=spec(pltpu.VMEM),
        scratch_shapes=[
            pltpu.VMEM((4, H_MID, TOK, HEAD_DIM), BF16),
            pltpu.SemaphoreType.DMA((4, H_MID)),
        ],
        cost_estimate=pl.CostEstimate(
            flops=8 * H_MID * MID_ROWS * TOK * HEAD_DIM,
            bytes_accessed=8 * H_MID * TOK * HEAD_DIM,
            transcendentals=0,
        ),
        compiler_params=params(8),
    )(offset_rows, *arrays)
    near = near_heads(EARLY_NEAR, wide_got, arrays)
    packed = pl.pallas_call(
        wide_pack_kernel,
        out_shape=shape(SLOTS, 128, 256),
        in_specs=[spec(pltpu.VMEM), spec(pltpu.VMEM), spec(pl.ANY)],
        out_specs=spec(pltpu.VMEM),
        input_output_aliases={1: 0},
        compiler_params=params(8),
    )(wide_got, packed, in_hbm(near[0]))
    own = lax.all_to_all(packed, "inner", 0, 0, axis_index_groups=ALONG_Z)
    other = lax.ppermute(own[:, 0:64, :], "inner", ACROSS_Y)
    other_queries = lax.ppermute(own[:, 64:128, :], "inner", ACROSS_Y)
    near = near_heads(LATE_NEAR, own, arrays, near)
    dq, own_sums, wide_rows = pl.pallas_call(
        own_work_kernel,
        out_shape=[
            shape(SLOTS, MID_ROWS, HEAD_DIM),
            shape(HALF_KEYS, 256, kind=F32),
            shape(SLOTS, 16, HEAD_DIM),
        ],
        in_specs=[spec(pltpu.VMEM)] * 2 + [spec(pl.ANY)],
        out_specs=[spec(pltpu.VMEM)] * 3,
        cost_estimate=work_cost(5),
        compiler_params=params(24),
    )(own, other, in_hbm(near[0]))
    results = pl.pallas_call(
        other_work_kernel,
        out_shape=shape(SLOTS, MID_ROWS, 3 * HEAD_DIM),
        in_specs=[spec(pltpu.VMEM)] * 6,
        out_specs=spec(pltpu.VMEM),
        cost_estimate=work_cost(4),
        compiler_params=params(24),
    )(own, other, other_queries, dq, own_sums, wide_rows)
    returned = lax.all_to_all(results, "inner", 0, 0, axis_index_groups=ALONG_Z)
    return tuple(
        pl.pallas_call(
            assemble_kernel,
            out_shape=[shape(TOK, HIDDEN)] * 3,
            in_specs=[spec(pltpu.VMEM)] * 2 + [spec(pltpu.HBM)] * 3,
            out_specs=[spec(pltpu.HBM)] * 3,
            scratch_shapes=[
                pltpu.VMEM((3, heads, TOK, HEAD_DIM), BF16),
                pltpu.SemaphoreType.DMA((3, heads)),
            ],
            input_output_aliases={2: 0, 3: 1, 4: 2},
            compiler_params=params(16),
        )(offset_rows, returned, *near)
    )


def solution(mesh):
    rows = P(("outer", "inner"), None)
    return jax.shard_map(
        body,
        mesh=mesh,
        in_specs=(rows, rows, rows, rows, P()),
        out_specs=(rows, rows, rows),
        check_vma=False,
    )
```

```python
import functools
import math

import jax
import jax.numpy as jnp
from jax import lax
from jax.experimental import pallas as pl
from jax.experimental.pallas import tpu as pltpu
from jax.sharding import PartitionSpec as P

HEAD_DIM = 128
H_NEAR = 4
H_MID = 5
H_WIDE = 3
R_MID = 4
R_WIDE = 128
TOK = 256
NEAR_END = H_NEAR * HEAD_DIM
MID_END = NEAR_END + H_MID * HEAD_DIM
HIDDEN = MID_END + H_WIDE * HEAD_DIM
OUTERS = 16
MID_ROWS = TOK // R_MID
SLOTS = 8
HALVES = 2
HALF_KEYS = SLOTS * MID_ROWS
Z_IN = (5, 6, 7, 3, 4, 1, 2, 0)
Z_OUT = (5, 6, 7, 3, 4, 1, 2, 0)
OUTER_ORDER = tuple(range(OUTERS - 1, -1, -1))
ALONG_Z_IN = [[HALVES * z + half for z in Z_IN] for half in range(HALVES)]
ALONG_Z_OUT = [[HALVES * z + half for z in Z_OUT] for half in range(HALVES)]
OUT_FROM_IN = [Z_IN.index(z) for z in Z_OUT]
ACROSS_Y = [(member, member ^ 1) for member in range(HALVES * SLOTS)]
SCALE = 1.0 / math.sqrt(HEAD_DIM)
EARLY_NEAR = (range(3), range(0))
LATE_NEAR = tuple(range(len(early), H_NEAR) for early in EARLY_NEAR)
EXP2_SCALE = SCALE * math.log2(math.e)
BF16 = jnp.bfloat16
F32 = jnp.float32


def dot(a, b):
    return lax.dot_general(a, b, (((1,), (0,)), ((), ())), preferred_element_type=F32)


def dot_nt(a, b):
    return lax.dot_general(a, b, (((1,), (1,)), ((), ())), preferred_element_type=F32)


def dot_tn(a, b):
    return lax.dot_general(a, b, (((0,), (0,)), ((), ())), preferred_element_type=F32)


def iota2(rows, columns):
    shape = (rows, columns)
    return (
        lax.broadcasted_iota(jnp.int32, shape, 0),
        lax.broadcasted_iota(jnp.int32, shape, 1),
    )


def one_hot(condition):
    return jnp.where(condition, 1.0, 0.0).astype(BF16)


def scaled_weights(parts, query, gradient):
    scores = [dot_nt(key, query) for key, unused in parts]
    top = functools.reduce(jnp.maximum, [jnp.max(s, axis=0, keepdims=True) for s in scores])
    exponents = [jnp.exp2((s - top) * EXP2_SCALE) for s in scores]
    inverse = 1.0 / sum(jnp.sum(e, axis=0, keepdims=True) for e in exponents)
    products = [dot_nt(value, gradient) for unused, value in parts]
    row_dots = inverse * sum(
        jnp.sum(e * p, axis=0, keepdims=True) for e, p in zip(exponents, products)
    )
    weights = exponents[0] * inverse
    score_gradients = weights * (products[0] - row_dots) * SCALE
    return weights.astype(BF16), score_gradients.astype(BF16)


def attention_transposed(query, key, value, gradient):
    return scaled_weights([(key, value)], query, gradient)


def fetch(sources, held, sems, heads, first=NEAR_END):
    copies = {}
    for at, head in enumerate(heads):
        for which, source in enumerate(sources):
            copies[head, which] = pltpu.make_async_copy(
                source.at[:, pl.ds(first + head * HEAD_DIM, HEAD_DIM)],
                held.at[which, at],
                sems.at[which, at],
            )
            copies[head, which].start()
    return copies


def pairs(copies, held, head, at):
    for which in range(4):
        copies[head, which].wait()
    kv = jnp.concatenate([held[1, at], held[2, at]], axis=1)
    qg = jnp.concatenate([held[0, at], held[3, at]], axis=1)
    return kv, qg


def wide_kernel(off_hbm, q_hbm, k_hbm, v_hbm, g_hbm, out_ref, off_out, off_ref, held, off_sem, sems):
    off_copy = pltpu.make_async_copy(off_hbm, off_ref, off_sem)
    off_copy.start()
    heads = range(H_MID, H_MID + H_WIDE)
    copies = fetch((q_hbm, k_hbm, v_hbm, g_hbm), held, sems, heads)
    off_copy.wait()
    for head in range(H_MID + H_WIDE):
        off_out[head : head + 1, :] = jnp.full((1, TOK), off_ref[head], jnp.int32)
    row, unused = iota2(16, HEAD_DIM)
    row_pair, unused = iota2(16, 2 * HEAD_DIM)
    rows = jnp.zeros((16, 2 * HEAD_DIM), F32)
    for at, head in enumerate(heads):
        offset = off_ref[head]
        base, place = lax.div(offset, 16) * 16, lax.rem(offset, 16)
        for which in range(4):
            copies[head, which].wait()
        for again in range(2):
            tile = pl.ds(pl.multiple_of(base + again * R_WIDE, 16), 16)
            picked = [
                jnp.sum(
                    jnp.where(row == place, held[which, at, tile, :].astype(F32), 0.0),
                    axis=0,
                    keepdims=True,
                )
                for which in range(4)
            ]
            kv = jnp.concatenate([picked[1], picked[2]], axis=1)
            qg = jnp.concatenate([picked[0], picked[3]], axis=1)
            rows = jnp.where(row_pair == 2 * at + again, kv, rows)
            rows = jnp.where(row_pair == 6 + 2 * at + again, qg, rows)
    rows = rows.astype(BF16)
    for target in range(OUTERS):
        out_ref[target] = rows


def mid_pack_kernel(off_ref, q_hbm, k_hbm, v_hbm, g_hbm, out_ref, held, sems):
    copies = fetch((q_hbm, k_hbm, v_hbm, g_hbm), held, sems, range(H_MID))
    row, column = iota2(MID_ROWS, TOK)
    for head in range(H_MID):
        pick = one_hot(column - R_MID * row == off_ref[head : head + 1, :])
        kv, qg = pairs(copies, held, head, head)
        out_ref[head, 0:64, :] = dot(pick, kv).astype(BF16)
        out_ref[head, 64:128, :] = dot(pick, qg).astype(BF16)
    for head in range(H_MID, SLOTS):
        out_ref[head, 64:128, :] = jnp.zeros((64, 2 * HEAD_DIM), BF16)


def wide_pack_kernel(got_ref, packed, after, out_ref):
    rows = got_ref[...].reshape(OUTERS * 16, 2 * HEAD_DIM)
    row, column = iota2(64, OUTERS * 16)
    base = 16 * ((row % 32) // 2) + row % 2 + jnp.where(row < 32, 0, 6)
    for head in range(H_WIDE):
        picked = dot(one_hot(column == base + 2 * head), rows)
        out_ref[H_MID + head, 0:64, :] = picked.astype(BF16)


def near_some(sources, targets, held, results, sems, out_sems, heads):
    copies = fetch(sources, held, sems, heads, 0)
    sends = []
    for at, head in enumerate(heads):
        for which in range(4):
            copies[head, which].wait()
        query, key, value, gradient = (held[which, at] for which in range(4))
        weights, score_gradients = attention_transposed(query, key, value, gradient)
        results[0, at] = dot_tn(score_gradients, key).astype(BF16)
        results[1, at] = dot(score_gradients, query).astype(BF16)
        results[2, at] = dot(weights, gradient).astype(BF16)
        for which, target in enumerate(targets):
            send = pltpu.make_async_copy(
                results.at[which, at],
                target.at[:, pl.ds(head * HEAD_DIM, HEAD_DIM)],
                out_sems.at[which, at],
            )
            send.start()
            sends.append(send)
    for send in sends:
        send.wait()


def near_kernel(heads_of_core, after, q_hbm, k_hbm, v_hbm, g_hbm, *rest):
    targets, (held, results, sems, out_sems) = rest[-7:-4], rest[-4:]
    for core, heads in enumerate(heads_of_core):
        if heads:

            @pl.when(lax.rem(lax.axis_index("outer"), 2) == core)
            def attend(heads=heads):
                sources = (q_hbm, k_hbm, v_hbm, g_hbm)
                near_some(sources, targets, held, results, sems, out_sems, heads)


def near_heads(heads_of_core, after, arrays, previous=()):
    return pl.pallas_call(
        functools.partial(near_kernel, heads_of_core),
        out_shape=[shape(TOK, HIDDEN)] * 3,
        in_specs=[spec(pl.ANY)] + [spec(pltpu.HBM)] * (4 + len(previous)),
        out_specs=[spec(pltpu.HBM)] * 3,
        scratch_shapes=[
            pltpu.VMEM((4, H_NEAR, TOK, HEAD_DIM), BF16),
            pltpu.VMEM((3, H_NEAR, TOK, HEAD_DIM), BF16),
            pltpu.SemaphoreType.DMA((4, H_NEAR)),
            pltpu.SemaphoreType.DMA((3, H_NEAR)),
        ],
        input_output_aliases={5 + which: which for which in range(len(previous))},
        cost_estimate=pl.CostEstimate(
            flops=10 * H_NEAR * TOK * TOK * HEAD_DIM,
            bytes_accessed=14 * TOK * NEAR_END,
            transcendentals=H_NEAR * TOK * TOK,
        ),
        compiler_params=params(16),
    )(after, *arrays, *previous)


def place_in(order, index):
    return sum(jnp.where(index == member, at, 0) for at, member in enumerate(order))


def slot():
    return place_in(Z_IN, lax.div(lax.axis_index("inner"), HALVES))


def attend_wide(own_ref, other_ref, out_ref):
    wide_rows = SLOTS * 32
    kv = [ref[:, 0:32, :].reshape(wide_rows, 2 * HEAD_DIM) for ref in (own_ref, other_ref)]
    qg = [ref[:, 32:64, :].reshape(wide_rows, 2 * HEAD_DIM) for ref in (own_ref, other_ref)]
    row, column = iota2(16, wide_rows)
    source = 32 * (row // 2) + 2 * place_in(OUTER_ORDER, lax.axis_index("outer")) + row % 2
    pick = one_hot(column == source)
    own_kv, own_qg = dot(pick, kv[0]).astype(BF16), dot(pick, qg[0]).astype(BF16)
    kv, qg = jnp.concatenate(kv, axis=0), jnp.concatenate(qg, axis=0)
    key, value = kv[:, :HEAD_DIM], kv[:, HEAD_DIM:]
    query, gradient = qg[:, :HEAD_DIM], qg[:, HEAD_DIM:]
    scores = dot_nt(key, query) * SCALE
    top = jnp.max(scores, axis=0, keepdims=True)
    exponent = jnp.exp(scores - top)
    inverse = 1.0 / jnp.sum(exponent, axis=0, keepdims=True)
    products = dot_nt(value, gradient)
    row_dots = jnp.sum(exponent * inverse * products, axis=0, keepdims=True)
    own_key, own_value = own_kv[:, :HEAD_DIM], own_kv[:, HEAD_DIM:]
    own_query, own_gradient = own_qg[:, :HEAD_DIM], own_qg[:, HEAD_DIM:]
    weights = jnp.exp(dot_nt(own_key, query) * SCALE - top) * inverse
    score_gradients = weights * (dot_nt(own_value, gradient) - row_dots) * SCALE
    dk = dot(score_gradients.astype(BF16), query).astype(BF16)
    dv = dot(weights.astype(BF16), gradient).astype(BF16)
    scores = dot_nt(own_query, key) * SCALE
    exponent = jnp.exp(scores - jnp.max(scores, axis=1, keepdims=True))
    weights = exponent * (1.0 / jnp.sum(exponent, axis=1, keepdims=True))
    products = dot_nt(own_gradient, value)
    row_dots = jnp.sum(weights * products, axis=1, keepdims=True)
    score_gradients = weights * (products - row_dots) * SCALE
    dq = dot(score_gradients.astype(BF16), key).astype(BF16)
    row, column = iota2(SLOTS * 16, 16)
    member, place = row // 16, row % 16
    spread = 0.0
    for which, rows in enumerate((dq, dk, dv)):
        mine = (place >= 2 * which) & (place < 2 * which + 2)
        spread += dot(one_hot(mine & (column == 2 * member + place - 2 * which)), rows)
    out_ref[...] = spread.astype(BF16).reshape(SLOTS, 16, HEAD_DIM)


def halves(ref, rows):
    block = ref[:, rows, :].reshape(HALF_KEYS, 2 * HEAD_DIM)
    return block[:, :HEAD_DIM], block[:, HEAD_DIM:]


def own_work_kernel(own_ref, other_ref, after, dq_ref, dkv_ref, wide_out):
    @pl.when(slot() >= H_MID)
    def wide():
        attend_wide(own_ref, other_ref, wide_out)

    @pl.when(slot() < H_MID)
    def attend():
        parts = [halves(own_ref, slice(0, 64)), halves(other_ref, slice(0, 64))]
        key, value = (jnp.concatenate(pieces, axis=0) for pieces in zip(*parts))
        query, gradient = halves(own_ref, slice(64, 128))
        weights, score_gradients = attention_transposed(query, key, value, gradient)
        dkv_ref[:, :HEAD_DIM] = dot(score_gradients[:HALF_KEYS], query)
        dkv_ref[:, HEAD_DIM:] = dot(weights[:HALF_KEYS], gradient)
        dq = dot_tn(key, score_gradients).T.astype(BF16)
        dq_ref[...] = dq.reshape(SLOTS, MID_ROWS, HEAD_DIM)


def other_work_kernel(own_ref, other_ref, query_ref, dq_ref, dkv_ref, wide_ref, out_ref):
    @pl.when(slot() < H_MID)
    def attend():
        parts = [halves(own_ref, slice(0, 64)), halves(other_ref, slice(0, 64))]
        query, gradient = halves(query_ref, slice(0, 64))
        weights, score_gradients = scaled_weights(parts, query, gradient)
        dk = dkv_ref[:, :HEAD_DIM] + dot(score_gradients, query)
        dv = dkv_ref[:, HEAD_DIM:] + dot(weights, gradient)
        dk, dv = (sums.astype(BF16).reshape(SLOTS, MID_ROWS, HEAD_DIM) for sums in (dk, dv))
        for at, member in enumerate(OUT_FROM_IN):
            out_ref[at, :, :HEAD_DIM] = dq_ref[member]
            out_ref[at, :, HEAD_DIM : 2 * HEAD_DIM] = dk[member]
            out_ref[at, :, 2 * HEAD_DIM :] = dv[member]

    @pl.when(slot() >= H_MID)
    def wide():
        for at, member in enumerate(OUT_FROM_IN):
            out_ref[at, 0:16, :HEAD_DIM] = wide_ref[member]


def assemble_kernel(off_ref, got_ref, nq, nk, nv, dq_hbm, dk_hbm, dv_hbm, held, sems):
    copies = []

    def send(which, head, block):
        held[which, head] = block.astype(BF16)
        target = (dq_hbm, dk_hbm, dv_hbm)[which]
        copy = pltpu.make_async_copy(
            held.at[which, head],
            target.at[:, pl.ds(NEAR_END + head * HEAD_DIM, HEAD_DIM)],
            sems.at[which, head],
        )
        copy.start()
        copies.append(copy)

    row, unused = iota2(TOK, HEAD_DIM)
    for head in range(H_MID, H_MID + H_WIDE):
        offset = off_ref[head : head + 1, :HEAD_DIM]
        rows = got_ref[OUT_FROM_IN.index(head), 0:16, :HEAD_DIM].astype(F32)
        first, second = row == offset, row == offset + R_WIDE
        for which in range(3):
            spread = jnp.where(first, rows[2 * which : 2 * which + 1], 0.0)
            send(which, head, jnp.where(second, rows[2 * which + 1 : 2 * which + 2], spread))
    row, column = iota2(TOK, MID_ROWS)
    for head in range(H_MID):
        place = one_hot(row - R_MID * column == off_ref[head : head + 1, :1])
        spread = dot(place, got_ref[OUT_FROM_IN.index(head)])
        for which in range(3):
            send(which, head, spread[:, which * HEAD_DIM : (which + 1) * HEAD_DIM])
    for copy in copies:
        copy.wait()


def spec(space):
    return pl.BlockSpec(memory_space=space)


def in_hbm(array):
    return pltpu.with_memory_space_constraint(array, pltpu.HBM)


def params(mebibytes):
    return pltpu.CompilerParams(vmem_limit_bytes=mebibytes * 1024 * 1024)


def shape(*sizes, kind=BF16):
    return jax.ShapeDtypeStruct(sizes, kind)


def work_cost(products):
    return pl.CostEstimate(
        flops=products * 4 * HALF_KEYS * HALF_KEYS * HEAD_DIM,
        bytes_accessed=0,
        transcendentals=2 * HALF_KEYS * HALF_KEYS,
    )


def body(queries, key_rows, values, out_grads, offsets):
    arrays = [in_hbm(array) for array in (queries, key_rows, values, out_grads)]
    heads = H_MID + H_WIDE
    wide_send, offset_rows = pl.pallas_call(
        wide_kernel,
        out_shape=[shape(OUTERS, 16, 256), shape(heads, TOK, kind=jnp.int32)],
        in_specs=[spec(pltpu.HBM)] * 5,
        out_specs=[spec(pltpu.VMEM)] * 2,
        scratch_shapes=[
            pltpu.SMEM((heads,), jnp.int32),
            pltpu.VMEM((4, H_WIDE, TOK, HEAD_DIM), BF16),
            pltpu.SemaphoreType.DMA,
            pltpu.SemaphoreType.DMA((4, H_WIDE)),
        ],
        compiler_params=params(8),
    )(in_hbm(offsets), *arrays)
    wide_got = lax.all_to_all(wide_send, "outer", 0, 0, axis_index_groups=[list(OUTER_ORDER)])
    packed = pl.pallas_call(
        mid_pack_kernel,
        out_shape=shape(SLOTS, 128, 256),
        in_specs=[spec(pltpu.VMEM)] + [spec(pltpu.HBM)] * 4,
        out_specs=spec(pltpu.VMEM),
        scratch_shapes=[
            pltpu.VMEM((4, H_MID, TOK, HEAD_DIM), BF16),
            pltpu.SemaphoreType.DMA((4, H_MID)),
        ],
        cost_estimate=pl.CostEstimate(
            flops=8 * H_MID * MID_ROWS * TOK * HEAD_DIM,
            bytes_accessed=8 * H_MID * TOK * HEAD_DIM,
            transcendentals=0,
        ),
        compiler_params=params(8),
    )(offset_rows, *arrays)
    near = near_heads(EARLY_NEAR, wide_got, arrays)
    packed = pl.pallas_call(
        wide_pack_kernel,
        out_shape=shape(SLOTS, 128, 256),
        in_specs=[spec(pltpu.VMEM), spec(pltpu.VMEM), spec(pl.ANY)],
        out_specs=spec(pltpu.VMEM),
        input_output_aliases={1: 0},
        compiler_params=params(8),
    )(wide_got, packed, in_hbm(near[0]))
    own = lax.all_to_all(packed, "inner", 0, 0, axis_index_groups=ALONG_Z_IN)
    other = lax.ppermute(own[:, 0:64, :], "inner", ACROSS_Y)
    other_queries = lax.ppermute(own[:, 64:128, :], "inner", ACROSS_Y)
    near = near_heads(LATE_NEAR, own, arrays, near)
    dq, own_sums, wide_rows = pl.pallas_call(
        own_work_kernel,
        out_shape=[
            shape(SLOTS, MID_ROWS, HEAD_DIM),
            shape(HALF_KEYS, 256, kind=F32),
            shape(SLOTS, 16, HEAD_DIM),
        ],
        in_specs=[spec(pltpu.VMEM)] * 2 + [spec(pl.ANY)],
        out_specs=[spec(pltpu.VMEM)] * 3,
        cost_estimate=work_cost(5),
        compiler_params=params(24),
    )(own, other, in_hbm(near[0]))
    results = pl.pallas_call(
        other_work_kernel,
        out_shape=shape(SLOTS, MID_ROWS, 3 * HEAD_DIM),
        in_specs=[spec(pltpu.VMEM)] * 6,
        out_specs=spec(pltpu.VMEM),
        cost_estimate=work_cost(4),
        compiler_params=params(24),
    )(own, other, other_queries, dq, own_sums, wide_rows)
    returned = lax.all_to_all(results, "inner", 0, 0, axis_index_groups=ALONG_Z_OUT)
    return tuple(
        pl.pallas_call(
            assemble_kernel,
            out_shape=[shape(TOK, HIDDEN)] * 3,
            in_specs=[spec(pltpu.VMEM)] * 2 + [spec(pltpu.HBM)] * 3,
            out_specs=[spec(pltpu.HBM)] * 3,
            scratch_shapes=[
                pltpu.VMEM((3, heads, TOK, HEAD_DIM), BF16),
                pltpu.SemaphoreType.DMA((3, heads)),
            ],
            input_output_aliases={2: 0, 3: 1, 4: 2},
            compiler_params=params(16),
        )(offset_rows, returned, *near)
    )


def solution(mesh):
    rows = P(("outer", "inner"), None)
    return jax.shard_map(
        body,
        mesh=mesh,
        in_specs=(rows, rows, rows, rows, P()),
        out_specs=(rows, rows, rows),
        check_vma=False,
    )
```

```python
import functools
import math

import jax
import jax.numpy as jnp
from jax import lax
from jax.experimental import pallas as pl
from jax.experimental.pallas import tpu as pltpu
from jax.sharding import PartitionSpec as P

HEAD_DIM = 128
H_NEAR = 4
H_MID = 5
H_WIDE = 3
R_MID = 4
R_WIDE = 128
TOK = 256
NEAR_END = H_NEAR * HEAD_DIM
MID_END = NEAR_END + H_MID * HEAD_DIM
HIDDEN = MID_END + H_WIDE * HEAD_DIM
OUTERS = 16
MID_ROWS = TOK // R_MID
SLOTS = 8
HALVES = 2
HALF_KEYS = SLOTS * MID_ROWS
Z_IN = (4, 5, 6, 2, 3, 0, 1, 7)
Z_OUT = (4, 5, 6, 2, 3, 0, 1, 7)
OUTER_ORDER = tuple(range(OUTERS - 1, -1, -1))
ALONG_Z_IN = [[HALVES * z + half for z in Z_IN] for half in range(HALVES)]
ALONG_Z_OUT = [[HALVES * z + half for z in Z_OUT] for half in range(HALVES)]
OUT_FROM_IN = [Z_IN.index(z) for z in Z_OUT]
ACROSS_Y = [(member, member ^ 1) for member in range(HALVES * SLOTS)]
SCALE = 1.0 / math.sqrt(HEAD_DIM)
EARLY_NEAR = (range(3), range(0))
LATE_NEAR = tuple(range(len(early), H_NEAR) for early in EARLY_NEAR)
EXP2_SCALE = SCALE * math.log2(math.e)
BF16 = jnp.bfloat16
F32 = jnp.float32


def dot(a, b):
    return lax.dot_general(a, b, (((1,), (0,)), ((), ())), preferred_element_type=F32)


def dot_nt(a, b):
    return lax.dot_general(a, b, (((1,), (1,)), ((), ())), preferred_element_type=F32)


def dot_tn(a, b):
    return lax.dot_general(a, b, (((0,), (0,)), ((), ())), preferred_element_type=F32)


def iota2(rows, columns):
    shape = (rows, columns)
    return (
        lax.broadcasted_iota(jnp.int32, shape, 0),
        lax.broadcasted_iota(jnp.int32, shape, 1),
    )


def one_hot(condition):
    return jnp.where(condition, 1.0, 0.0).astype(BF16)


def scaled_weights(parts, query, gradient):
    scores = [dot_nt(key, query) for key, unused in parts]
    top = functools.reduce(jnp.maximum, [jnp.max(s, axis=0, keepdims=True) for s in scores])
    exponents = [jnp.exp2((s - top) * EXP2_SCALE) for s in scores]
    inverse = 1.0 / sum(jnp.sum(e, axis=0, keepdims=True) for e in exponents)
    products = [dot_nt(value, gradient) for unused, value in parts]
    row_dots = inverse * sum(
        jnp.sum(e * p, axis=0, keepdims=True) for e, p in zip(exponents, products)
    )
    weights = exponents[0] * inverse
    score_gradients = weights * (products[0] - row_dots) * SCALE
    return weights.astype(BF16), score_gradients.astype(BF16)


def attention_transposed(query, key, value, gradient):
    return scaled_weights([(key, value)], query, gradient)


def fetch(sources, held, sems, heads, first=NEAR_END):
    copies = {}
    for at, head in enumerate(heads):
        for which, source in enumerate(sources):
            copies[head, which] = pltpu.make_async_copy(
                source.at[:, pl.ds(first + head * HEAD_DIM, HEAD_DIM)],
                held.at[which, at],
                sems.at[which, at],
            )
            copies[head, which].start()
    return copies


def pairs(copies, held, head, at):
    for which in range(4):
        copies[head, which].wait()
    kv = jnp.concatenate([held[1, at], held[2, at]], axis=1)
    qg = jnp.concatenate([held[0, at], held[3, at]], axis=1)
    return kv, qg


def wide_kernel(off_hbm, q_hbm, k_hbm, v_hbm, g_hbm, out_ref, off_out, off_ref, held, off_sem, sems):
    off_copy = pltpu.make_async_copy(off_hbm, off_ref, off_sem)
    off_copy.start()
    heads = range(H_MID, H_MID + H_WIDE)
    copies = fetch((q_hbm, k_hbm, v_hbm, g_hbm), held, sems, heads)
    off_copy.wait()
    for head in range(H_MID + H_WIDE):
        off_out[head : head + 1, :] = jnp.full((1, TOK), off_ref[head], jnp.int32)
    row, unused = iota2(16, HEAD_DIM)
    row_pair, unused = iota2(16, 2 * HEAD_DIM)
    rows = jnp.zeros((16, 2 * HEAD_DIM), F32)
    for at, head in enumerate(heads):
        offset = off_ref[head]
        base, place = lax.div(offset, 16) * 16, lax.rem(offset, 16)
        for which in range(4):
            copies[head, which].wait()
        for again in range(2):
            tile = pl.ds(pl.multiple_of(base + again * R_WIDE, 16), 16)
            picked = [
                jnp.sum(
                    jnp.where(row == place, held[which, at, tile, :].astype(F32), 0.0),
                    axis=0,
                    keepdims=True,
                )
                for which in range(4)
            ]
            kv = jnp.concatenate([picked[1], picked[2]], axis=1)
            qg = jnp.concatenate([picked[0], picked[3]], axis=1)
            rows = jnp.where(row_pair == 2 * at + again, kv, rows)
            rows = jnp.where(row_pair == 6 + 2 * at + again, qg, rows)
    rows = rows.astype(BF16)
    for target in range(OUTERS):
        out_ref[target] = rows


def mid_pack_kernel(off_ref, q_hbm, k_hbm, v_hbm, g_hbm, out_ref, held, sems):
    copies = fetch((q_hbm, k_hbm, v_hbm, g_hbm), held, sems, range(H_MID))
    row, column = iota2(MID_ROWS, TOK)
    for head in range(H_MID):
        pick = one_hot(column - R_MID * row == off_ref[head : head + 1, :])
        kv, qg = pairs(copies, held, head, head)
        out_ref[head, 0:64, :] = dot(pick, kv).astype(BF16)
        out_ref[head, 64:128, :] = dot(pick, qg).astype(BF16)
    for head in range(H_MID, SLOTS):
        out_ref[head, 64:128, :] = jnp.zeros((64, 2 * HEAD_DIM), BF16)


def wide_pack_kernel(got_ref, packed, after, out_ref):
    rows = got_ref[...].reshape(OUTERS * 16, 2 * HEAD_DIM)
    row, column = iota2(64, OUTERS * 16)
    base = 16 * ((row % 32) // 2) + row % 2 + jnp.where(row < 32, 0, 6)
    for head in range(H_WIDE):
        picked = dot(one_hot(column == base + 2 * head), rows)
        out_ref[H_MID + head, 0:64, :] = picked.astype(BF16)


def near_some(sources, targets, held, results, sems, out_sems, heads):
    copies = fetch(sources, held, sems, heads, 0)
    sends = []
    for at, head in enumerate(heads):
        for which in range(4):
            copies[head, which].wait()
        query, key, value, gradient = (held[which, at] for which in range(4))
        weights, score_gradients = attention_transposed(query, key, value, gradient)
        results[0, at] = dot_tn(score_gradients, key).astype(BF16)
        results[1, at] = dot(score_gradients, query).astype(BF16)
        results[2, at] = dot(weights, gradient).astype(BF16)
        for which, target in enumerate(targets):
            send = pltpu.make_async_copy(
                results.at[which, at],
                target.at[:, pl.ds(head * HEAD_DIM, HEAD_DIM)],
                out_sems.at[which, at],
            )
            send.start()
            sends.append(send)
    for send in sends:
        send.wait()


def near_kernel(heads_of_core, after, q_hbm, k_hbm, v_hbm, g_hbm, *rest):
    targets, (held, results, sems, out_sems) = rest[-7:-4], rest[-4:]
    for core, heads in enumerate(heads_of_core):
        if heads:

            @pl.when(lax.rem(lax.axis_index("outer"), 2) == core)
            def attend(heads=heads):
                sources = (q_hbm, k_hbm, v_hbm, g_hbm)
                near_some(sources, targets, held, results, sems, out_sems, heads)


def near_heads(heads_of_core, after, arrays, previous=()):
    return pl.pallas_call(
        functools.partial(near_kernel, heads_of_core),
        out_shape=[shape(TOK, HIDDEN)] * 3,
        in_specs=[spec(pl.ANY)] + [spec(pltpu.HBM)] * (4 + len(previous)),
        out_specs=[spec(pltpu.HBM)] * 3,
        scratch_shapes=[
            pltpu.VMEM((4, H_NEAR, TOK, HEAD_DIM), BF16),
            pltpu.VMEM((3, H_NEAR, TOK, HEAD_DIM), BF16),
            pltpu.SemaphoreType.DMA((4, H_NEAR)),
            pltpu.SemaphoreType.DMA((3, H_NEAR)),
        ],
        input_output_aliases={5 + which: which for which in range(len(previous))},
        cost_estimate=pl.CostEstimate(
            flops=10 * H_NEAR * TOK * TOK * HEAD_DIM,
            bytes_accessed=14 * TOK * NEAR_END,
            transcendentals=H_NEAR * TOK * TOK,
        ),
        compiler_params=params(16),
    )(after, *arrays, *previous)


def place_in(order, index):
    return sum(jnp.where(index == member, at, 0) for at, member in enumerate(order))


def slot():
    return place_in(Z_IN, lax.div(lax.axis_index("inner"), HALVES))


def attend_wide(own_ref, other_ref, out_ref):
    wide_rows = SLOTS * 32
    kv = [ref[:, 0:32, :].reshape(wide_rows, 2 * HEAD_DIM) for ref in (own_ref, other_ref)]
    qg = [ref[:, 32:64, :].reshape(wide_rows, 2 * HEAD_DIM) for ref in (own_ref, other_ref)]
    row, column = iota2(16, wide_rows)
    source = 32 * (row // 2) + 2 * place_in(OUTER_ORDER, lax.axis_index("outer")) + row % 2
    pick = one_hot(column == source)
    own_kv, own_qg = dot(pick, kv[0]).astype(BF16), dot(pick, qg[0]).astype(BF16)
    kv, qg = jnp.concatenate(kv, axis=0), jnp.concatenate(qg, axis=0)
    key, value = kv[:, :HEAD_DIM], kv[:, HEAD_DIM:]
    query, gradient = qg[:, :HEAD_DIM], qg[:, HEAD_DIM:]
    scores = dot_nt(key, query) * SCALE
    top = jnp.max(scores, axis=0, keepdims=True)
    exponent = jnp.exp(scores - top)
    inverse = 1.0 / jnp.sum(exponent, axis=0, keepdims=True)
    products = dot_nt(value, gradient)
    row_dots = jnp.sum(exponent * inverse * products, axis=0, keepdims=True)
    own_key, own_value = own_kv[:, :HEAD_DIM], own_kv[:, HEAD_DIM:]
    own_query, own_gradient = own_qg[:, :HEAD_DIM], own_qg[:, HEAD_DIM:]
    weights = jnp.exp(dot_nt(own_key, query) * SCALE - top) * inverse
    score_gradients = weights * (dot_nt(own_value, gradient) - row_dots) * SCALE
    dk = dot(score_gradients.astype(BF16), query).astype(BF16)
    dv = dot(weights.astype(BF16), gradient).astype(BF16)
    scores = dot_nt(own_query, key) * SCALE
    exponent = jnp.exp(scores - jnp.max(scores, axis=1, keepdims=True))
    weights = exponent * (1.0 / jnp.sum(exponent, axis=1, keepdims=True))
    products = dot_nt(own_gradient, value)
    row_dots = jnp.sum(weights * products, axis=1, keepdims=True)
    score_gradients = weights * (products - row_dots) * SCALE
    dq = dot(score_gradients.astype(BF16), key).astype(BF16)
    row, column = iota2(SLOTS * 16, 16)
    member, place = row // 16, row % 16
    spread = 0.0
    for which, rows in enumerate((dq, dk, dv)):
        mine = (place >= 2 * which) & (place < 2 * which + 2)
        spread += dot(one_hot(mine & (column == 2 * member + place - 2 * which)), rows)
    out_ref[...] = spread.astype(BF16).reshape(SLOTS, 16, HEAD_DIM)


def halves(ref, rows):
    block = ref[:, rows, :].reshape(HALF_KEYS, 2 * HEAD_DIM)
    return block[:, :HEAD_DIM], block[:, HEAD_DIM:]


def own_work_kernel(own_ref, other_ref, after, dq_ref, dkv_ref, wide_out):
    @pl.when(slot() >= H_MID)
    def wide():
        attend_wide(own_ref, other_ref, wide_out)

    @pl.when(slot() < H_MID)
    def attend():
        parts = [halves(own_ref, slice(0, 64)), halves(other_ref, slice(0, 64))]
        key, value = (jnp.concatenate(pieces, axis=0) for pieces in zip(*parts))
        query, gradient = halves(own_ref, slice(64, 128))
        weights, score_gradients = attention_transposed(query, key, value, gradient)
        dkv_ref[:, :HEAD_DIM] = dot(score_gradients[:HALF_KEYS], query)
        dkv_ref[:, HEAD_DIM:] = dot(weights[:HALF_KEYS], gradient)
        dq = dot_tn(key, score_gradients).T.astype(BF16)
        dq_ref[...] = dq.reshape(SLOTS, MID_ROWS, HEAD_DIM)


def other_work_kernel(own_ref, other_ref, query_ref, dq_ref, dkv_ref, wide_ref, out_ref):
    @pl.when(slot() < H_MID)
    def attend():
        parts = [halves(own_ref, slice(0, 64)), halves(other_ref, slice(0, 64))]
        query, gradient = halves(query_ref, slice(0, 64))
        weights, score_gradients = scaled_weights(parts, query, gradient)
        dk = dkv_ref[:, :HEAD_DIM] + dot(score_gradients, query)
        dv = dkv_ref[:, HEAD_DIM:] + dot(weights, gradient)
        dk, dv = (sums.astype(BF16).reshape(SLOTS, MID_ROWS, HEAD_DIM) for sums in (dk, dv))
        for at, member in enumerate(OUT_FROM_IN):
            out_ref[at, :, :HEAD_DIM] = dq_ref[member]
            out_ref[at, :, HEAD_DIM : 2 * HEAD_DIM] = dk[member]
            out_ref[at, :, 2 * HEAD_DIM :] = dv[member]

    @pl.when(slot() >= H_MID)
    def wide():
        for at, member in enumerate(OUT_FROM_IN):
            out_ref[at, 0:16, :HEAD_DIM] = wide_ref[member]


def assemble_kernel(off_ref, got_ref, nq, nk, nv, dq_hbm, dk_hbm, dv_hbm, held, sems):
    copies = []

    def send(which, head, block):
        held[which, head] = block.astype(BF16)
        target = (dq_hbm, dk_hbm, dv_hbm)[which]
        copy = pltpu.make_async_copy(
            held.at[which, head],
            target.at[:, pl.ds(NEAR_END + head * HEAD_DIM, HEAD_DIM)],
            sems.at[which, head],
        )
        copy.start()
        copies.append(copy)

    row, unused = iota2(TOK, HEAD_DIM)
    for head in range(H_MID, H_MID + H_WIDE):
        offset = off_ref[head : head + 1, :HEAD_DIM]
        rows = got_ref[OUT_FROM_IN.index(head), 0:16, :HEAD_DIM].astype(F32)
        first, second = row == offset, row == offset + R_WIDE
        for which in range(3):
            spread = jnp.where(first, rows[2 * which : 2 * which + 1], 0.0)
            send(which, head, jnp.where(second, rows[2 * which + 1 : 2 * which + 2], spread))
    row, column = iota2(TOK, MID_ROWS)
    for head in range(H_MID):
        place = one_hot(row - R_MID * column == off_ref[head : head + 1, :1])
        spread = dot(place, got_ref[OUT_FROM_IN.index(head)])
        for which in range(3):
            send(which, head, spread[:, which * HEAD_DIM : (which + 1) * HEAD_DIM])
    for copy in copies:
        copy.wait()


def spec(space):
    return pl.BlockSpec(memory_space=space)


def in_hbm(array):
    return pltpu.with_memory_space_constraint(array, pltpu.HBM)


def params(mebibytes):
    return pltpu.CompilerParams(vmem_limit_bytes=mebibytes * 1024 * 1024)


def shape(*sizes, kind=BF16):
    return jax.ShapeDtypeStruct(sizes, kind)


def work_cost(products):
    return pl.CostEstimate(
        flops=products * 4 * HALF_KEYS * HALF_KEYS * HEAD_DIM,
        bytes_accessed=0,
        transcendentals=2 * HALF_KEYS * HALF_KEYS,
    )


def body(queries, key_rows, values, out_grads, offsets):
    arrays = [in_hbm(array) for array in (queries, key_rows, values, out_grads)]
    heads = H_MID + H_WIDE
    wide_send, offset_rows = pl.pallas_call(
        wide_kernel,
        out_shape=[shape(OUTERS, 16, 256), shape(heads, TOK, kind=jnp.int32)],
        in_specs=[spec(pltpu.HBM)] * 5,
        out_specs=[spec(pltpu.VMEM)] * 2,
        scratch_shapes=[
            pltpu.SMEM((heads,), jnp.int32),
            pltpu.VMEM((4, H_WIDE, TOK, HEAD_DIM), BF16),
            pltpu.SemaphoreType.DMA,
            pltpu.SemaphoreType.DMA((4, H_WIDE)),
        ],
        compiler_params=params(8),
    )(in_hbm(offsets), *arrays)
    wide_got = lax.all_to_all(wide_send, "outer", 0, 0, axis_index_groups=[list(OUTER_ORDER)])
    packed = pl.pallas_call(
        mid_pack_kernel,
        out_shape=shape(SLOTS, 128, 256),
        in_specs=[spec(pltpu.VMEM)] + [spec(pltpu.HBM)] * 4,
        out_specs=spec(pltpu.VMEM),
        scratch_shapes=[
            pltpu.VMEM((4, H_MID, TOK, HEAD_DIM), BF16),
            pltpu.SemaphoreType.DMA((4, H_MID)),
        ],
        cost_estimate=pl.CostEstimate(
            flops=8 * H_MID * MID_ROWS * TOK * HEAD_DIM,
            bytes_accessed=8 * H_MID * TOK * HEAD_DIM,
            transcendentals=0,
        ),
        compiler_params=params(8),
    )(offset_rows, *arrays)
    near = near_heads(EARLY_NEAR, wide_got, arrays)
    packed = pl.pallas_call(
        wide_pack_kernel,
        out_shape=shape(SLOTS, 128, 256),
        in_specs=[spec(pltpu.VMEM), spec(pltpu.VMEM), spec(pl.ANY)],
        out_specs=spec(pltpu.VMEM),
        input_output_aliases={1: 0},
        compiler_params=params(8),
    )(wide_got, packed, in_hbm(near[0]))
    own = lax.all_to_all(packed, "inner", 0, 0, axis_index_groups=ALONG_Z_IN)
    other = lax.ppermute(own[:, 0:64, :], "inner", ACROSS_Y)
    other_queries = lax.ppermute(own[:, 64:128, :], "inner", ACROSS_Y)
    near = near_heads(LATE_NEAR, own, arrays, near)
    dq, own_sums, wide_rows = pl.pallas_call(
        own_work_kernel,
        out_shape=[
            shape(SLOTS, MID_ROWS, HEAD_DIM),
            shape(HALF_KEYS, 256, kind=F32),
            shape(SLOTS, 16, HEAD_DIM),
        ],
        in_specs=[spec(pltpu.VMEM)] * 2 + [spec(pl.ANY)],
        out_specs=[spec(pltpu.VMEM)] * 3,
        cost_estimate=work_cost(5),
        compiler_params=params(24),
    )(own, other, in_hbm(near[0]))
    results = pl.pallas_call(
        other_work_kernel,
        out_shape=shape(SLOTS, MID_ROWS, 3 * HEAD_DIM),
        in_specs=[spec(pltpu.VMEM)] * 6,
        out_specs=spec(pltpu.VMEM),
        cost_estimate=work_cost(4),
        compiler_params=params(24),
    )(own, other, other_queries, dq, own_sums, wide_rows)
    returned = lax.all_to_all(results, "inner", 0, 0, axis_index_groups=ALONG_Z_OUT)
    return tuple(
        pl.pallas_call(
            assemble_kernel,
            out_shape=[shape(TOK, HIDDEN)] * 3,
            in_specs=[spec(pltpu.VMEM)] * 2 + [spec(pltpu.HBM)] * 3,
            out_specs=[spec(pltpu.HBM)] * 3,
            scratch_shapes=[
                pltpu.VMEM((3, heads, TOK, HEAD_DIM), BF16),
                pltpu.SemaphoreType.DMA((3, heads)),
            ],
            input_output_aliases={2: 0, 3: 1, 4: 2},
            compiler_params=params(16),
        )(offset_rows, returned, *near)
    )


def solution(mesh):
    rows = P(("outer", "inner"), None)
    return jax.shard_map(
        body,
        mesh=mesh,
        in_specs=(rows, rows, rows, rows, P()),
        out_specs=(rows, rows, rows),
        check_vma=False,
    )
```
